128 devices in a mesh: blk: 8 (over z, y_lo), group: 16 (over x, y_hi, core).
Axes of the slice: x: 4, y: 4 (y_hi: 2, y_lo: 2; y = y_hi * 2 + y_lo), z: 4, core: 2. Of those that a mesh axis runs over, the one named last changes fastest.
Arguments:
- img_feat: bfloat16 [16384, 1152], P(('blk', 'group')), may hold values from -150 to 150
- txt_feat: bfloat16 [16384, 1152], P(('blk', 'group')), may hold values from -150 to 150
- w_img: bfloat16 [1152, 1152], replicated, may hold values from -1 to 2
- w_txt: bfloat16 [1152, 1152], replicated, may hold values from -1 to 2
- logit_scale_log: float32 [1], replicated, may hold values from 2.3 to 4.8
- bias: float32 [1], replicated, may hold values from -12 to -6
Outputs:
- grad_img_feat: bfloat16 [16384, 1152], P(('blk', 'group'))
- grad_txt_feat: bfloat16 [16384, 1152], P(('blk', 'group'))
- grad_w_img: float32 [1152, 1152], P(('blk', 'group'))
- grad_w_txt: float32 [1152, 1152], P(('blk', 'group'))
The draws below stay inside these ranges and needn't reach their ends.
All inputs are finite; a program needn't handle non-finite values.
Results may differ from the reference program's by a relative error of at most 0.025.
Values may be sent and summed in bfloat16 or wider, within the bound.
A program may use at most 128 MiB of HBM per device.

```python
import math
import jax
import jax.numpy as jnp
from jax import lax

D = 1152
BLOCK_ROWS = 2048
PAIRS = 16384
N_BLK = 8


def common_part(key):
    count = max(PAIRS // 64, 2)
    key_centers, key_member, key_strength, key_shared = jax.random.split(key, 4)
    centers = jnp.clip(jax.random.normal(key_centers, (count, D), jnp.float32), -4.0, 4.0)
    member = jax.random.randint(key_member, (PAIRS,), 0, count)
    strength = jnp.exp(jax.random.uniform(key_strength, (count,), jnp.float32, math.log(0.35), math.log(1.75)))
    shared = jnp.clip(jax.random.normal(key_shared, (PAIRS, D), jnp.float32), -4.0, 4.0)
    base = centers[member] * strength[member][:, None] + shared
    return base


def own_part(key):
    key_noise = jax.random.fold_in(key, 0)
    noise = jnp.clip(jax.random.normal(key_noise, (PAIRS, D), jnp.float32), -4.0, 4.0)
    return noise


def draw_img_feat(key, part):
    base = common_part(key)
    key = jax.random.fold_in(key, 11)
    noise = own_part(key)
    return (base + noise).astype(jnp.bfloat16)


def draw_txt_feat(key, part):
    base = common_part(key)
    key = jax.random.fold_in(key, 13)
    noise = own_part(key)
    return (base + noise).astype(jnp.bfloat16)


def near_identity(key, mixing):
    spread_part = jnp.clip(jax.random.normal(key, (D, D), jnp.float32), -4.0, 4.0)
    return jnp.eye(D, dtype=jnp.float32) + mixing * spread_part / math.sqrt(D)


def draw_w_img(key, part):
    key = jax.random.fold_in(key, 21)
    matrix = near_identity(key, 0.6)
    return matrix.astype(jnp.bfloat16)


def draw_w_txt(key, part):
    key = jax.random.fold_in(key, 23)
    matrix = near_identity(key, 0.6)
    return matrix.astype(jnp.bfloat16)


def setup_inputs(seed: int = 0) -> dict:
    key_list = jax.random.split(jax.random.key(seed), 7)
    return {
        "img_feat": draw_img_feat(jax.random.fold_in(key_list[6], 71), 0),
        "txt_feat": draw_txt_feat(jax.random.fold_in(key_list[6], 71), 0),
        "w_img": draw_w_img(jax.random.fold_in(key_list[6], 71), 0),
        "w_txt": draw_w_txt(jax.random.fold_in(key_list[6], 71), 0),
        "logit_scale_log": jnp.clip(jax.random.uniform(key_list[4], (1,), jnp.float32, 2.3, 4.8), 2.3, 4.8),
        "bias": jnp.clip(jax.random.uniform(key_list[5], (1,), jnp.float32, -12.0, -6.0), -12.0, -6.0),
    }


def unit_rows(projected):
    inverse = lax.rsqrt(lax.optimization_barrier(jnp.sum(projected * projected, axis=1, keepdims=True)) + 1e-06)
    return (projected * inverse, inverse)

def through_norm(unit, inverse, upstream):
    return inverse * (upstream - unit * lax.optimization_barrier(jnp.sum(unit * upstream, axis=1, keepdims=True)))

def reference(img_feat, txt_feat, w_img, w_txt, logit_scale_log, bias):
    scale_factor = jnp.exp(logit_scale_log[0])
    logit_bias_value = bias[0]
    unit_img, inverse_img = unit_rows(jnp.dot(img_feat, w_img, preferred_element_type=jnp.float32))
    unit_txt, inverse_txt = unit_rows(jnp.dot(txt_feat, w_txt, preferred_element_type=jnp.float32))
    emb_img = unit_img.astype(jnp.bfloat16)
    emb_txt = unit_txt.astype(jnp.bfloat16)
    pair_index = jnp.arange(PAIRS, dtype=jnp.int32)
    image_blocks = emb_img.reshape(N_BLK, BLOCK_ROWS, D)
    block_index = pair_index.reshape(N_BLK, BLOCK_ROWS)

    def per_block(carried, inputs):
        block_emb, block_ids = inputs
        similarity_grid = lax.dot_general(block_emb, emb_txt, (((1,), (1,)), ((), ())), preferred_element_type=jnp.float32)
        pair_scores = scale_factor * similarity_grid + logit_bias_value
        match_signs = jnp.where(block_ids[:, None] == pair_index[None, :], 1.0, -1.0).astype(jnp.float32)
        weight_matrices = (-match_signs * jax.nn.sigmoid(-match_signs * pair_scores) * scale_factor).astype(jnp.bfloat16)
        image_part = jnp.dot(weight_matrices, emb_txt, preferred_element_type=jnp.float32)
        text_part = lax.dot_general(weight_matrices, block_emb, (((0,), (0,)), ((), ())), preferred_element_type=jnp.float32)
        return (carried + text_part, image_part)
    grad_emb_txt, grad_emb_img = lax.scan(per_block, jnp.zeros((PAIRS, D), jnp.float32), (image_blocks, block_index))
    grad_emb_img = grad_emb_img.reshape(PAIRS, D)
    grad_proj_img = through_norm(unit_img, inverse_img, grad_emb_img).astype(jnp.bfloat16)
    grad_proj_txt = through_norm(unit_txt, inverse_txt, grad_emb_txt).astype(jnp.bfloat16)
    grad_img_feat = lax.dot_general(grad_proj_img, w_img, (((1,), (1,)), ((), ())), preferred_element_type=jnp.float32).astype(jnp.bfloat16)
    grad_txt_feat = lax.dot_general(grad_proj_txt, w_txt, (((1,), (1,)), ((), ())), preferred_element_type=jnp.float32).astype(jnp.bfloat16)
    grad_w_img = lax.dot_general(img_feat, grad_proj_img, (((0,), (0,)), ((), ())), preferred_element_type=jnp.float32)
    grad_w_txt = lax.dot_general(txt_feat, grad_proj_txt, (((0,), (0,)), ((), ())), preferred_element_type=jnp.float32)
    return (grad_img_feat, grad_txt_feat, grad_w_img, grad_w_txt)
```

```python
import jax
import jax.numpy as jnp
from jax import lax
from jax.experimental import pallas as pl
from jax.experimental.pallas import tpu as pltpu
from jax.sharding import PartitionSpec as P

R = 128
H = 64
LOG2E = 1.4426950408889634
NT = (((1,), (1,)), ((), ()))
TN = (((0,), (0,)), ((), ()))
F32 = jnp.float32
BF16 = jnp.bfloat16


def neighbours():
    b, g = lax.axis_index("blk"), lax.axis_index("group")
    z, yl = b // 2, b % 2
    x, rest = g // 4, g % 4
    yh, core = rest // 2, rest % 2
    return {
        "core": (b, x * 4 + yh * 2 + (1 - core)),
        "yh": (b, x * 4 + (1 - yh) * 2 + core),
        "x+": (b, ((x + 1) % 4) * 4 + rest),
        "x-": (b, ((x + 3) % 4) * 4 + rest),
        "yl": (z * 2 + (1 - yl), g),
        "z+": (((z + 1) % 4) * 2 + yl, g),
        "z-": (((z + 3) % 4) * 2 + yl, g),
    }


def kernel(img_ref, txt_ref, wi_ref, wt_ref, ls_ref, bias_ref,
           gfi_ref, gft_ref, gpi_ref, gpt_ref,
           I, T, accI, accT, SC, RC, SXI, SXT, RXI, RXT, RFI, RFT, SY, RY,
           unitI, unitT, invI, invT, ssem, rsem):
    D = img_ref.shape[1]
    near = neighbours()
    barrier = pltpu.get_barrier_semaphore()
    for there in near.values():
        pl.semaphore_signal(barrier, inc=1, device_id=there, device_id_type=pl.DeviceIdType.MESH)

    sent = []

    def send(src, dst, to):
        k = len(sent)
        copy = pltpu.make_async_remote_copy(
            src_ref=src, dst_ref=dst, send_sem=ssem.at[k], recv_sem=rsem.at[k],
            device_id=near[to], device_id_type=pl.DeviceIdType.MESH)
        copy.start()
        sent.append(copy)
        return copy

    def project(feat, w, unit, inv, emb):
        p = jnp.dot(feat[...], w[...], preferred_element_type=F32)
        r = lax.rsqrt(jnp.sum(p * p, axis=1, keepdims=True) + 1e-06)
        u = p * r
        unit[...] = u
        inv[...] = jnp.broadcast_to(r, (R, 128))
        emb[0:R, :] = u.astype(BF16)

    def islot(p, y, c, lo=0, n=R):
        return I.at[pl.ds(((p * 2 + y) * 2 + c) * R + lo, n), :]

    def tslot(p, y, lo=0, n=R):
        return T.at[pl.ds((p * 2 + y) * R + lo, n), :]

    project(img_ref, wi_ref, unitI, invI, I)
    pl.semaphore_wait(barrier, len(near))

    ig, tg, core_in = {}, {}, []

    def spread(got, slot, y, ring):
        got["+", y] = send(slot(0, y), slot(2, y), ring + "+")
        got["-", y] = send(slot(0, y), slot(1, y), ring + "-")

    def halves(got, slot, y, ring):
        got["+", y].wait_recv()
        got["++", y] = send(slot(2, y, 0, H), slot(3, y, 0, H), ring + "+")
        got["-", y].wait_recv()
        got["--", y] = send(slot(1, y, H, H), slot(3, y, H, H), ring + "-")

    own = lambda p, y, lo=0, n=R: islot(p, y, 0, lo, n)

    def to_core(p, y):
        core_in.append(send(islot(p, y, 0), islot(p, y, 1), "core"))

    spread(ig, own, 0, "x")
    ig["y"] = send(own(0, 0), own(0, 1), "yh")
    to_core(0, 0)
    project(txt_ref, wt_ref, unitT, invT, T)
    spread(tg, tslot, 0, "z")
    tg["y"] = send(tslot(0, 0), tslot(0, 1), "yl")
    tg["y"].wait_recv()
    spread(tg, tslot, 1, "z")
    ig["y"].wait_recv()
    spread(ig, own, 1, "x")
    to_core(0, 1)

    scale = jnp.exp(jnp.full((1, 256), ls_ref[0], F32))
    slope = scale * (-LOG2E)
    offset = jnp.full((1, 256), bias_ref[0], F32) * (-LOG2E)

    def unit(p, q, first_i=False, first_t=False, diag=False):
        images = I[pl.ds(pl.multiple_of(p * 512, 512), 512), :]
        texts = T[pl.ds(pl.multiple_of(q * 256, 256), 256), :]
        s = lax.dot_general(images, texts, NT, preferred_element_type=F32)
        e = jnp.exp2(jnp.minimum(s * slope + offset, 126.0))
        if diag:
            row = lax.broadcasted_iota(jnp.int32, e.shape, 0)
            col = lax.broadcasted_iota(jnp.int32, e.shape, 1)
            match = (row == col) & (row < R)
            up = jnp.exp2(jnp.minimum(-(s * slope + offset), 126.0))
            c = jnp.where(match, -1.0 / (1.0 + up), 1.0 / (1.0 + e)).astype(BF16)
        else:
            c = pl.reciprocal(1.0 + e, approx=True).astype(BF16)
        di = jnp.dot(c, texts, preferred_element_type=F32)
        dt = lax.dot_general(c, images, TN, preferred_element_type=F32)
        irows = pl.ds(pl.multiple_of(p * 512, 512), 512)
        trows = pl.ds(pl.multiple_of(q * 256, 256), 256)
        if first_i:
            accI[irows, :] = di
        else:
            accI[irows, :] += di
        if first_t:
            accT[trows, :] = dt
        else:
            accT[trows, :] += dt

    def clear(p, q):
        accI[pl.ds(p * 512, 512), :] = jnp.zeros((512, D), F32)
        accT[pl.ds(q * 256, 256), :] = jnp.zeros((256, D), F32)

    for k in range(1, 4):
        clear(k, k)
    for c in core_in[:2]:
        c.wait_recv()
    halves(tg, tslot, 0, "z")
    halves(ig, own, 0, "x")
    to_core(2, 0)
    to_core(1, 0)
    unit(0, 0, True, True, True)
    halves(tg, tslot, 1, "z")
    halves(ig, own, 1, "x")
    to_core(2, 1)
    to_core(1, 1)
    for c in core_in[2:6]:
        c.wait_recv()

    def middle(k, carry):
        unit(k // 3, k % 3)
        return carry

    lax.fori_loop(1, 9, middle, 0)

    for y in range(2):
        for d in ("++", "--"):
            ig[d, y].wait_recv()
        to_core(3, y)
    for y in range(2):
        for d in ("++", "--"):
            tg[d, y].wait_recv()
    for c in core_in[6:8]:
        c.wait_recv()

    def last_images(k, carry):
        unit(3, k)
        return carry

    lax.fori_loop(0, 4, last_images, 0)

    def rows(n, step):
        def one(k, carry):
            step(k * 16)
            return carry
        lax.fori_loop(0, n // 16, one, 0)

    def at(base, r, n=16):
        return pl.ds(pl.multiple_of(base + r, 16), n)

    core_out = {}

    def core_send(p):
        for y in range(2):
            src, dst = ((p * 2 + y) * 2 + 1) * R, (p * 2 + y) * R

            def step(r, src=src, dst=dst):
                SC[at(dst, r), :] = accI[at(src, r), :].astype(BF16)
            rows(R, step)
            core_out[p, y] = send(SC.at[pl.ds(dst, R), :], RC.at[pl.ds(dst, R), :], "core")

    def core_wait(p):
        for y in range(2):
            core_out[p, y].wait_recv()

    def value_i(p, y, r):
        return accI[at((p * 2 + y) * 2 * R, r), :] + RC[at((p * 2 + y) * R, r), :].astype(F32)

    def value_t(p, y, r):
        return accT[at((p * 2 + y) * R, r), :]

    class Ring:
        def __init__(self, value, stage, rx, rf, axis, n):
            self.value, self.stage, self.rx, self.rf = value, stage, rx, rf
            self.axis, self.n, self.got = axis, n, {}

        def piece(self, p, y, lo, direction, dst, add=None):
            base = (p * 2 + y) * R

            def step(r):
                v = self.value(p, y, lo + r)
                if add is not None:
                    v = v + self.rx[at(add, r), :].astype(F32)
                self.stage[at(base + lo, r), :] = v.astype(BF16)
            rows(H, step)
            return send(self.stage.at[pl.ds(base + lo, H), :], dst, self.axis + direction)

        def far(self):
            for y in range(2):
                self.got["far+", y] = self.piece(3, y, 0, "+", self.rx.at[pl.ds(y * H, H), :])
                self.got["far-", y] = self.piece(3, y, H, "-", self.rx.at[pl.ds((2 + y) * H, H), :])

        def near_plus(self):
            for y in range(2):
                self.got["b+", y] = self.piece(1, y, H, "+", self.rf.at[pl.ds(y * R + H, H), :])

        def near_minus(self):
            for y in range(2):
                self.got["a-", y] = self.piece(2, y, 0, "-", self.rf.at[pl.ds((2 + y) * R, H), :])

        def onward(self):
            for y in range(2):
                self.got["far+", y].wait_recv()
                self.got["a+", y] = self.piece(1, y, 0, "+", self.rf.at[pl.ds(y * R, H), :], y * H)
                self.got["far-", y].wait_recv()
                self.got["b-", y] = self.piece(
                    2, y, H, "-", self.rf.at[pl.ds((2 + y) * R + H, H), :], (2 + y) * H)

        def total(self, y, r):
            return (self.value(0, y, r) + self.rf[at(y * R, r), :].astype(F32)
                    + self.rf[at((2 + y) * R, r), :].astype(F32))

        def cross(self, to):
            for key in ("a+", "b+", "a-", "b-"):
                self.got[key, 1].wait_recv()

            def step(r):
                SY[at(self.n * R, r), :] = self.total(1, r).astype(BF16)
            rows(R, step)
            self.got["y"] = send(SY.at[pl.ds(self.n * R, R), :], RY.at[pl.ds(self.n * R, R), :], to)
            for key in ("a+", "b+", "a-", "b-"):
                self.got[key, 0].wait_recv()

        def finish(self, unit_ref, inv_ref, w_ref, gp_ref, gf_ref):
            self.got["y"].wait_recv()
            t = jnp.exp(jnp.full((1, D), ls_ref[0], F32))

            def step(r):
                g = (self.total(0, r) + RY[at(self.n * R, r), :].astype(F32)) * t
                u = unit_ref[at(0, r), :]
                inv = inv_ref[at(0, r), :][:, 0:1]
                along = jnp.sum(u * g, axis=1, keepdims=True)
                gp_ref[at(0, r), :] = (inv * (g - u * along)).astype(BF16)
            rows(R, step)
            gf_ref[...] = lax.dot_general(
                gp_ref[...], w_ref[...], NT, preferred_element_type=F32).astype(BF16)

    ring_i = Ring(value_i, SXI, RXI, RFI, "x", 0)
    ring_t = Ring(value_t, SXT, RXT, RFT, "z", 1)

    core_send(3)
    unit(1, 3)
    core_send(1)
    core_wait(3)
    ring_i.far()
    unit(2, 3)
    core_send(2)
    core_wait(1)
    ring_i.near_plus()
    unit(0, 3)
    ring_t.far()
    core_send(0)
    core_wait(2)
    ring_i.near_minus()
    ring_t.near_plus()
    ring_t.near_minus()
    core_wait(0)
    ring_i.onward()
    ring_t.onward()
    ring_i.cross("yh")
    ring_t.cross("yl")
    ring_i.finish(unitI, invI, wi_ref, gpi_ref, gfi_ref)
    ring_t.finish(unitT, invT, wt_ref, gpt_ref, gft_ref)
    for copy in sent:
        copy.wait_send()


def fused(img_feat, txt_feat, w_img, w_txt, ls, bias):
    D = img_feat.shape[1]
    vmem = pl.BlockSpec(memory_space=pltpu.VMEM)
    smem = pl.BlockSpec(memory_space=pltpu.SMEM)
    row = jax.ShapeDtypeStruct((R, D), BF16)
    sizes = [(2048, BF16), (1024, BF16), (2048, F32), (1024, F32), (1024, BF16), (1024, BF16),
             (1024, BF16), (1024, BF16), (256, BF16), (256, BF16), (512, BF16), (512, BF16),
             (256, BF16), (256, BF16), (R, F32), (R, F32)]
    return pl.pallas_call(
        kernel,
        out_shape=(row,) * 4,
        in_specs=[vmem] * 4 + [smem] * 2,
        out_specs=(vmem,) * 4,
        scratch_shapes=[pltpu.VMEM((n, D), t) for n, t in sizes]
        + [pltpu.VMEM((R, 128), F32)] * 2
        + [pltpu.SemaphoreType.DMA((72,))] * 2,
        compiler_params=pltpu.CompilerParams(
            collective_id=0, has_side_effects=True, vmem_limit_bytes=60 * 2**20),
    )(img_feat, txt_feat, w_img, w_txt, ls, bias)


def body(img_feat, txt_feat, w_img, w_txt, logit_scale_log, bias):
    gfi, gft, gpi, gpt = fused(img_feat, txt_feat, w_img, w_txt, logit_scale_log, bias)
    img_term = lax.dot_general(img_feat, gpi, TN, preferred_element_type=F32).astype(BF16)
    txt_term = lax.dot_general(txt_feat, gpt, TN, preferred_element_type=F32).astype(BF16)
    both = lax.psum_scatter(jnp.concatenate([img_term, txt_term], axis=1), ("blk", "group"),
                            scatter_dimension=0, tiled=True).astype(F32)
    width = img_feat.shape[1]
    return gfi, gft, both[:, :width], both[:, width:]


def solution(mesh):
    rows = P(("blk", "group"), None)
    return jax.shard_map(
        body, mesh=mesh, in_specs=(rows, rows, P(), P(), P(), P()),
        out_specs=(rows,) * 4, check_vma=False)
```

```python
import jax
import jax.numpy as jnp
from jax import lax
from jax.experimental import pallas as pl
from jax.experimental.pallas import tpu as pltpu
from jax.sharding import PartitionSpec as P

R = 128
H = 64
LOG2E = 1.4426950408889634
NT = (((1,), (1,)), ((), ()))
TN = (((0,), (0,)), ((), ()))
F32 = jnp.float32
BF16 = jnp.bfloat16


AXES = (("z", "x", "y"), ("x", "y", "z"), ("y", "z", "x"))
SLOT = 80


def place():
    b, g = lax.axis_index("blk"), lax.axis_index("group")
    return {"x": g // 4, "y": (g // 2) % 2 * 2 + b % 2, "z": b // 2, "core": g % 2}


def neighbours(me):
    def device(**moved):
        c = {**me, **moved}
        return (c["z"] * 2 + c["y"] % 2, c["x"] * 4 + c["y"] // 2 * 2 + c["core"])

    near = {"core": device(core=1 - me["core"])}
    for axis in "xyz":
        for name, step in (("+", 1), ("-", 3), ("2", 2)):
            near[axis + name] = device(**{axis: (me[axis] + step) % 4})
    greeted = list(near.values())
    near["yl"] = device(y=me["y"] + 1 - 2 * (me["y"] % 2))
    return near, greeted


def ring_place(p, here):
    step = jnp.where(p == 1, 1, jnp.where(p == 2, 3, jnp.where(p == 3, 2, 0)))
    return (here + step) & 3


def row_share(axis, v):
    if axis == "y":
        return (v & 1) * 144 + (v >> 1) * 18
    return v * (288 if axis == "z" else 36)


def over(v, step):
    return sum((v >= step * k).astype(jnp.int32) for k in range(1, 4))


def kernel(img_ref, txt_ref, wi_ref, wt_ref, ls_ref, bias_ref,
           gfi_ref, gft_ref, dw_ref,
           I, T, accI, accT, SC, RC, SXI, SXT, RXI, RXT, RFI, RFT, SY, RY,
           unitI, unitT, gpI, gpT, FL, GL, OUT, invI, invT,
           XP, S1, RX1, RF1, S2, RX2, RF2, Z, DM, DR, ssem, rsem):
    D = img_ref.shape[1]
    me = place()
    near, greeted = neighbours(me)
    first = me["core"] == 0
    barrier = pltpu.get_barrier_semaphore()
    for there in greeted:
        pl.semaphore_signal(barrier, inc=1, device_id=there, device_id_type=pl.DeviceIdType.MESH)

    sent = []

    def send(src, dst, to):
        k = len(sent)
        copy = pltpu.make_async_remote_copy(
            src_ref=src, dst_ref=dst, send_sem=ssem.at[k], recv_sem=rsem.at[k],
            device_id=near[to], device_id_type=pl.DeviceIdType.MESH)
        copy.start()
        sent.append(copy)
        return copy

    def project(feat, w, unit, inv, emb):
        p = jnp.dot(feat[...], w[...], preferred_element_type=F32)
        r = lax.rsqrt(jnp.sum(p * p, axis=1, keepdims=True) + 1e-06)
        u = p * r
        unit[...] = u
        inv[...] = jnp.broadcast_to(r, (R, 128))
        emb[0:R, :] = u.astype(BF16)

    def islot(p, y, c, lo=0, n=R):
        return I.at[pl.ds(((p * 2 + y) * 2 + c) * R + lo, n), :]

    def tslot(p, y, lo=0, n=R):
        return T.at[pl.ds((p * 2 + y) * R + lo, n), :]

    project(img_ref, wi_ref, unitI, invI, I)
    pl.semaphore_wait(barrier, len(greeted))

    ig, tg, core_in = {}, {}, []

    def spread(got, slot, y, ring):
        got["+", y] = send(slot(0, y), slot(2, y), ring + "+")
        got["-", y] = send(slot(0, y), slot(1, y), ring + "-")

    def halves(got, slot, y, ring):
        got["+", y].wait_recv()
        got["++", y] = send(slot(2, y, 0, H), slot(3, y, 0, H), ring + "+")
        got["-", y].wait_recv()
        got["--", y] = send(slot(1, y, H, H), slot(3, y, H, H), ring + "-")

    own = lambda p, y, lo=0, n=R: islot(p, y, 0, lo, n)

    def to_core(p, y):
        core_in.append(send(islot(p, y, 0), islot(p, y, 1), "core"))

    spread(ig, own, 0, "x")
    ig["y"] = send(own(0, 0), own(0, 1), "y2")
    to_core(0, 0)
    project(txt_ref, wt_ref, unitT, invT, T)
    FL[0:R, :] = jnp.where(first, img_ref[...], txt_ref[...])
    OUT[...] = jnp.where(first, txt_ref[...], img_ref[...])
    feat_out = send(OUT, FL.at[pl.ds(R, R), :], "core")
    spread(tg, tslot, 0, "z")
    tg["y"] = send(tslot(0, 0), tslot(0, 1), "yl")
    tg["y"].wait_recv()
    spread(tg, tslot, 1, "z")
    ig["y"].wait_recv()
    spread(ig, own, 1, "x")
    to_core(0, 1)

    scale = jnp.exp(jnp.full((1, 256), ls_ref[0], F32))
    slope = scale * (-LOG2E)
    offset = jnp.full((1, 256), bias_ref[0], F32) * (-LOG2E)

    def unit(p, q, first_i=False, first_t=False, diag=False):
        images = I[pl.ds(pl.multiple_of(p * 512, 512), 512), :]
        texts = T[pl.ds(pl.multiple_of(q * 256, 256), 256), :]
        s = lax.dot_general(images, texts, NT, preferred_element_type=F32)
        e = jnp.exp2(jnp.minimum(s * slope + offset, 126.0))
        if diag:
            row = lax.broadcasted_iota(jnp.int32, e.shape, 0)
            col = lax.broadcasted_iota(jnp.int32, e.shape, 1)
            match = (row == col) & (row < R)
            up = jnp.exp2(jnp.minimum(-(s * slope + offset), 126.0))
            c = jnp.where(match, -1.0 / (1.0 + up), 1.0 / (1.0 + e)).astype(BF16)
        else:
            c = pl.reciprocal(1.0 + e, approx=True).astype(BF16)
        di = jnp.dot(c, texts, preferred_element_type=F32)
        dt = lax.dot_general(c, images, TN, preferred_element_type=F32)
        irows = pl.ds(pl.multiple_of(p * 512, 512), 512)
        trows = pl.ds(pl.multiple_of(q * 256, 256), 256)
        if first_i:
            accI[irows, :] = di
        else:
            accI[irows, :] += di
        if first_t:
            accT[trows, :] = dt
        else:
            accT[trows, :] += dt

    def clear(p, q):
        accI[pl.ds(p * 512, 512), :] = jnp.zeros((512, D), F32)
        accT[pl.ds(q * 256, 256), :] = jnp.zeros((256, D), F32)

    for k in range(1, 4):
        clear(k, k)
    feat_out.wait_recv()

    feats = FL[...]
    for third, (a_axis, b_axis, c_axis) in enumerate(AXES):
        def arrange(a, carry):
            s = lax.broadcasted_iota(jnp.int32, (4 * SLOT, 128), 0)
            b = over(s, SLOT)
            k = s - SLOT * b
            c = over(k, 18)
            r = (row_share(a_axis, ring_place(a, me[a_axis]))
                 + row_share(b_axis, ring_place(b, me[b_axis]))
                 + row_share(c_axis, c) + k - 18 * c)
            r = jnp.where(k < 72, r, -1)
            lane = lax.broadcasted_iota(jnp.int32, (4 * SLOT, 128), 1)
            pick = jnp.concatenate(
                [jnp.where(r == lane + 128 * j, 1.0, 0.0).astype(BF16) for j in range(D // 128)],
                axis=1)
            XP[third, pl.ds(pl.multiple_of(a * 4 * SLOT, 16), 4 * SLOT), :] = lax.dot_general(
                pick, feats, NT, preferred_element_type=F32).astype(BF16)
            return carry
        lax.fori_loop(0, 4, arrange, 0)

    for c in core_in[:2]:
        c.wait_recv()
    halves(tg, tslot, 0, "z")
    halves(ig, own, 0, "x")
    to_core(2, 0)
    to_core(1, 0)
    unit(0, 0, True, True, True)
    halves(tg, tslot, 1, "z")
    halves(ig, own, 1, "x")
    to_core(2, 1)
    to_core(1, 1)
    for c in core_in[2:6]:
        c.wait_recv()

    def middle(k, carry):
        unit(k // 3, k % 3)
        return carry

    lax.fori_loop(1, 9, middle, 0)

    for y in range(2):
        for d in ("++", "--"):
            ig[d, y].wait_recv()
        to_core(3, y)
    for y in range(2):
        for d in ("++", "--"):
            tg[d, y].wait_recv()
    for c in core_in[6:8]:
        c.wait_recv()

    def last_images(k, carry):
        unit(3, k)
        return carry

    lax.fori_loop(0, 4, last_images, 0)

    def rows(n, step):
        def one(k, carry):
            step(k * 16)
            return carry
        lax.fori_loop(0, n // 16, one, 0)

    def at(base, r, n=16):
        return pl.ds(pl.multiple_of(base + r, 16), n)

    core_out = {}

    def core_send(p):
        for y in range(2):
            src, dst = ((p * 2 + y) * 2 + 1) * R, (p * 2 + y) * R

            def step(r, src=src, dst=dst):
                SC[at(dst, r), :] = accI[at(src, r), :].astype(BF16)
            rows(R, step)
            core_out[p, y] = send(SC.at[pl.ds(dst, R), :], RC.at[pl.ds(dst, R), :], "core")

    def core_wait(p):
        for y in range(2):
            core_out[p, y].wait_recv()

    def value_i(p, y, r):
        return accI[at((p * 2 + y) * 2 * R, r), :] + RC[at((p * 2 + y) * R, r), :].astype(F32)

    def value_t(p, y, r):
        return accT[at((p * 2 + y) * R, r), :]

    class Ring:
        def __init__(self, axis, n, lo, value, stage, rx, rf):
            self.axis, self.n, self.lo, self.got = axis, n, lo, {}
            self.value, self.stage, self.rx, self.rf = value, stage, rx, rf

        def piece(self, key, p, low, direction, dst, add=None):
            start, n = (0, self.lo) if low else (self.lo, self.n - self.lo)

            def step(r):
                v = self.value(p, start + r)
                if add is not None:
                    v = v + self.rx(add)[at(0, r), :].astype(F32)
                self.stage(p)[at(start, r), :] = v.astype(BF16)
            rows(n, step)
            some = pl.ds(start, n)
            if p == 3:
                some_there = pl.ds(0, n)
            else:
                some_there = some
            self.got[key] = send(self.stage(p).at[some, :], dst.at[some_there, :], self.axis + direction)

        def far(self):
            self.piece("far+", 3, True, "+", self.rx(0))
            self.piece("far-", 3, False, "-", self.rx(1))

        def near_plus(self):
            self.piece("b+", 1, False, "+", self.rf(0))

        def near_minus(self):
            self.piece("a-", 2, True, "-", self.rf(1))

        def onward(self):
            self.got["far+"].wait_recv()
            self.piece("a+", 1, True, "+", self.rf(0), 0)
            self.got["far-"].wait_recv()
            self.piece("b-", 2, False, "-", self.rf(1), 1)

        def arrive(self):
            for key in ("a+", "b+", "a-", "b-"):
                self.got[key].wait_recv()

        def total(self, r):
            return (self.value(0, r) + self.rf(0)[at(0, r), :].astype(F32)
                    + self.rf(1)[at(0, r), :].astype(F32))

    def block_ring(axis, y, value, stage, rx, rf):
        return Ring(
            axis, R, H, lambda p, r: value(p, y, r),
            lambda p: stage.at[pl.ds((p * 2 + y) * R, R), :],
            lambda d: rx.at[pl.ds((d * 2 + y) * H, H), :],
            lambda d: rf.at[pl.ds((d * 2 + y) * R, R), :])

    ring_i = [block_ring("x", y, value_i, SXI, RXI, RFI) for y in range(2)]
    ring_t = [block_ring("z", y, value_t, SXT, RXT, RFT) for y in range(2)]

    def every(rings, what):
        for ring in rings:
            getattr(ring, what)()

    def cross(rings, n, to):
        rings[1].arrive()

        def step(r):
            SY[at(n * R, r), :] = rings[1].total(r).astype(BF16)
        rows(R, step)
        mine = pl.ds(n * R, R)
        return send(SY.at[mine, :], RY.at[mine, :], to)

    def finish(rings, n, crossed, unit_ref, inv_ref, gp):
        rings[0].arrive()
        crossed.wait_recv()
        t = jnp.exp(jnp.full((1, D), ls_ref[0], F32))

        def step(r):
            g = (rings[0].total(r) + RY[at(n * R, r), :].astype(F32)) * t
            u = unit_ref[at(0, r), :]
            inv = inv_ref[at(0, r), :][:, 0:1]
            along = jnp.sum(u * g, axis=1, keepdims=True)
            gp[at(0, r), :] = (inv * (g - u * along)).astype(BF16)
        rows(R, step)

    def feature_grad(gp, w_ref, gf_ref):
        gf_ref[...] = lax.dot_general(
            gp[...], w_ref[...], NT, preferred_element_type=F32).astype(BF16)

    core_send(3)
    unit(1, 3)
    core_send(1)
    core_wait(3)
    every(ring_i, "far")
    unit(2, 3)
    core_send(2)
    core_wait(1)
    every(ring_i, "near_plus")
    unit(0, 3)
    every(ring_t, "far")
    core_send(0)
    core_wait(2)
    every(ring_i, "near_minus")
    every(ring_t, "near_plus")
    every(ring_t, "near_minus")
    core_wait(0)
    every(ring_i, "onward")
    every(ring_t, "onward")
    cross_i = cross(ring_i, 0, "y2")
    cross_t = cross(ring_t, 1, "yl")
    finish(ring_i, 0, cross_i, unitI, invI, gpI)
    finish(ring_t, 1, cross_t, unitT, invT, gpT)

    GL[0:R, :] = jnp.where(first, gpI[...], gpT[...])
    feat_out.wait_send()
    OUT[...] = jnp.where(first, gpT[...], gpI[...])
    grad_in = send(OUT, GL.at[pl.ds(R, R), :], "core")

    def columns(third):
        return slice(third * 384, third * 384 + 384)

    def products(a):
        for third in range(3):
            accI[a * 4 * SLOT:(a + 1) * 4 * SLOT, columns(third)] = jnp.dot(
                XP[third, a * 4 * SLOT:(a + 1) * 4 * SLOT, :], GL[:, columns(third)],
                preferred_element_type=F32)

    def weight_ring(third, axis, n, lo, stage, rx, rf):
        return Ring(
            axis, n, lo, lambda p, r: accI[at(p * n, r), columns(third)],
            lambda p: stage.at[third, pl.ds(p * n, n), :],
            lambda d: rx.at[third, d], lambda d: rf.at[third, d])

    outer = [weight_ring(k, AXES[k][0], 4 * SLOT, 2 * SLOT, S1, RX1, RF1) for k in range(3)]
    inner = [weight_ring(k, AXES[k][1], SLOT, 48, S2, RX2, RF2) for k in range(3)]
    grad_in.wait_recv()
    products(3)
    every(outer, "far")
    products(1)
    every(outer, "near_plus")
    products(2)
    every(outer, "near_minus")
    every(outer, "onward")
    products(0)
    feature_grad(gpI, wi_ref, gfi_ref)
    feature_grad(gpT, wt_ref, gft_ref)
    for third in range(3):
        outer[third].arrive()

        def step(r):
            accI[at(0, r), columns(third)] = outer[third].total(r)
        rows(4 * SLOT, step)
        inner[third].far()
    every(inner, "near_plus")
    every(inner, "near_minus")
    every(inner, "onward")
    last = []
    for third in range(3):
        inner[third].arrive()

        def step(r):
            Z[third, at(0, r), :] = inner[third].total(r).astype(BF16)
        rows(SLOT, step)
        for k, there in enumerate("+-2"):
            last.append(send(Z.at[third, pl.ds(0, SLOT), :],
                             Z.at[third, pl.ds((k + 1) * SLOT, SLOT), :], AXES[third][2] + there))
    for third in range(3):
        for copy in last[third * 3:third * 3 + 3]:
            copy.wait_recv()
        row = lax.broadcasted_iota(jnp.int32, (32, 4 * SLOT), 0)
        k = lax.broadcasted_iota(jnp.int32, (32, 4 * SLOT), 1)
        k = k - SLOT * over(k, SLOT)
        theirs = (row >= 16).astype(jnp.int32)
        i = row - 16 * theirs
        core = theirs + me["core"] - 2 * theirs * me["core"]
        want = me[AXES[third][2]] * 18 + core * 9 + i
        pick = jnp.where((k == want) & (i < 9), 1.0, 0.0).astype(BF16)
        DM[:, columns(third)] = jnp.dot(pick, Z[third], preferred_element_type=F32)
    swap = send(DM.at[pl.ds(16, 16), :], DR, "core")
    swap.wait_recv()
    dw_ref[0:16, :] = jnp.where(first, DM[0:16, :], DR[...])
    dw_ref[16:32, :] = jnp.where(first, DR[...], DM[0:16, :])
    for copy in sent:
        if copy is not feat_out:
            copy.wait_send()


def fused(img_feat, txt_feat, w_img, w_txt, ls, bias):
    D = img_feat.shape[1]
    vmem = pl.BlockSpec(memory_space=pltpu.VMEM)
    smem = pl.BlockSpec(memory_space=pltpu.SMEM)
    row = jax.ShapeDtypeStruct((R, D), BF16)
    sizes = [(2048, BF16), (1024, BF16), (2048, F32), (1024, F32), (1024, BF16), (1024, BF16),
             (1024, BF16), (1024, BF16), (256, BF16), (256, BF16), (512, BF16), (512, BF16),
             (256, BF16), (256, BF16), (R, F32), (R, F32), (R, BF16), (R, BF16),
             (2 * R, BF16), (2 * R, BF16), (R, BF16)]
    thirds = [(4 * 4 * SLOT,), (2, 2 * SLOT), (2, 4 * SLOT), (4 * SLOT,), (2, 48), (2, SLOT),
              (4 * SLOT,)]
    return pl.pallas_call(
        kernel,
        out_shape=(row, row, jax.ShapeDtypeStruct((32, D), F32)),
        in_specs=[vmem] * 4 + [smem] * 2,
        out_specs=(vmem,) * 3,
        scratch_shapes=[pltpu.VMEM((n, D), t) for n, t in sizes]
        + [pltpu.VMEM((R, 128), F32)] * 2
        + [pltpu.VMEM((3, 16 * SLOT, 2 * R), BF16)]
        + [pltpu.VMEM((3,) + n + (D // 3,), BF16) for n in thirds]
        + [pltpu.VMEM((32, D), F32), pltpu.VMEM((16, D), F32)]
        + [pltpu.SemaphoreType.DMA((120,))] * 2,
        compiler_params=pltpu.CompilerParams(
            collective_id=0, has_side_effects=True, vmem_limit_bytes=62 * 2**20),
    )(img_feat, txt_feat, w_img, w_txt, ls, bias)


def body(img_feat, txt_feat, w_img, w_txt, logit_scale_log, bias):
    gfi, gft, dw = fused(img_feat, txt_feat, w_img, w_txt, logit_scale_log, bias)
    return gfi, gft, dw[0:9], dw[16:25]


def solution(mesh):
    rows = P(("blk", "group"), None)
    return jax.shard_map(
        body, mesh=mesh, in_specs=(rows, rows, P(), P(), P(), P()),
        out_specs=(rows,) * 4, check_vma=False)
```

```python
import jax
import jax.numpy as jnp
from jax import lax
from jax.experimental import pallas as pl
from jax.experimental.pallas import tpu as pltpu
from jax.sharding import PartitionSpec as P

R = 128
H = 64
LOG2E = 1.4426950408889634
NT = (((1,), (1,)), ((), ()))
TN = (((0,), (0,)), ((), ()))
F32 = jnp.float32
BF16 = jnp.bfloat16


AXES = (("z", "x", "y"), ("x", "y", "z"), ("y", "z", "x"))
SLOT = 80


def place():
    b, g = lax.axis_index("blk"), lax.axis_index("group")
    return {"x": g // 4, "y": (g // 2) % 2 * 2 + b % 2, "z": b // 2, "core": g % 2}


def neighbours(me):
    def device(**moved):
        c = {**me, **moved}
        return (c["z"] * 2 + c["y"] % 2, c["x"] * 4 + c["y"] // 2 * 2 + c["core"])

    near = {"core": device(core=1 - me["core"])}
    for axis in "xyz":
        for name, step in (("+", 1), ("-", 3), ("2", 2)):
            near[axis + name] = device(**{axis: (me[axis] + step) % 4})
    greeted = list(near.values())
    near["yi"] = device(y=me["y"] + 1 - 2 * (me["y"] % 2))
    near["yt"] = device(y=3 - me["y"])
    return near, greeted


def ring_place(p, here):
    step = jnp.where(p == 1, 1, jnp.where(p == 2, 3, jnp.where(p == 3, 2, 0)))
    return (here + step) & 3


def row_share(axis, v):
    if axis == "y":
        return (v & 1) * 144 + (v >> 1) * 18
    return v * (288 if axis == "z" else 36)


def over(v, step):
    return sum((v >= step * k).astype(jnp.int32) for k in range(1, 4))


def kernel(img_hbm, txt_hbm, wi_hbm, wt_hbm, ls_ref, bias_ref,
           gfi_ref, gft_ref, dw_ref,
           I, T, accI, accT, SC, RC, SXI, SXT, RXI, RXT, RFI, RFT, SY, RY, SF, RYF, WI, WT, IMG, TXT,
           unitI, unitT, gpI, gpT, FL, GL, OUT, invI, invT,
           XP, S1, RX1, RF1, S2, RX2, RF2, Z, DM, DR, lsem, ssem, rsem):
    D = IMG.shape[1]
    loads = [pltpu.make_async_copy(src, dst, lsem.at[k]) for k, (src, dst) in enumerate(
        ((img_hbm, IMG), (wi_hbm, WI), (txt_hbm, TXT), (wt_hbm, WT)))]
    for load in loads:
        load.start()
    me = place()
    near, greeted = neighbours(me)
    first = me["core"] == 0
    barrier = pltpu.get_barrier_semaphore()
    for there in greeted:
        pl.semaphore_signal(barrier, inc=1, device_id=there, device_id_type=pl.DeviceIdType.MESH)

    sent = []

    def send(src, dst, to):
        k = len(sent)
        copy = pltpu.make_async_remote_copy(
            src_ref=src, dst_ref=dst, send_sem=ssem.at[k], recv_sem=rsem.at[k],
            device_id=near[to], device_id_type=pl.DeviceIdType.MESH)
        copy.start()
        sent.append(copy)
        return copy

    def project(feat, w, unit, inv, emb):
        p = jnp.dot(feat[...], w[...], preferred_element_type=F32)
        r = lax.rsqrt(jnp.sum(p * p, axis=1, keepdims=True) + 1e-06)
        u = p * r
        unit[...] = u
        inv[...] = jnp.broadcast_to(r, (R, 128))
        emb[0:R, :] = u.astype(BF16)

    ORDER = ((0, 1), (2, 4), (3, 5), (6, 7))

    def islot(p, y, c=0, lo=0, n=R):
        return I.at[pl.ds((ORDER[p][y] * 2 + c) * R + lo, n), :]

    def tslot(p, y, lo=0, n=R):
        return T.at[pl.ds(ORDER[p][y] * R + lo, n), :]

    def own(p, y, lo=0, n=R):
        return islot(p, y, 0, lo, n)

    ig, tg, core_in = {}, {}, {}

    def spread(got, slot, y, ring):
        got["+", y] = send(slot(0, y), slot(2, y), ring + "+")
        got["-", y] = send(slot(0, y), slot(1, y), ring + "-")

    def near_in(got, y):
        got["+", y].wait_recv()
        got["-", y].wait_recv()

    def onward_halves(got, slot, ring):
        got["far+"] = send(slot(2, 0, 0, H), slot(3, 0, 0, H), ring + "+")
        got["far-"] = send(slot(1, 0, H, H), slot(3, 0, H, H), ring + "-")

    def far_in(got, slot, to):
        got["far+"].wait_recv()
        got["far-"].wait_recv()
        got["far y"] = send(slot(3, 0), slot(3, 1), to)

    def to_core(*places):
        for p, y in places:
            core_in[p, y] = send(islot(p, y, 0), islot(p, y, 1), "core")

    def from_core(*places):
        for place_y in places:
            core_in[place_y].wait_recv()

    loads[0].wait()
    loads[1].wait()
    project(IMG, WI, unitI, invI, I)
    pl.semaphore_wait(barrier, len(greeted))
    ig["y"] = send(own(0, 0), own(0, 1), "yi")
    spread(ig, own, 0, "x")
    to_core((0, 0))
    loads[2].wait()
    loads[3].wait()
    project(TXT, WT, unitT, invT, T)
    tg["y"] = send(tslot(0, 0), tslot(0, 1), "yt")
    spread(tg, tslot, 0, "z")
    FL[0:R, :] = jnp.where(first, IMG[...], TXT[...])
    OUT[...] = jnp.where(first, TXT[...], IMG[...])
    feat_out = send(OUT, FL.at[pl.ds(R, R), :], "core")
    accI[512:2048, :] = jnp.zeros((1536, D), F32)
    accT[256:1024, :] = jnp.zeros((768, D), F32)

    ig["y"].wait_recv()
    spread(ig, own, 1, "x")
    to_core((0, 1))
    tg["y"].wait_recv()
    spread(tg, tslot, 1, "z")

    scale = jnp.exp(jnp.full((1, 256), ls_ref[0], F32))
    slope = scale * (-LOG2E)
    offset = jnp.full((1, 256), bias_ref[0], F32) * (-LOG2E)

    def unit(p, q, first_i=False, first_t=False, diag=False):
        images = I[pl.ds(pl.multiple_of(p * 512, 512), 512), :]
        texts = T[pl.ds(pl.multiple_of(q * 256, 256), 256), :]
        s = lax.dot_general(images, texts, NT, preferred_element_type=F32)
        e = jnp.exp2(jnp.minimum(s * slope + offset, 126.0))
        if diag:
            row = lax.broadcasted_iota(jnp.int32, e.shape, 0)
            col = lax.broadcasted_iota(jnp.int32, e.shape, 1)
            match = (row == col) & (row < R)
            up = jnp.exp2(jnp.minimum(-(s * slope + offset), 126.0))
            c = jnp.where(match, -1.0 / (1.0 + up), 1.0 / (1.0 + e)).astype(BF16)
        else:
            c = pl.reciprocal(1.0 + e, approx=True).astype(BF16)
        di = jnp.dot(c, texts, preferred_element_type=F32)
        dt = lax.dot_general(c, images, TN, preferred_element_type=F32)
        irows = pl.ds(pl.multiple_of(p * 512, 512), 512)
        trows = pl.ds(pl.multiple_of(q * 256, 256), 256)
        if first_i:
            accI[irows, :] = di
        else:
            accI[irows, :] += di
        if first_t:
            accT[trows, :] = dt
        else:
            accT[trows, :] += dt

    feat_out.wait_recv()
    feats = FL[...]
    for third, (a_axis, b_axis, c_axis) in enumerate(AXES):
        def arrange(a, carry):
            s = lax.broadcasted_iota(jnp.int32, (4 * SLOT, 128), 0)
            b = over(s, SLOT)
            k = s - SLOT * b
            c = over(k, 18)
            r = (row_share(a_axis, ring_place(a, me[a_axis]))
                 + row_share(b_axis, ring_place(b, me[b_axis]))
                 + row_share(c_axis, c) + k - 18 * c)
            r = jnp.where(k < 72, r, -1)
            lane = lax.broadcasted_iota(jnp.int32, (4 * SLOT, 128), 1)
            pick = jnp.concatenate(
                [jnp.where(r == lane + 128 * j, 1.0, 0.0).astype(BF16) for j in range(D // 128)],
                axis=1)
            XP[third, pl.ds(pl.multiple_of(a * 4 * SLOT, 16), 4 * SLOT), :] = lax.dot_general(
                pick, feats, NT, preferred_element_type=F32).astype(BF16)
            return carry
        lax.fori_loop(0, 4, arrange, 0)

    near_in(ig, 0)
    onward_halves(ig, own, "x")
    to_core((1, 0), (2, 0))
    near_in(tg, 0)
    onward_halves(tg, tslot, "z")
    from_core((0, 0), (0, 1))
    unit(0, 0, True, True, True)
    from_core((1, 0), (2, 0))

    def level1(k, carry):
        unit(k // 2, k % 2)
        return carry
    lax.fori_loop(1, 4, level1, 0)

    near_in(ig, 1)
    to_core((1, 1), (2, 1))
    near_in(tg, 1)
    far_in(ig, own, "yi")
    to_core((3, 0))
    far_in(tg, tslot, "yt")

    def level2_texts(k, carry):
        unit(k, 2)
        return carry
    lax.fori_loop(0, 2, level2_texts, 0)
    ig["far y"].wait_recv()
    to_core((3, 1))
    from_core((1, 1), (2, 1))

    def level2_images(k, carry):
        unit(2, k)
        return carry
    lax.fori_loop(0, 3, level2_images, 0)
    tg["far y"].wait_recv()
    from_core((3, 0), (3, 1))

    def level3_images(k, carry):
        unit(3, k)
        return carry
    lax.fori_loop(0, 4, level3_images, 0)

    def rows(n, step):
        def one(k, carry):
            step(k * 16)
            return carry
        lax.fori_loop(0, n // 16, one, 0)

    def at(base, r, n=16):
        return pl.ds(pl.multiple_of(base + r, 16), n)

    core_out = {}

    def core_send(level):
        for k in (2 * level, 2 * level + 1):
            def step(r):
                SC[at(k * R, r), :] = accI[at((k * 2 + 1) * R, r), :].astype(BF16)
            rows(R, step)
            block = pl.ds(k * R, R)
            core_out[k] = send(SC.at[block, :], RC.at[block, :], "core")

    def core_wait(level):
        core_out[2 * level].wait_recv()
        core_out[2 * level + 1].wait_recv()

    def value_i(p, y, r):
        k = ORDER[p][y]
        return accI[at(k * 2 * R, r), :] + RC[at(k * R, r), :].astype(F32)

    def value_t(p, y, r):
        return accT[at(ORDER[p][y] * R, r), :]

    class Ring:
        def __init__(self, axis, n, lo, value, stage, rx, rf):
            self.axis, self.n, self.lo, self.got = axis, n, lo, {}
            self.value, self.stage, self.rx, self.rf = value, stage, rx, rf

        def piece(self, key, p, start, n, direction, dst, dst_start, add=None):
            def step(r):
                v = self.value(p, start + r)
                if add is not None:
                    v = v + add(r).astype(F32)
                self.stage(p)[at(start, r), :] = v.astype(BF16)
            rows(n, step)
            self.got[key] = send(self.stage(p).at[pl.ds(start, n), :],
                                 dst.at[pl.ds(dst_start, n), :], self.axis + direction)

        def far(self, add=None):
            lo, hi = self.lo, self.n - self.lo
            high = None if add is None else lambda r: add(lo + r)
            self.piece("far+", 3, 0, lo, "+", self.rx(0), 0, add)
            self.piece("far-", 3, lo, hi, "-", self.rx(1), 0, high)

        def near(self):
            self.piece("b+", 1, self.lo, self.n - self.lo, "+", self.rf(0), self.lo)
            self.piece("a-", 2, 0, self.lo, "-", self.rf(1), 0)

        def whole(self):
            self.piece("a+", 1, 0, self.n, "+", self.rf(0), 0)
            self.piece("a-", 2, 0, self.n, "-", self.rf(1), 0)

        def onward(self):
            lo, hi = self.lo, self.n - self.lo
            self.got["far+"].wait_recv()
            self.piece("a+", 1, 0, lo, "+", self.rf(0), 0, lambda r: self.rx(0)[at(0, r), :])
            self.got["far-"].wait_recv()
            self.piece("b-", 2, lo, hi, "-", self.rf(1), lo, lambda r: self.rx(1)[at(0, r), :])

        def arrive(self):
            for key in ("a+", "b+", "a-", "b-"):
                if key in self.got:
                    self.got[key].wait_recv()

        def total(self, r):
            return (self.value(0, r) + self.rf(0)[at(0, r), :].astype(F32)
                    + self.rf(1)[at(0, r), :].astype(F32))

    def block_ring(axis, y, value, stage, rx, rf):
        return Ring(
            axis, R, H, lambda p, r: value(p, y, r),
            lambda p: stage.at[pl.ds(ORDER[p][y] * R, R), :],
            lambda d: rx.at[pl.ds(d * H, H), :],
            lambda d: rf.at[pl.ds((d * 2 + y) * R, R), :])

    ring_i = [block_ring("x", y, value_i, SXI, RXI, RFI) for y in range(2)]
    ring_t = [block_ring("z", y, value_t, SXT, RXT, RFT) for y in range(2)]

    def every(rings, what):
        for ring in rings:
            getattr(ring, what)()

    def cross(rings, n, to):
        rings[1].arrive()

        def step(r):
            SY[at(n * R, r), :] = rings[1].total(r).astype(BF16)
        rows(R, step)
        mine = pl.ds(n * R, R)
        return send(SY.at[mine, :], RY.at[mine, :], to)

    def finish(rings, n, crossed, unit_ref, inv_ref, gp):
        rings[0].arrive()
        crossed.wait_recv()
        t = jnp.exp(jnp.full((1, D), ls_ref[0], F32))

        def step(r):
            g = (rings[0].total(r) + RY[at(n * R, r), :].astype(F32)) * t
            u = unit_ref[at(0, r), :]
            inv = inv_ref[at(0, r), :][:, 0:1]
            along = jnp.sum(u * g, axis=1, keepdims=True)
            gp[at(0, r), :] = (inv * (g - u * along)).astype(BF16)
        rows(R, step)

    def feature_grad(gp, w_ref, gf_ref):
        gf_ref[...] = lax.dot_general(
            gp[...], w_ref[...], NT, preferred_element_type=F32).astype(BF16)

    def far_over(ring, n, to):
        def step(r):
            SF[at(n * R, r), :] = ring.value(3, r).astype(BF16)
        rows(R, step)
        mine = pl.ds(n * R, R)
        return send(SF.at[mine, :], RYF.at[mine, :], to)

    def far_sum(ring, n, over_y):
        over_y.wait_recv()
        ring.far(lambda r: RYF[at(n * R, r), :])

    core_send(3)
    unit(2, 3)
    core_send(2)
    core_wait(3)
    over_i = far_over(ring_i[1], 0, "yi")
    unit(1, 3)
    core_send(1)
    core_wait(2)
    ring_i[1].whole()
    unit(0, 3)
    over_t = far_over(ring_t[1], 1, "yt")
    core_send(0)
    ring_t[1].whole()
    far_sum(ring_i[0], 0, over_i)
    core_wait(1)
    ring_i[0].near()
    ring_t[0].near()
    far_sum(ring_t[0], 1, over_t)
    core_wait(0)
    cross_i = cross(ring_i, 0, "yi")
    ring_i[0].onward()
    cross_t = cross(ring_t, 1, "yt")
    ring_t[0].onward()
    finish(ring_i, 0, cross_i, unitI, invI, gpI)
    finish(ring_t, 1, cross_t, unitT, invT, gpT)

    GL[0:R, :] = jnp.where(first, gpI[...], gpT[...])
    feat_out.wait_send()
    OUT[...] = jnp.where(first, gpT[...], gpI[...])
    grad_in = send(OUT, GL.at[pl.ds(R, R), :], "core")

    def columns(third):
        return slice(third * 384, third * 384 + 384)

    def products(a):
        for third in range(3):
            accI[a * 4 * SLOT:(a + 1) * 4 * SLOT, columns(third)] = jnp.dot(
                XP[third, a * 4 * SLOT:(a + 1) * 4 * SLOT, :], GL[:, columns(third)],
                preferred_element_type=F32)

    def weight_ring(third, axis, n, lo, stage, rx, rf):
        return Ring(
            axis, n, lo, lambda p, r: accI[at(p * n, r), columns(third)],
            lambda p: stage.at[third, pl.ds(p * n, n), :],
            lambda d: rx.at[third, d], lambda d: rf.at[third, d])

    outer = [weight_ring(k, AXES[k][0], 4 * SLOT, 2 * SLOT, S1, RX1, RF1) for k in range(3)]
    inner = [weight_ring(k, AXES[k][1], SLOT, 48, S2, RX2, RF2) for k in range(3)]
    grad_in.wait_recv()
    products(3)
    every(outer, "far")
    products(1)
    products(2)
    every(outer, "near")
    every(outer, "onward")
    products(0)
    feature_grad(gpI, WI, gfi_ref)
    feature_grad(gpT, WT, gft_ref)
    for third in range(3):
        outer[third].arrive()

        def step(r):
            accI[at(0, r), columns(third)] = outer[third].total(r)
        rows(4 * SLOT, step)
        inner[third].far()
    every(inner, "near")
    every(inner, "onward")
    last = []
    for third in range(3):
        inner[third].arrive()

        def step(r):
            Z[third, at(0, r), :] = inner[third].total(r).astype(BF16)
        rows(SLOT, step)
        for k, there in enumerate("+-2"):
            last.append(send(Z.at[third, pl.ds(0, SLOT), :],
                             Z.at[third, pl.ds((k + 1) * SLOT, SLOT), :], AXES[third][2] + there))
    for third in range(3):
        for copy in last[third * 3:third * 3 + 3]:
            copy.wait_recv()
        row = lax.broadcasted_iota(jnp.int32, (32, 4 * SLOT), 0)
        k = lax.broadcasted_iota(jnp.int32, (32, 4 * SLOT), 1)
        k = k - SLOT * over(k, SLOT)
        theirs = (row >= 16).astype(jnp.int32)
        i = row - 16 * theirs
        core = theirs + me["core"] - 2 * theirs * me["core"]
        want = me[AXES[third][2]] * 18 + core * 9 + i
        pick = jnp.where((k == want) & (i < 9), 1.0, 0.0).astype(BF16)
        DM[:, columns(third)] = jnp.dot(pick, Z[third], preferred_element_type=F32)
    swap = send(DM.at[pl.ds(16, 16), :], DR, "core")
    swap.wait_recv()
    dw_ref[0:16, :] = jnp.where(first, DM[0:16, :], DR[...])
    dw_ref[16:32, :] = jnp.where(first, DR[...], DM[0:16, :])
    for copy in sent:
        if copy is not feat_out:
            copy.wait_send()


def fused(img_feat, txt_feat, w_img, w_txt, ls, bias):
    D = img_feat.shape[1]
    vmem = pl.BlockSpec(memory_space=pltpu.VMEM)
    hbm = pl.BlockSpec(memory_space=pl.ANY)
    smem = pl.BlockSpec(memory_space=pltpu.SMEM)
    row = jax.ShapeDtypeStruct((R, D), BF16)
    sizes = [(2048, BF16), (1024, BF16), (2048, F32), (1024, F32), (1024, BF16), (1024, BF16),
             (1024, BF16), (1024, BF16), (R, BF16), (R, BF16), (512, BF16), (512, BF16),
             (256, BF16), (256, BF16), (256, BF16), (256, BF16), (D, BF16), (D, BF16),
             (R, BF16), (R, BF16), (R, F32), (R, F32), (R, BF16), (R, BF16),
             (2 * R, BF16), (2 * R, BF16), (R, BF16)]
    thirds = [(4 * 4 * SLOT,), (2, 2 * SLOT), (2, 4 * SLOT), (4 * SLOT,), (2, 48), (2, SLOT),
              (4 * SLOT,)]
    return pl.pallas_call(
        kernel,
        out_shape=(row, row, jax.ShapeDtypeStruct((32, D), F32)),
        in_specs=[hbm] * 4 + [smem] * 2,
        out_specs=(vmem,) * 3,
        scratch_shapes=[pltpu.VMEM((n, D), t) for n, t in sizes]
        + [pltpu.VMEM((R, 128), F32)] * 2
        + [pltpu.VMEM((3, 16 * SLOT, 2 * R), BF16)]
        + [pltpu.VMEM((3,) + n + (D // 3,), BF16) for n in thirds]
        + [pltpu.VMEM((32, D), F32), pltpu.VMEM((16, D), F32)]
        + [pltpu.SemaphoreType.DMA((4,))] + [pltpu.SemaphoreType.DMA((120,))] * 2,
        compiler_params=pltpu.CompilerParams(
            collective_id=0, has_side_effects=True, vmem_limit_bytes=62 * 2**20),
    )(img_feat, txt_feat, w_img, w_txt, ls, bias)


def body(img_feat, txt_feat, w_img, w_txt, logit_scale_log, bias):
    gfi, gft, dw = fused(img_feat, txt_feat, w_img, w_txt, logit_scale_log, bias)
    return gfi, gft, dw[0:9], dw[16:25]


def solution(mesh):
    rows = P(("blk", "group"), None)
    return jax.shard_map(
        body, mesh=mesh, in_specs=(rows, rows, P(), P(), P(), P()),
        out_specs=(rows,) * 4, check_vma=False)
```

```python
import jax
import jax.numpy as jnp
from jax import lax
from jax.experimental import pallas as pl
from jax.experimental.pallas import tpu as pltpu
from jax.sharding import PartitionSpec as P

R = 128
H = 64
LOG2E = 1.4426950408889634
NT = (((1,), (1,)), ((), ()))
TN = (((0,), (0,)), ((), ()))
F32 = jnp.float32
BF16 = jnp.bfloat16


AXES = (("z", "x", "y"), ("x", "y", "z"), ("y", "z", "x"))
SLOT = 80


def place():
    b, g = lax.axis_index("blk"), lax.axis_index("group")
    return {"x": g // 4, "y": (g // 2) % 2 * 2 + b % 2, "z": b // 2, "core": g % 2}


def neighbours(me):
    def device(**moved):
        c = {**me, **moved}
        return (c["z"] * 2 + c["y"] % 2, c["x"] * 4 + c["y"] // 2 * 2 + c["core"])

    near = {"core": device(core=1 - me["core"])}
    for axis in "xyz":
        for name, step in (("+", 1), ("-", 3), ("2", 2)):
            near[axis + name] = device(**{axis: (me[axis] + step) % 4})
    greeted = list(near.values())
    near["yi"] = device(y=me["y"] + 1 - 2 * (me["y"] % 2))
    near["yt"] = device(y=3 - me["y"])
    return near, greeted


def ring_place(p, here):
    step = jnp.where(p == 1, 1, jnp.where(p == 2, 3, jnp.where(p == 3, 2, 0)))
    return (here + step) & 3


def row_share(axis, v):
    if axis == "y":
        return (v & 1) * 144 + (v >> 1) * 18
    return v * (288 if axis == "z" else 36)


def over(v, step):
    return sum((v >= step * k).astype(jnp.int32) for k in range(1, 4))


def kernel(img_hbm, txt_hbm, wi_hbm, wt_hbm, ls_ref, bias_ref,
           gf_ref, dw_ref,
           I, T, accI, accT, SC, RC, SXI, SXT, RXI, RXT, RFI, RFT, SY, RY, SF, RYF, WI, WT, IMG, TXT,
           unitI, unitT, gpI, gpT, FL, GL, OUT, invI, invT,
           XP, S1, RX1, RF1, S2, RF2, Z, DM, DR, lsem, ssem, rsem):
    D = IMG.shape[1]
    loads = [pltpu.make_async_copy(src, dst, lsem.at[k]) for k, (src, dst) in enumerate(
        ((img_hbm, IMG), (wi_hbm, WI), (txt_hbm, TXT), (wt_hbm, WT)))]
    for load in loads:
        load.start()
    me = place()
    near, greeted = neighbours(me)
    first = me["core"] == 0
    barrier = pltpu.get_barrier_semaphore()
    for there in greeted:
        pl.semaphore_signal(barrier, inc=1, device_id=there, device_id_type=pl.DeviceIdType.MESH)

    sent = []

    def send(src, dst, to):
        k = len(sent)
        copy = pltpu.make_async_remote_copy(
            src_ref=src, dst_ref=dst, send_sem=ssem.at[k], recv_sem=rsem.at[k],
            device_id=near[to], device_id_type=pl.DeviceIdType.MESH)
        copy.start()
        sent.append(copy)
        return copy

    def project(feat, w, unit, inv, emb):
        p = jnp.dot(feat[...], w[...], preferred_element_type=F32)
        r = lax.rsqrt(jnp.sum(p * p, axis=1, keepdims=True) + 1e-06)
        u = p * r
        unit[...] = u
        inv[...] = jnp.broadcast_to(r, (R, 128))
        emb[0:R, :] = u.astype(BF16)

    ORDER = ((0, 1), (2, 4), (3, 5), (6, 7))

    def islot(p, y, c=0, lo=0, n=R):
        return I.at[pl.ds((ORDER[p][y] * 2 + c) * R + lo, n), :]

    def tslot(p, y, lo=0, n=R):
        return T.at[pl.ds(ORDER[p][y] * R + lo, n), :]

    def own(p, y, lo=0, n=R):
        return islot(p, y, 0, lo, n)

    ig, tg, core_in = {}, {}, {}

    def spread(got, slot, y, ring):
        got["+", y] = send(slot(0, y), slot(2, y), ring + "+")
        got["-", y] = send(slot(0, y), slot(1, y), ring + "-")

    def near_in(got, y):
        got["+", y].wait_recv()
        got["-", y].wait_recv()

    def onward_halves(got, slot, ring):
        got["far+"] = send(slot(2, 0, 0, H), slot(3, 0, 0, H), ring + "+")
        got["far-"] = send(slot(1, 0, H, H), slot(3, 0, H, H), ring + "-")

    def far_in(got, slot, to):
        got["far+"].wait_recv()
        got["far-"].wait_recv()
        got["far y"] = send(slot(3, 0), slot(3, 1), to)

    def to_core(*places):
        for p, y in places:
            core_in[p, y] = send(islot(p, y, 0), islot(p, y, 1), "core")

    def from_core(*places):
        for place_y in places:
            core_in[place_y].wait_recv()

    loads[0].wait()
    loads[1].wait()
    project(IMG, WI, unitI, invI, I)
    pl.semaphore_wait(barrier, len(greeted))
    ig["y"] = send(own(0, 0), own(0, 1), "yi")
    spread(ig, own, 0, "x")
    to_core((0, 0))
    loads[2].wait()
    loads[3].wait()
    project(TXT, WT, unitT, invT, T)
    tg["y"] = send(tslot(0, 0), tslot(0, 1), "yt")
    spread(tg, tslot, 0, "z")
    FL[0:R, :] = jnp.where(first, IMG[...], TXT[...])
    OUT[...] = jnp.where(first, TXT[...], IMG[...])
    feat_out = send(OUT, FL.at[pl.ds(R, R), :], "core")
    accT[768:1024, :] = jnp.zeros((256, D), F32)

    near_in(ig, 0)
    onward_halves(ig, own, "x")
    to_core((1, 0), (2, 0))
    near_in(tg, 0)
    onward_halves(tg, tslot, "z")
    ig["y"].wait_recv()
    spread(ig, own, 1, "x")
    to_core((0, 1))
    tg["y"].wait_recv()
    spread(tg, tslot, 1, "z")

    scale = jnp.exp(jnp.full((1, 512), ls_ref[0], F32))
    slope = scale * (-LOG2E)
    offset = jnp.full((1, 512), bias_ref[0], F32) * (-LOG2E)

    def unit(ilo, m, tlo, n, new_i=False, new_t=False, diag=False):
        irows, trows = slice(ilo, ilo + m), slice(tlo, tlo + n)
        images, texts = I[irows, :], T[trows, :]
        parts = []
        for k in range(0, m, 256):
            s = lax.dot_general(I[ilo + k:ilo + k + 256, :], texts, NT, preferred_element_type=F32)
            x = s * slope[:, :n] + offset[:, :n]
            c = pltpu.reciprocal(1.0 + jnp.exp2(jnp.minimum(x, 126.0)), approx=True).astype(BF16)
            if diag and k == 0:
                up = jnp.exp2(jnp.minimum(-x[:R, :R], 126.0))
                row = lax.broadcasted_iota(jnp.int32, (R, R), 0)
                col = lax.broadcasted_iota(jnp.int32, (R, R), 1)
                corner = jnp.where(row == col, -1.0 / (1.0 + up), c[:R, :R].astype(F32)).astype(BF16)
                c = jnp.concatenate(
                    [jnp.concatenate([corner, c[:R, R:]], axis=1), c[R:, :]], axis=0)
            parts.append(c)
        c = jnp.concatenate(parts, axis=0)
        di = jnp.dot(c, texts, preferred_element_type=F32)
        dt = lax.dot_general(c, images, TN, preferred_element_type=F32)
        accI[irows, :] = di if new_i else accI[irows, :] + di
        accT[trows, :] = dt if new_t else accT[trows, :] + dt

    feat_out.wait_recv()
    feats = FL[...]
    for third, (a_axis, b_axis, c_axis) in enumerate(AXES):
        def arrange(a, carry):
            s = lax.broadcasted_iota(jnp.int32, (4 * SLOT, 128), 0)
            b = over(s, SLOT)
            k = s - SLOT * b
            c = over(k, 18)
            r = (row_share(a_axis, ring_place(a, me[a_axis]))
                 + row_share(b_axis, ring_place(b, me[b_axis]))
                 + row_share(c_axis, c) + k - 18 * c)
            r = jnp.where(k < 72, r, -1)
            lane = lax.broadcasted_iota(jnp.int32, (4 * SLOT, 128), 1)
            pick = jnp.concatenate(
                [jnp.where(r == lane + 128 * j, 1.0, 0.0).astype(BF16) for j in range(D // 128)],
                axis=1)
            XP[third, pl.ds(pl.multiple_of(a * 4 * SLOT, 16), 4 * SLOT), :] = lax.dot_general(
                pick, feats, NT, preferred_element_type=F32).astype(BF16)
            return carry
        lax.fori_loop(0, 4, arrange, 0)

    far_in(ig, own, "yi")
    to_core((3, 0))
    far_in(tg, tslot, "yt")
    from_core((0, 0), (0, 1), (1, 0), (2, 0))
    unit(0, 1024, 0, 512, True, True, True)
    near_in(ig, 1)
    to_core((1, 1), (2, 1))
    near_in(tg, 1)
    unit(0, 1024, 512, 256, False, True)
    ig["far y"].wait_recv()
    to_core((3, 1))
    from_core((1, 1), (2, 1))
    unit(1024, 512, 0, 512, True)
    tg["far y"].wait_recv()
    from_core((3, 0), (3, 1))
    unit(1536, 512, 0, 512, True)
    unit(1536, 512, 512, 512)

    def rows(n, step):
        def one(k, carry):
            step(k * 16)
            return carry
        lax.fori_loop(0, n // 16, one, 0)

    def at(base, r, n=16):
        return pl.ds(pl.multiple_of(base + r, 16), n)

    core_out = {}

    def core_send(level):
        for k in (2 * level, 2 * level + 1):
            def step(r):
                SC[at(k * R, r), :] = accI[at((k * 2 + 1) * R, r), :].astype(BF16)
            rows(R, step)
            block = pl.ds(k * R, R)
            core_out[k] = send(SC.at[block, :], RC.at[block, :], "core")

    def core_wait(level):
        core_out[2 * level].wait_recv()
        core_out[2 * level + 1].wait_recv()

    def value_i(p, y, r):
        k = ORDER[p][y]
        return accI[at(k * 2 * R, r), :] + RC[at(k * R, r), :].astype(F32)

    def value_t(p, y, r):
        return accT[at(ORDER[p][y] * R, r), :]

    class Ring:
        def __init__(self, axis, n, lo, value, stage, rx, rf, sources=2):
            self.sources = sources
            self.axis, self.n, self.lo, self.got = axis, n, lo, {}
            self.value, self.stage, self.rx, self.rf = value, stage, rx, rf

        def piece(self, key, p, start, n, direction, dst, dst_start, add=None):
            def step(r):
                v = self.value(p, start + r)
                if add is not None:
                    v = v + add(r).astype(F32)
                self.stage(p)[at(start, r), :] = v.astype(BF16)
            rows(n, step)
            self.got[key] = send(self.stage(p).at[pl.ds(start, n), :],
                                 dst.at[pl.ds(dst_start, n), :], self.axis + direction)

        def far(self, add=None):
            lo, hi = self.lo, self.n - self.lo
            high = None if add is None else lambda r: add(lo + r)
            self.piece("far+", 3, 0, lo, "+", self.rx(0), 0, add)
            self.piece("far-", 3, lo, hi, "-", self.rx(1), 0, high)

        def near(self):
            self.piece("b+", 1, self.lo, self.n - self.lo, "+", self.rf(0), self.lo)
            self.piece("a-", 2, 0, self.lo, "-", self.rf(1), 0)

        def whole(self):
            self.piece("a+", 1, 0, self.n, "+", self.rf(0), 0)
            self.piece("a-", 2, 0, self.n, "-", self.rf(1), 0)

        def direct(self):
            for k, (p, there) in enumerate(((3, "2"), (1, "+"), (2, "-"))):
                self.piece(there, p, 0, self.n, there, self.rf(k), 0)

        def onward(self):
            lo, hi = self.lo, self.n - self.lo
            self.got["far+"].wait_recv()
            self.piece("a+", 1, 0, lo, "+", self.rf(0), 0, lambda r: self.rx(0)[at(0, r), :])
            self.got["far-"].wait_recv()
            self.piece("b-", 2, lo, hi, "-", self.rf(1), lo, lambda r: self.rx(1)[at(0, r), :])

        def arrive(self):
            for key in ("a+", "b+", "a-", "b-", "+", "-", "2"):
                if key in self.got:
                    self.got[key].wait_recv()

        def total(self, r):
            v = self.value(0, r)
            for k in range(self.sources):
                v = v + self.rf(k)[at(0, r), :].astype(F32)
            return v

    def block_ring(axis, y, value, stage, rx, rf):
        return Ring(
            axis, R, H, lambda p, r: value(p, y, r),
            lambda p: stage.at[pl.ds(ORDER[p][y] * R, R), :],
            lambda d: rx.at[pl.ds(d * H, H), :],
            lambda d: rf.at[pl.ds((d * 2 + y) * R, R), :])

    ring_i = [block_ring("x", y, value_i, SXI, RXI, RFI) for y in range(2)]
    ring_t = [block_ring("z", y, value_t, SXT, RXT, RFT) for y in range(2)]

    def every(rings, what):
        for ring in rings:
            getattr(ring, what)()

    def cross(rings, n, to):
        rings[1].arrive()

        def step(r):
            SY[at(n * R, r), :] = rings[1].total(r).astype(BF16)
        rows(R, step)
        mine = pl.ds(n * R, R)
        return send(SY.at[mine, :], RY.at[mine, :], to)

    def finish(rings, n, crossed, unit_ref, inv_ref, gp):
        rings[0].arrive()
        crossed.wait_recv()
        t = jnp.exp(jnp.full((1, D), ls_ref[0], F32))

        def step(r):
            g = (rings[0].total(r) + RY[at(n * R, r), :].astype(F32)) * t
            u = unit_ref[at(0, r), :]
            inv = inv_ref[at(0, r), :][:, 0:1]
            along = jnp.sum(u * g, axis=1, keepdims=True)
            gp[at(0, r), :] = (inv * (g - u * along)).astype(BF16)
        rows(R, step)

    def feature_grad(gp, w_ref, lo):
        gf_ref[lo:lo + R, :] = lax.dot_general(
            gp[...], w_ref[...], NT, preferred_element_type=F32).astype(BF16)

    def far_over(ring, n, to):
        def step(r):
            SF[at(n * R, r), :] = ring.value(3, r).astype(BF16)
        rows(R, step)
        mine = pl.ds(n * R, R)
        return send(SF.at[mine, :], RYF.at[mine, :], to)

    def far_sum(ring, n, over_y):
        over_y.wait_recv()
        ring.far(lambda r: RYF[at(n * R, r), :])

    core_send(3)
    unit(1024, 512, 512, 512)
    core_send(2)
    core_wait(3)
    over_i = far_over(ring_i[1], 0, "yi")
    core_wait(2)
    ring_i[1].whole()
    unit(0, 1024, 768, 256)
    over_t = far_over(ring_t[1], 1, "yt")
    core_send(1)
    core_send(0)
    ring_t[1].whole()
    far_sum(ring_i[0], 0, over_i)
    core_wait(1)
    ring_i[0].near()
    ring_t[0].near()
    far_sum(ring_t[0], 1, over_t)
    core_wait(0)
    cross_i = cross(ring_i, 0, "yi")
    ring_i[0].onward()
    cross_t = cross(ring_t, 1, "yt")
    ring_t[0].onward()
    finish(ring_i, 0, cross_i, unitI, invI, gpI)
    finish(ring_t, 1, cross_t, unitT, invT, gpT)

    GL[0:R, :] = jnp.where(first, gpI[...], gpT[...])
    feat_out.wait_send()
    OUT[...] = jnp.where(first, gpT[...], gpI[...])
    grad_in = send(OUT, GL.at[pl.ds(R, R), :], "core")

    def columns(third):
        return slice(third * 384, third * 384 + 384)

    def products(a):
        for third in range(3):
            accI[a * 4 * SLOT:(a + 1) * 4 * SLOT, columns(third)] = jnp.dot(
                XP[third, a * 4 * SLOT:(a + 1) * 4 * SLOT, :], GL[:, columns(third)],
                preferred_element_type=F32)

    def weight_ring(third, axis, n, lo, stage, rx, rf, sources):
        return Ring(
            axis, n, lo, lambda p, r: accI[at(p * n, r), columns(third)],
            lambda p: stage.at[third, pl.ds(p * n, n), :],
            lambda d: rx.at[third, d], lambda d: rf.at[third, d], sources)

    outer = [weight_ring(k, AXES[k][0], 4 * SLOT, 2 * SLOT, S1, RX1, RF1, 2) for k in range(3)]
    inner = [weight_ring(k, AXES[k][1], SLOT, 0, S2, None, RF2, 3) for k in range(3)]
    grad_in.wait_recv()
    products(3)
    every(outer, "far")
    products(1)
    products(2)
    every(outer, "near")
    every(outer, "onward")
    products(0)
    feature_grad(gpI, WI, 0)
    feature_grad(gpT, WT, R)
    for third in range(3):
        outer[third].arrive()

        def step(r):
            accI[at(0, r), columns(third)] = outer[third].total(r)
        rows(4 * SLOT, step)
        inner[third].direct()
    last = []
    for third in range(3):
        inner[third].arrive()

        def step(r):
            Z[third, at(0, r), :] = inner[third].total(r).astype(BF16)
        rows(SLOT, step)
        for k, there in enumerate("+-2"):
            last.append(send(Z.at[third, pl.ds(0, SLOT), :],
                             Z.at[third, pl.ds((k + 1) * SLOT, SLOT), :], AXES[third][2] + there))
    for third in range(3):
        for copy in last[third * 3:third * 3 + 3]:
            copy.wait_recv()
        row = lax.broadcasted_iota(jnp.int32, (32, 4 * SLOT), 0)
        k = lax.broadcasted_iota(jnp.int32, (32, 4 * SLOT), 1)
        k = k - SLOT * over(k, SLOT)
        theirs = (row >= 16).astype(jnp.int32)
        i = row - 16 * theirs
        core = theirs + me["core"] - 2 * theirs * me["core"]
        want = me[AXES[third][2]] * 18 + core * 9 + i
        pick = jnp.where((k == want) & (i < 9), 1.0, 0.0).astype(BF16)
        DM[:, columns(third)] = jnp.dot(pick, Z[third], preferred_element_type=F32)
    swap = send(DM.at[pl.ds(16, 16), :], DR, "core")
    swap.wait_recv()
    dw_ref[0:16, :] = jnp.where(first, DM[0:16, :], DR[...])
    dw_ref[16:32, :] = jnp.where(first, DR[...], DM[0:16, :])
    for copy in sent:
        if copy is not feat_out:
            copy.wait_send()


def fused(img_feat, txt_feat, w_img, w_txt, ls, bias):
    D = img_feat.shape[1]
    vmem = pl.BlockSpec(memory_space=pltpu.VMEM)
    hbm = pl.BlockSpec(memory_space=pl.ANY)
    smem = pl.BlockSpec(memory_space=pltpu.SMEM)
    sizes = [(2048, BF16), (1024, BF16), (2048, F32), (1024, F32), (1024, BF16), (1024, BF16),
             (1024, BF16), (1024, BF16), (R, BF16), (R, BF16), (512, BF16), (512, BF16),
             (256, BF16), (256, BF16), (256, BF16), (256, BF16), (D, BF16), (D, BF16),
             (R, BF16), (R, BF16), (R, F32), (R, F32), (R, BF16), (R, BF16),
             (2 * R, BF16), (2 * R, BF16), (R, BF16)]
    thirds = [(4 * 4 * SLOT,), (2, 2 * SLOT), (2, 4 * SLOT), (4 * SLOT,), (3, SLOT),
              (4 * SLOT,)]
    return pl.pallas_call(
        kernel,
        out_shape=(jax.ShapeDtypeStruct((2 * R, D), BF16), jax.ShapeDtypeStruct((32, D), F32)),
        in_specs=[hbm] * 4 + [smem] * 2,
        out_specs=(vmem,) * 2,
        scratch_shapes=[pltpu.VMEM((n, D), t) for n, t in sizes]
        + [pltpu.VMEM((R, 128), F32)] * 2
        + [pltpu.VMEM((3, 16 * SLOT, 2 * R), BF16)]
        + [pltpu.VMEM((3,) + n + (D // 3,), BF16) for n in thirds]
        + [pltpu.VMEM((32, D), F32), pltpu.VMEM((16, D), F32)]
        + [pltpu.SemaphoreType.DMA((4,))] + [pltpu.SemaphoreType.DMA((120,))] * 2,
        compiler_params=pltpu.CompilerParams(
            collective_id=0, has_side_effects=True, vmem_limit_bytes=62 * 2**20),
    )(img_feat, txt_feat, w_img, w_txt, ls, bias)


def body(img_feat, txt_feat, w_img, w_txt, logit_scale_log, bias):
    gf, dw = fused(img_feat, txt_feat, w_img, w_txt, logit_scale_log, bias)
    return gf[:R], gf[R:], dw[0:9], dw[16:25]


def solution(mesh):
    rows = P(("blk", "group"), None)
    return jax.shard_map(
        body, mesh=mesh, in_specs=(rows, rows, P(), P(), P(), P()),
        out_specs=(rows,) * 4, check_vma=False)
```

```python
import jax
import jax.numpy as jnp
from jax import lax
from jax.experimental import pallas as pl
from jax.experimental.pallas import tpu as pltpu
from jax.sharding import PartitionSpec as P

R = 128
H = 64
LOG2E = 1.4426950408889634
NT = (((1,), (1,)), ((), ()))
TN = (((0,), (0,)), ((), ()))
F32 = jnp.float32
BF16 = jnp.bfloat16


AXES = (("z", "x", "y"), ("x", "y", "z"), ("y", "z", "x"))
SLOT = 80


def place():
    b, g = lax.axis_index("blk"), lax.axis_index("group")
    return {"x": g // 4, "y": (g // 2) % 2 * 2 + b % 2, "z": b // 2, "core": g % 2}


def neighbours(me):
    def device(**moved):
        c = {**me, **moved}
        return (c["z"] * 2 + c["y"] % 2, c["x"] * 4 + c["y"] // 2 * 2 + c["core"])

    near = {"core": device(core=1 - me["core"])}
    for axis in "xyz":
        for name, step in (("+", 1), ("-", 3), ("2", 2)):
            moved = {axis: (me[axis] + step) % 4}
            near[axis + name] = device(**moved)
            near[axis + name + "c"] = device(**moved, core=1 - me["core"])
    greeted = list(near.values())
    near["yi"] = device(y=me["y"] + 1 - 2 * (me["y"] % 2))
    near["yt"] = device(y=3 - me["y"])
    return near, greeted


def ring_place(p, here):
    step = jnp.where(p == 1, 1, jnp.where(p == 2, 3, jnp.where(p == 3, 2, 0)))
    return (here + step) & 3


def row_share(axis, v):
    if axis == "y":
        return (v & 1) * 144 + (v >> 1) * 18
    return v * (288 if axis == "z" else 36)


def over(v, step):
    return sum((v >= step * k).astype(jnp.int32) for k in range(1, 4))


def kernel(img_hbm, txt_hbm, wi_hbm, wt_hbm, ls_ref, bias_ref,
           gf_ref, dw_ref,
           I, T, accI, accT, SC, RC, SXI, SXT, RXI, RXT, RFI, RFT, SY, RY, SF, RYF, WI, WT, IMG, TXT,
           unitI, unitT, gpI, gpT, FL, GL, OUT, invI, invT,
           XP, S1, RX1, RF1, S2, RF2, E, Z, lsem, ssem, rsem):
    D = IMG.shape[1]
    loads = [pltpu.make_async_copy(src, dst, lsem.at[k]) for k, (src, dst) in enumerate(
        ((img_hbm, IMG), (wi_hbm, WI), (txt_hbm, TXT), (wt_hbm, WT)))]
    for load in loads:
        load.start()
    me = place()
    near, greeted = neighbours(me)
    first = me["core"] == 0
    barrier = pltpu.get_barrier_semaphore()
    for there in greeted:
        pl.semaphore_signal(barrier, inc=1, device_id=there, device_id_type=pl.DeviceIdType.MESH)

    sent = []

    def send(src, dst, to):
        k = len(sent)
        copy = pltpu.make_async_remote_copy(
            src_ref=src, dst_ref=dst, send_sem=ssem.at[k], recv_sem=rsem.at[k],
            device_id=near[to], device_id_type=pl.DeviceIdType.MESH)
        copy.start()
        sent.append(copy)
        return copy

    def project(feat, w, unit, inv, emb):
        p = jnp.dot(feat[...], w[...], preferred_element_type=F32)
        r = lax.rsqrt(jnp.sum(p * p, axis=1, keepdims=True) + 1e-06)
        u = p * r
        unit[...] = u
        inv[...] = jnp.broadcast_to(r, (R, 128))
        emb[0:R, :] = u.astype(BF16)

    ORDER = ((0, 1), (2, 4), (3, 5), (6, 7))

    def islot(p, y, c=0, lo=0, n=R):
        return I.at[pl.ds((ORDER[p][y] * 2 + c) * R + lo, n), :]

    def tslot(p, y, lo=0, n=R):
        return T.at[pl.ds(ORDER[p][y] * R + lo, n), :]

    def own(p, y, lo=0, n=R):
        return islot(p, y, 0, lo, n)

    ig, tg, core_in = {}, {}, {}

    def spread(got, slot, y, ring):
        got["+", y] = send(slot(0, y), slot(2, y), ring + "+")
        got["-", y] = send(slot(0, y), slot(1, y), ring + "-")

    def near_in(got, y):
        got["+", y].wait_recv()
        got["-", y].wait_recv()

    def onward_halves(got, slot, ring):
        got["far+"] = send(slot(2, 0, 0, H), slot(3, 0, 0, H), ring + "+")
        got["far-"] = send(slot(1, 0, H, H), slot(3, 0, H, H), ring + "-")

    def far_in(got, slot, to):
        got["far+"].wait_recv()
        got["far-"].wait_recv()
        got["far y"] = send(slot(3, 0), slot(3, 1), to)

    def to_core(*places):
        for p, y in places:
            core_in[p, y] = send(islot(p, y, 0), islot(p, y, 1), "core")

    def from_core(*places):
        for place_y in places:
            core_in[place_y].wait_recv()

    loads[0].wait()
    loads[1].wait()
    project(IMG, WI, unitI, invI, I)
    pl.semaphore_wait(barrier, len(greeted))
    ig["y"] = send(own(0, 0), own(0, 1), "yi")
    spread(ig, own, 0, "x")
    to_core((0, 0))
    loads[2].wait()
    loads[3].wait()
    project(TXT, WT, unitT, invT, T)
    tg["y"] = send(tslot(0, 0), tslot(0, 1), "yt")
    spread(tg, tslot, 0, "z")
    FL[0:R, :] = jnp.where(first, IMG[...], TXT[...])
    OUT[...] = jnp.where(first, TXT[...], IMG[...])
    feat_out = send(OUT, FL.at[pl.ds(R, R), :], "core")
    accT[768:1024, :] = jnp.zeros((256, D), F32)

    feat_out.wait_recv()
    feats = FL[...]
    for third, (a_axis, b_axis, c_axis) in enumerate(AXES):
        def arrange(a, carry):
            s = lax.broadcasted_iota(jnp.int32, (4 * SLOT, 128), 0)
            b = over(s, SLOT)
            k = s - SLOT * b
            c = over(k, 18)
            r = (row_share(a_axis, ring_place(a, me[a_axis]))
                 + row_share(b_axis, ring_place(b, me[b_axis]))
                 + row_share(c_axis, c) + k - 18 * c)
            r = jnp.where(k < 72, r, -1)
            lane = lax.broadcasted_iota(jnp.int32, (4 * SLOT, 128), 1)
            pick = jnp.concatenate(
                [jnp.where(r == lane + 128 * j, 1.0, 0.0).astype(BF16) for j in range(D // 128)],
                axis=1)
            XP[third, pl.ds(pl.multiple_of(a * 4 * SLOT, 16), 4 * SLOT), :] = lax.dot_general(
                pick, feats, NT, preferred_element_type=F32).astype(BF16)
            return carry
        lax.fori_loop(0, 4, arrange, 0)

    near_in(ig, 0)
    onward_halves(ig, own, "x")
    to_core((1, 0), (2, 0))
    near_in(tg, 0)
    onward_halves(tg, tslot, "z")
    ig["y"].wait_recv()
    spread(ig, own, 1, "x")
    to_core((0, 1))
    tg["y"].wait_recv()
    spread(tg, tslot, 1, "z")

    scale = jnp.exp(jnp.full((1, 512), ls_ref[0], F32))
    slope = scale * (-LOG2E)
    offset = jnp.full((1, 512), bias_ref[0], F32) * (-LOG2E)

    def unit(ilo, m, tlo, n, new_i=False, new_t=False, diag=False):
        irows, trows = slice(ilo, ilo + m), slice(tlo, tlo + n)
        images, texts = I[irows, :], T[trows, :]
        parts = []
        for k in range(0, m, 256):
            s = lax.dot_general(I[ilo + k:ilo + k + 256, :], texts, NT, preferred_element_type=F32)
            x = s * slope[:, :n] + offset[:, :n]
            c = pltpu.reciprocal(1.0 + jnp.exp2(jnp.minimum(x, 126.0)), approx=True).astype(BF16)
            if diag and k == 0:
                up = jnp.exp2(jnp.minimum(-x[:R, :R], 126.0))
                row = lax.broadcasted_iota(jnp.int32, (R, R), 0)
                col = lax.broadcasted_iota(jnp.int32, (R, R), 1)
                corner = jnp.where(row == col, -1.0 / (1.0 + up), c[:R, :R].astype(F32)).astype(BF16)
                c = jnp.concatenate(
                    [jnp.concatenate([corner, c[:R, R:]], axis=1), c[R:, :]], axis=0)
            parts.append(c)
        c = jnp.concatenate(parts, axis=0)
        di = jnp.dot(c, texts, preferred_element_type=F32)
        dt = lax.dot_general(c, images, TN, preferred_element_type=F32)
        accI[irows, :] = di if new_i else accI[irows, :] + di
        accT[trows, :] = dt if new_t else accT[trows, :] + dt

    far_in(ig, own, "yi")
    to_core((3, 0))
    far_in(tg, tslot, "yt")
    from_core((0, 0), (0, 1), (1, 0), (2, 0))
    unit(0, 1024, 0, 512, True, True, True)
    near_in(ig, 1)
    to_core((1, 1), (2, 1))
    near_in(tg, 1)
    unit(0, 1024, 512, 256, False, True)
    ig["far y"].wait_recv()
    to_core((3, 1))
    from_core((1, 1), (2, 1))
    unit(1024, 512, 0, 512, True)
    unit(1024, 512, 512, 256)
    tg["far y"].wait_recv()
    from_core((3, 0), (3, 1))
    unit(1536, 512, 0, 512, True)
    unit(1536, 512, 512, 512)

    def rows(n, step, size=32):
        def one(k, carry):
            step(k * size, size)
            return carry
        lax.fori_loop(0, n // size, one, 0)

    def at(base, r, n):
        return pl.ds(pl.multiple_of(base + r, 16), n)

    core_out = {}

    def core_send(level):
        for k in (2 * level, 2 * level + 1):
            def step(r, w):
                SC[at(k * R, r, w), :] = accI[at((k * 2 + 1) * R, r, w), :].astype(BF16)
            rows(R, step)
            block = pl.ds(k * R, R)
            core_out[k] = send(SC.at[block, :], RC.at[block, :], "core")

    def core_wait(level):
        core_out[2 * level].wait_recv()
        core_out[2 * level + 1].wait_recv()

    def value_i(p, y, r, w):
        k = ORDER[p][y]
        return accI[at(k * 2 * R, r, w), :] + RC[at(k * R, r, w), :].astype(F32)

    def value_t(p, y, r, w):
        return accT[at(ORDER[p][y] * R, r, w), :]

    class Ring:
        def __init__(self, axis, n, lo, value, stage, rx, rf, sources=2, size=32):
            self.sources, self.size = sources, size
            self.axis, self.n, self.lo, self.got = axis, n, lo, {}
            self.value, self.stage, self.rx, self.rf = value, stage, rx, rf

        def piece(self, key, p, start, n, direction, dst, dst_start, add=None):
            def step(r, w):
                v = self.value(p, start + r, w)
                if add is not None:
                    v = v + add(r, w).astype(F32)
                self.stage(p)[at(start, r, w), :] = v.astype(BF16)
            rows(n, step, self.size)
            self.launch(key, p, start, n, direction, dst, dst_start)

        def launch(self, key, p, start, n, direction, dst, dst_start):
            self.got[key] = send(self.stage(p).at[pl.ds(start, n), :],
                                 dst.at[pl.ds(dst_start, n), :], self.axis + direction)

        def far(self, add=None):
            lo, hi = self.lo, self.n - self.lo
            high = None if add is None else lambda r, w: add(lo + r, w)
            self.piece("far+", 3, 0, lo, "+", self.rx(0), 0, add)
            self.piece("far-", 3, lo, hi, "-", self.rx(1), 0, high)

        def near(self):
            self.piece("b+", 1, self.lo, self.n - self.lo, "+", self.rf(0), self.lo)
            self.piece("a-", 2, 0, self.lo, "-", self.rf(1), 0)

        def whole(self):
            self.piece("a+", 1, 0, self.n, "+", self.rf(0), 0)
            self.piece("a-", 2, 0, self.n, "-", self.rf(1), 0)

        def direct(self):
            for k, (p, there) in enumerate(((3, "2"), (1, "+"), (2, "-"))):
                self.piece(there, p, 0, self.n, there, self.rf(k), 0)

        def onward(self):
            lo, hi = self.lo, self.n - self.lo
            self.got["far+"].wait_recv()
            self.piece("a+", 1, 0, lo, "+", self.rf(0), 0, lambda r, w: self.rx(0)[at(0, r, w), :])
            self.got["far-"].wait_recv()
            self.piece("b-", 2, lo, hi, "-", self.rf(1), lo, lambda r, w: self.rx(1)[at(0, r, w), :])

        def arrive(self):
            for key in ("a+", "b+", "a-", "b-", "+", "-", "2"):
                if key in self.got:
                    self.got[key].wait_recv()

        def staged_far(self):
            lo, hi = self.lo, self.n - self.lo
            self.launch("far+", 3, 0, lo, "+", self.rx(0), 0)
            self.launch("far-", 3, lo, hi, "-", self.rx(1), 0)

        def staged_near(self):
            self.launch("b+", 1, self.lo, self.n - self.lo, "+", self.rf(0), self.lo)
            self.launch("a-", 2, 0, self.lo, "-", self.rf(1), 0)

        def total(self, r, w):
            v = self.value(0, r, w)
            for k in range(self.sources):
                v = v + self.rf(k)[at(0, r, w), :].astype(F32)
            return v

    def block_ring(axis, y, value, stage, rx, rf):
        return Ring(
            axis, R, H, lambda p, r, w: value(p, y, r, w),
            lambda p: stage.at[pl.ds(ORDER[p][y] * R, R), :],
            lambda d: rx.at[pl.ds(d * H, H), :],
            lambda d: rf.at[pl.ds((d * 2 + y) * R, R), :])

    ring_i = [block_ring("x", y, value_i, SXI, RXI, RFI) for y in range(2)]
    ring_t = [block_ring("z", y, value_t, SXT, RXT, RFT) for y in range(2)]

    def every(rings, what):
        for ring in rings:
            getattr(ring, what)()

    def cross(rings, n, to):
        rings[1].arrive()

        def step(r, w):
            SY[at(n * R, r, w), :] = rings[1].total(r, w).astype(BF16)
        rows(R, step)
        mine = pl.ds(n * R, R)
        return send(SY.at[mine, :], RY.at[mine, :], to)

    def finish(rings, n, crossed, unit_ref, inv_ref, gp):
        rings[0].arrive()
        crossed.wait_recv()
        t = jnp.exp(jnp.full((1, D), ls_ref[0], F32))

        def step(r, w):
            g = (rings[0].total(r, w) + RY[at(n * R, r, w), :].astype(F32)) * t
            u = unit_ref[at(0, r, w), :]
            inv = inv_ref[at(0, r, w), :][:, 0:1]
            along = jnp.sum(u * g, axis=1, keepdims=True)
            gp[at(0, r, w), :] = (inv * (g - u * along)).astype(BF16)
        rows(R, step, 16)

    def feature_grad(gp, w_ref, lo):
        gf_ref[lo:lo + R, :] = lax.dot_general(
            gp[...], w_ref[...], NT, preferred_element_type=F32).astype(BF16)

    def far_over(ring, n, to):
        def step(r, w):
            SF[at(n * R, r, w), :] = ring.value(3, r, w).astype(BF16)
        rows(R, step)
        mine = pl.ds(n * R, R)
        return send(SF.at[mine, :], RYF.at[mine, :], to)

    def far_sum(ring, n, over_y):
        over_y.wait_recv()
        ring.far(lambda r, w: RYF[at(n * R, r, w), :])

    core_send(3)
    unit(1024, 512, 768, 256)
    core_send(2)
    core_wait(3)
    over_i = far_over(ring_i[1], 0, "yi")
    core_wait(2)
    ring_i[1].whole()
    unit(0, 1024, 768, 256)
    over_t = far_over(ring_t[1], 1, "yt")
    core_send(1)
    core_send(0)
    ring_t[1].whole()
    far_sum(ring_i[0], 0, over_i)
    core_wait(1)
    ring_i[0].near()
    core_wait(0)
    cross_i = cross(ring_i, 0, "yi")
    far_sum(ring_t[0], 1, over_t)
    ring_t[0].near()
    cross_t = cross(ring_t, 1, "yt")
    ring_i[0].onward()
    ring_t[0].onward()
    finish(ring_i, 0, cross_i, unitI, invI, gpI)
    finish(ring_t, 1, cross_t, unitT, invT, gpT)

    GL[0:R, :] = jnp.where(first, gpI[...], gpT[...])
    feat_out.wait_send()
    OUT[...] = jnp.where(first, gpT[...], gpI[...])
    grad_in = send(OUT, GL.at[pl.ds(R, R), :], "core")

    def columns(third):
        return slice(third * 384, third * 384 + 384)

    def product(third, lo, n):
        return jnp.dot(XP[third, lo:lo + n, :], GL[:, columns(third)], preferred_element_type=F32)

    def weight_ring(third, axis, n, lo, stage, rx, rf, sources):
        return Ring(
            axis, n, lo, lambda p, r, w: accI[at(p * n, r, w), columns(third)],
            lambda p: stage.at[third, pl.ds(p * n, n), :],
            lambda d: rx.at[third, d], lambda d: rf.at[third, d], sources, SLOT)

    N, half = 4 * SLOT, 2 * SLOT
    outer = [weight_ring(k, AXES[k][0], N, half, S1, RX1, RF1, 2) for k in range(3)]
    inner = [weight_ring(k, AXES[k][1], SLOT, 0, S2, None, RF2, 3) for k in range(3)]
    grad_in.wait_recv()
    for third in range(3):
        S1[third, 3 * N:4 * N, :] = product(third, 3 * N, N).astype(BF16)
        outer[third].staged_far()
    for third in range(3):
        v = product(third, N, N)
        accI[N:N + half, columns(third)] = v[:half]
        S1[third, N + half:2 * N, :] = v[half:].astype(BF16)
        v = product(third, 2 * N, N)
        S1[third, 2 * N:2 * N + half, :] = v[:half].astype(BF16)
        accI[2 * N + half:3 * N, columns(third)] = v[half:]
        outer[third].staged_near()
    every(outer, "onward")
    for third in range(3):
        accI[0:N, columns(third)] = product(third, 0, N)
    feature_grad(gpI, WI, 0)
    feature_grad(gpT, WT, R)
    for third in range(3):
        outer[third].arrive()

        def step(r, w):
            accI[at(0, r, w), columns(third)] = outer[third].total(r, w)
        rows(N, step, SLOT)
        inner[third].direct()

    last = []
    for third in range(3):
        c_axis = AXES[third][2]
        row = lax.broadcasted_iota(jnp.int32, (R, SLOT), 0)
        k = lax.broadcasted_iota(jnp.int32, (R, SLOT), 1)
        block, i = row >> 4, row & 15
        other = block & 1
        core = other + me["core"] - 2 * other * me["core"]
        want = ring_place(block >> 1, me[c_axis]) * 18 + core * 9 + i
        pick = jnp.where((k == want) & (i < 9), 1.0, 0.0).astype(BF16)
        inner[third].arrive()
        mine = inner[third].total(0, SLOT).astype(BF16)
        E[third] = jnp.dot(pick, mine, preferred_element_type=F32).astype(BF16)
        for j, there in enumerate(("core", "+", "+c", "-", "-c", "2", "2c"), 1):
            some = pl.ds(j * 16, 16)
            last.append(send(E.at[third, some, :], Z.at[third, some, :],
                             there if j == 1 else c_axis + there))
    for third in range(3):
        for copy in last[third * 7:third * 7 + 7]:
            copy.wait_recv()
        z = Z[third, 16:128, :].astype(F32)
        same = E[third, 0:16, :].astype(F32) + z[16:32] + z[48:64] + z[80:96]
        swapped = z[0:16] + z[32:48] + z[64:80] + z[96:112]
        dw_ref[0:16, columns(third)] = jnp.where(first, same, swapped)
        dw_ref[16:32, columns(third)] = jnp.where(first, swapped, same)
    for copy in sent:
        if copy is not feat_out:
            copy.wait_send()


def fused(img_feat, txt_feat, w_img, w_txt, ls, bias):
    D = img_feat.shape[1]
    vmem = pl.BlockSpec(memory_space=pltpu.VMEM)
    hbm = pl.BlockSpec(memory_space=pl.ANY)
    smem = pl.BlockSpec(memory_space=pltpu.SMEM)
    sizes = [(2048, BF16), (1024, BF16), (2048, F32), (1024, F32), (1024, BF16), (1024, BF16),
             (1024, BF16), (1024, BF16), (R, BF16), (R, BF16), (512, BF16), (512, BF16),
             (256, BF16), (256, BF16), (256, BF16), (256, BF16), (D, BF16), (D, BF16),
             (R, BF16), (R, BF16), (R, F32), (R, F32), (R, BF16), (R, BF16),
             (2 * R, BF16), (2 * R, BF16), (R, BF16)]
    thirds = [(4 * 4 * SLOT,), (2, 2 * SLOT), (2, 4 * SLOT), (4 * SLOT,), (3, SLOT), (R,), (R,)]
    return pl.pallas_call(
        kernel,
        out_shape=(jax.ShapeDtypeStruct((2 * R, D), BF16), jax.ShapeDtypeStruct((32, D), F32)),
        in_specs=[hbm] * 4 + [smem] * 2,
        out_specs=(vmem,) * 2,
        scratch_shapes=[pltpu.VMEM((n, D), t) for n, t in sizes]
        + [pltpu.VMEM((R, 128), F32)] * 2
        + [pltpu.VMEM((3, 16 * SLOT, 2 * R), BF16)]
        + [pltpu.VMEM((3,) + n + (D // 3,), BF16) for n in thirds]
        + [pltpu.SemaphoreType.DMA((4,))] + [pltpu.SemaphoreType.DMA((120,))] * 2,
        compiler_params=pltpu.CompilerParams(
            collective_id=0, has_side_effects=True, vmem_limit_bytes=62 * 2**20),
    )(img_feat, txt_feat, w_img, w_txt, ls, bias)


def body(img_feat, txt_feat, w_img, w_txt, logit_scale_log, bias):
    gf, dw = fused(img_feat, txt_feat, w_img, w_txt, logit_scale_log, bias)
    return gf[:R], gf[R:], dw[0:9], dw[16:25]


def solution(mesh):
    rows = P(("blk", "group"), None)
    return jax.shard_map(
        body, mesh=mesh, in_specs=(rows, rows, P(), P(), P(), P()),
        out_specs=(rows,) * 4, check_vma=False)
```

```python
import jax
import jax.numpy as jnp
from jax import lax
from jax.experimental import pallas as pl
from jax.experimental.pallas import tpu as pltpu
from jax.sharding import PartitionSpec as P

R = 128
H = 64
LOG2E = 1.4426950408889634
NT = (((1,), (1,)), ((), ()))
TN = (((0,), (0,)), ((), ()))
F32 = jnp.float32
BF16 = jnp.bfloat16


AXES = (("z", "x", "y"), ("x", "y", "z"), ("y", "z", "x"))
SLOT = 80


def place():
    b, g = lax.axis_index("blk"), lax.axis_index("group")
    return {"x": g // 4, "y": (g // 2) % 2 * 2 + b % 2, "z": b // 2, "core": g % 2}


def neighbours(me):
    def device(**moved):
        c = {**me, **moved}
        return (c["z"] * 2 + c["y"] % 2, c["x"] * 4 + c["y"] // 2 * 2 + c["core"])

    near = {"core": device(core=1 - me["core"])}
    for axis in "xyz":
        for name, step in (("+", 1), ("-", 3), ("2", 2)):
            moved = {axis: (me[axis] + step) % 4}
            near[axis + name] = device(**moved)
            near[axis + name + "c"] = device(**moved, core=1 - me["core"])
    greeted = list(near.values())
    near["yi"] = device(y=me["y"] + 1 - 2 * (me["y"] % 2))
    near["yt"] = device(y=3 - me["y"])
    return near, greeted


def ring_place(p, here):
    step = jnp.where(p == 1, 1, jnp.where(p == 2, 3, jnp.where(p == 3, 2, 0)))
    return (here + step) & 3


def row_share(axis, v):
    if axis == "y":
        return (v & 1) * 144 + (v >> 1) * 18
    return v * (288 if axis == "z" else 36)


def over(v, step):
    return sum((v >= step * k).astype(jnp.int32) for k in range(1, 4))


def kernel(img_hbm, txt_hbm, wi_hbm, wt_hbm, ls_ref, bias_ref,
           gf_ref, dw_ref,
           I, T, accI, accT, SC, RC, SXI, SXT, RXI, RXT, RFI, RFT, SY, RY, SF, RYF, WI, WT, IMG, TXT,
           unitI, unitT, gpI, gpT, FL, GL, OUT, invI, invT,
           XP, S1, RX1, RF1, S2, RF2, E, Z, lsem, ssem, rsem):
    D = IMG.shape[1]
    loads = [pltpu.make_async_copy(src, dst, lsem.at[k]) for k, (src, dst) in enumerate(
        ((img_hbm, IMG), (wi_hbm, WI), (txt_hbm, TXT), (wt_hbm, WT)))]
    for load in loads[:2]:
        load.start()
    me = place()
    near, greeted = neighbours(me)
    first = me["core"] == 0
    barrier = pltpu.get_barrier_semaphore()
    for there in greeted:
        pl.semaphore_signal(barrier, inc=1, device_id=there, device_id_type=pl.DeviceIdType.MESH)

    sent = []

    def send(src, dst, to):
        k = len(sent)
        copy = pltpu.make_async_remote_copy(
            src_ref=src, dst_ref=dst, send_sem=ssem.at[k], recv_sem=rsem.at[k],
            device_id=near[to], device_id_type=pl.DeviceIdType.MESH)
        copy.start()
        sent.append(copy)
        return copy

    def project(feat, w, unit, inv, emb):
        p = jnp.dot(feat[...], w[...], preferred_element_type=F32)
        r = lax.rsqrt(jnp.sum(p * p, axis=1, keepdims=True) + 1e-06)
        u = p * r
        unit[...] = u
        inv[...] = jnp.broadcast_to(r, (R, 128))
        emb[0:R, :] = u.astype(BF16)

    ORDER = ((0, 1), (2, 4), (3, 5), (6, 7))

    def islot(p, y, c=0, lo=0, n=R):
        return I.at[pl.ds((ORDER[p][y] * 2 + c) * R + lo, n), :]

    def tslot(p, y, lo=0, n=R):
        return T.at[pl.ds(ORDER[p][y] * R + lo, n), :]

    def own(p, y, lo=0, n=R):
        return islot(p, y, 0, lo, n)

    ig, tg, core_in = {}, {}, {}

    def spread(got, slot, y, ring, halves=(0, 1)):
        for h in halves:
            got["+", y, h] = send(slot(0, y, h * H, H), slot(2, y, h * H, H), ring + "+")
            low = h * H if y else H - h * H
            got["-", y, h] = send(slot(0, y, low, H), slot(1, y, low, H), ring + "-")

    def to_y(got, slot, to):
        for h in range(2):
            got["y", h] = send(slot(0, 0, h * H, H), slot(0, 1, h * H, H), to)

    def pass_on(got, slot, ring):
        got["+", 0, 0].wait_recv()
        got["far+"] = send(slot(2, 0, 0, H), slot(3, 0, 0, H), ring + "+")
        got["-", 0, 0].wait_recv()
        got["far-"] = send(slot(1, 0, H, H), slot(3, 0, H, H), ring + "-")
        got["y", 0].wait_recv()
        spread(got, slot, 1, ring, (0,))

    def pass_rest(got, slot, ring):
        got["y", 1].wait_recv()
        spread(got, slot, 1, ring, (1,))
        got["+", 0, 1].wait_recv()
        got["-", 0, 1].wait_recv()

    def second_in(got):
        for d in "+-":
            for h in range(2):
                got[d, 1, h].wait_recv()

    def far_in(got, slot, to):
        got["far+"].wait_recv()
        got["far-"].wait_recv()
        got["far y"] = send(slot(3, 0), slot(3, 1), to)

    def to_core(*places):
        for p, y in places:
            core_in[p, y] = send(islot(p, y, 0), islot(p, y, 1), "core")

    def from_core(*places):
        for place_y in places:
            core_in[place_y].wait_recv()

    loads[0].wait()
    loads[1].wait()
    loads[2].start()
    loads[3].start()
    project(IMG, WI, unitI, invI, I)
    pl.semaphore_wait(barrier, len(greeted))
    to_y(ig, own, "yi")
    spread(ig, own, 0, "x")
    to_core((0, 0))
    loads[2].wait()
    loads[3].wait()
    project(TXT, WT, unitT, invT, T)
    to_y(tg, tslot, "yt")
    spread(tg, tslot, 0, "z")
    FL[0:R, :] = jnp.where(first, IMG[...], TXT[...])
    OUT[...] = jnp.where(first, TXT[...], IMG[...])
    feat_out = send(OUT, FL.at[pl.ds(R, R), :], "core")
    accT[768:1024, :] = jnp.zeros((256, D), F32)

    feat_out.wait_recv()
    feats = FL[...]
    def arrange_third(third):
        a_axis, b_axis, c_axis = AXES[third]

        def arrange(a, carry):
            s = lax.broadcasted_iota(jnp.int32, (4 * SLOT, 128), 0)
            b = over(s, SLOT)
            k = s - SLOT * b
            c = over(k, 18)
            r = (row_share(a_axis, ring_place(a, me[a_axis]))
                 + row_share(b_axis, ring_place(b, me[b_axis]))
                 + row_share(c_axis, c) + k - 18 * c)
            r = jnp.where(k < 72, r, -1)
            lane = lax.broadcasted_iota(jnp.int32, (4 * SLOT, 128), 1)
            pick = jnp.concatenate(
                [jnp.where(r == lane + 128 * j, 1.0, 0.0).astype(BF16) for j in range(D // 128)],
                axis=1)
            XP[third, pl.ds(pl.multiple_of(a * 4 * SLOT, 16), 4 * SLOT), :] = lax.dot_general(
                pick, feats, NT, preferred_element_type=F32).astype(BF16)
            return carry
        lax.fori_loop(0, 4, arrange, 0)

    arrange_third(0)
    arrange_third(1)
    pass_on(ig, own, "x")
    pass_on(tg, tslot, "z")
    arrange_third(2)
    pass_rest(ig, own, "x")
    to_core((0, 1), (1, 0), (2, 0))
    pass_rest(tg, tslot, "z")

    scale = jnp.exp(jnp.full((1, 512), ls_ref[0], F32))
    slope = scale * (-LOG2E)
    offset = jnp.full((1, 512), bias_ref[0], F32) * (-LOG2E)

    def unit(ilo, m, tlo, n, new_i=False, new_t=False, diag=False):
        irows, trows = slice(ilo, ilo + m), slice(tlo, tlo + n)
        images, texts = I[irows, :], T[trows, :]
        parts = []
        for k in range(0, m, 256):
            s = lax.dot_general(I[ilo + k:ilo + k + 256, :], texts, NT, preferred_element_type=F32)
            x = s * slope[:, :n] + offset[:, :n]
            c = pltpu.reciprocal(1.0 + jnp.exp2(jnp.minimum(x, 126.0)), approx=True).astype(BF16)
            if diag and k == 0:
                up = jnp.exp2(jnp.minimum(-x[:R, :R], 126.0))
                row = lax.broadcasted_iota(jnp.int32, (R, R), 0)
                col = lax.broadcasted_iota(jnp.int32, (R, R), 1)
                corner = jnp.where(row == col, -1.0 / (1.0 + up), c[:R, :R].astype(F32)).astype(BF16)
                c = jnp.concatenate(
                    [jnp.concatenate([corner, c[:R, R:]], axis=1), c[R:, :]], axis=0)
            parts.append(c)
        c = jnp.concatenate(parts, axis=0)
        di = jnp.dot(c, texts, preferred_element_type=F32)
        dt = lax.dot_general(c, images, TN, preferred_element_type=F32)
        accI[irows, :] = di if new_i else accI[irows, :] + di
        accT[trows, :] = dt if new_t else accT[trows, :] + dt

    far_in(ig, own, "yi")
    to_core((3, 0))
    far_in(tg, tslot, "yt")
    from_core((0, 0), (0, 1), (1, 0), (2, 0))
    unit(0, 1024, 0, 512, True, True, True)
    second_in(ig)
    to_core((1, 1), (2, 1))
    second_in(tg)
    unit(0, 1024, 512, 256, False, True)
    ig["far y"].wait_recv()
    to_core((3, 1))
    from_core((1, 1), (2, 1))
    unit(1024, 512, 0, 512, True)
    tg["far y"].wait_recv()
    from_core((3, 0), (3, 1))
    unit(1536, 512, 0, 512, True)
    unit(1536, 512, 512, 512)

    def rows(n, step, size=32):
        def one(k, carry):
            step(k * size, size)
            return carry
        lax.fori_loop(0, n // size, one, 0)

    def at(base, r, n):
        return pl.ds(pl.multiple_of(base + r, 16), n)

    core_out = {}

    def core_send(level):
        for k in (2 * level, 2 * level + 1):
            def step(r, w):
                SC[at(k * R, r, w), :] = accI[at((k * 2 + 1) * R, r, w), :].astype(BF16)
            rows(R, step)
            block = pl.ds(k * R, R)
            core_out[k] = send(SC.at[block, :], RC.at[block, :], "core")

    def core_wait(level):
        core_out[2 * level].wait_recv()
        core_out[2 * level + 1].wait_recv()

    def value_i(p, y, r, w):
        k = ORDER[p][y]
        return accI[at(k * 2 * R, r, w), :] + RC[at(k * R, r, w), :].astype(F32)

    def value_t(p, y, r, w):
        return accT[at(ORDER[p][y] * R, r, w), :]

    class Ring:
        def __init__(self, axis, n, lo, value, stage, rx, rf, sources=2, size=32):
            self.sources, self.size = sources, size
            self.axis, self.n, self.lo, self.got = axis, n, lo, {}
            self.value, self.stage, self.rx, self.rf = value, stage, rx, rf

        def piece(self, key, p, start, n, direction, dst, dst_start, add=None):
            def step(r, w):
                v = self.value(p, start + r, w)
                if add is not None:
                    v = v + add(r, w).astype(F32)
                self.stage(p)[at(start, r, w), :] = v.astype(BF16)
            rows(n, step, self.size)
            self.launch(key, p, start, n, direction, dst, dst_start)

        def launch(self, key, p, start, n, direction, dst, dst_start):
            self.got[key] = send(self.stage(p).at[pl.ds(start, n), :],
                                 dst.at[pl.ds(dst_start, n), :], self.axis + direction)

        def far(self, add=None):
            lo, hi = self.lo, self.n - self.lo
            high = None if add is None else lambda r, w: add(lo + r, w)
            self.piece("far+", 3, 0, lo, "+", self.rx(0), 0, add)
            self.piece("far-", 3, lo, hi, "-", self.rx(1), 0, high)

        def near(self):
            self.piece("b+", 1, self.lo, self.n - self.lo, "+", self.rf(0), self.lo)
            self.piece("a-", 2, 0, self.lo, "-", self.rf(1), 0)

        def whole(self):
            self.piece("a+", 1, 0, self.n, "+", self.rf(0), 0)
            self.piece("a-", 2, 0, self.n, "-", self.rf(1), 0)

        def direct(self):
            for k, (p, there) in enumerate(((3, "2"), (1, "+"), (2, "-"))):
                self.piece(there, p, 0, self.n, there, self.rf(k), 0)

        def onward(self):
            lo, hi = self.lo, self.n - self.lo
            self.got["far+"].wait_recv()
            self.piece("a+", 1, 0, lo, "+", self.rf(0), 0, lambda r, w: self.rx(0)[at(0, r, w), :])
            self.got["far-"].wait_recv()
            self.piece("b-", 2, lo, hi, "-", self.rf(1), lo, lambda r, w: self.rx(1)[at(0, r, w), :])

        def arrive(self):
            for key in ("a+", "b+", "a-", "b-", "+", "-", "2"):
                if key in self.got:
                    self.got[key].wait_recv()

        def staged_far(self):
            lo, hi = self.lo, self.n - self.lo
            self.launch("far+", 3, 0, lo, "+", self.rx(0), 0)
            self.launch("far-", 3, lo, hi, "-", self.rx(1), 0)

        def staged_near(self):
            self.launch("b+", 1, self.lo, self.n - self.lo, "+", self.rf(0), self.lo)
            self.launch("a-", 2, 0, self.lo, "-", self.rf(1), 0)

        def total(self, r, w):
            v = self.value(0, r, w)
            for k in range(self.sources):
                v = v + self.rf(k)[at(0, r, w), :].astype(F32)
            return v

    def block_rings(axis, y, value, stage, rx, rf):
        def half(h):
            return Ring(
                axis, H, H // 2, lambda p, r, w: value(p, y, h * H + r, w),
                lambda p: stage.at[pl.ds(ORDER[p][y] * R + h * H, H), :],
                lambda d: rx.at[pl.ds(d * H + h * (H // 2), H // 2), :],
                lambda d: rf.at[pl.ds((d * 2 + y) * R + h * H, H), :])
        return [half(0), half(1)]

    ring_i = [block_rings("x", y, value_i, SXI, RXI, RFI) for y in range(2)]
    ring_t = [block_rings("z", y, value_t, SXT, RXT, RFT) for y in range(2)]

    def every(rings, what):
        for ring in rings:
            getattr(ring, what)()

    def over_y(n, h, value, stage, arrived, to):
        lo = n * R + h * H

        def step(r, w):
            stage[at(lo, r, w), :] = value(r, w).astype(BF16)
        rows(H, step)
        mine = pl.ds(lo, H)
        return send(stage.at[mine, :], arrived.at[mine, :], to)

    def far_over(rings, n, to):
        return [over_y(n, h, lambda r, w: rings[1][h].value(3, r, w), SF, RYF, to)
                for h in range(2)]

    def far_sum(rings, n, copies):
        for h in range(2):
            copies[h].wait_recv()
            rings[0][h].far(lambda r, w: RYF[at(n * R + h * H, r, w), :])

    def cross(rings, n, to):
        copies = []
        for h in range(2):
            rings[1][h].arrive()
            copies.append(over_y(n, h, rings[1][h].total, SY, RY, to))
        return copies

    def finish(rings, n, crossed, unit_ref, inv_ref, gp):
        t = jnp.exp(jnp.full((1, D), ls_ref[0], F32))

        for h in range(2):
            rings[0][h].arrive()
            crossed[h].wait_recv()

            def step(r, w):
                low = h * H + r
                g = (rings[0][h].total(r, w) + RY[at(n * R, low, w), :].astype(F32)) * t
                u = unit_ref[at(0, low, w), :]
                inv = inv_ref[at(0, low, w), :][:, 0:1]
                along = jnp.sum(u * g, axis=1, keepdims=True)
                gp[at(0, low, w), :] = (inv * (g - u * along)).astype(BF16)
            rows(H, step, 16)

    def feature_grad(gp, w_ref, lo):
        gf_ref[lo:lo + R, :] = lax.dot_general(
            gp[...], w_ref[...], NT, preferred_element_type=F32).astype(BF16)

    core_send(3)
    unit(1024, 512, 512, 512)
    core_send(2)
    core_wait(3)
    over_i = far_over(ring_i, 0, "yi")
    core_wait(2)
    every(ring_i[1], "whole")
    unit(0, 1024, 768, 256)
    over_t = far_over(ring_t, 1, "yt")
    core_send(1)
    core_send(0)
    every(ring_t[1], "whole")
    far_sum(ring_i, 0, over_i)
    core_wait(1)
    every(ring_i[0], "near")
    core_wait(0)
    cross_i = cross(ring_i, 0, "yi")
    far_sum(ring_t, 1, over_t)
    every(ring_t[0], "near")
    cross_t = cross(ring_t, 1, "yt")
    every(ring_i[0], "onward")
    every(ring_t[0], "onward")
    finish(ring_i, 0, cross_i, unitI, invI, gpI)
    finish(ring_t, 1, cross_t, unitT, invT, gpT)

    GL[0:R, :] = jnp.where(first, gpI[...], gpT[...])
    feat_out.wait_send()
    OUT[...] = jnp.where(first, gpT[...], gpI[...])
    grad_in = send(OUT, GL.at[pl.ds(R, R), :], "core")

    def columns(third):
        return slice(third * 384, third * 384 + 384)

    def product(third, lo, n):
        return jnp.dot(XP[third, lo:lo + n, :], GL[:, columns(third)], preferred_element_type=F32)

    def weight_ring(third, axis, n, lo, stage, rx, rf, sources):
        return Ring(
            axis, n, lo, lambda p, r, w: accI[at(p * n, r, w), columns(third)],
            lambda p: stage.at[third, pl.ds(p * n, n), :],
            lambda d: rx.at[third, d], lambda d: rf.at[third, d], sources, SLOT)

    N, half = 4 * SLOT, 2 * SLOT
    outer = [weight_ring(k, AXES[k][0], N, half, S1, RX1, RF1, 2) for k in range(3)]
    inner = [weight_ring(k, AXES[k][1], SLOT, 0, S2, None, RF2, 3) for k in range(3)]
    grad_in.wait_recv()
    for third in range(3):
        S1[third, 3 * N:4 * N, :] = product(third, 3 * N, N).astype(BF16)
        outer[third].staged_far()
    for third in range(3):
        v = product(third, N, N)
        accI[N:N + half, columns(third)] = v[:half]
        S1[third, N + half:2 * N, :] = v[half:].astype(BF16)
        v = product(third, 2 * N, N)
        S1[third, 2 * N:2 * N + half, :] = v[:half].astype(BF16)
        accI[2 * N + half:3 * N, columns(third)] = v[half:]
        outer[third].staged_near()
    every(outer, "onward")
    for third in range(3):
        accI[0:N, columns(third)] = product(third, 0, N)
    feature_grad(gpI, WI, 0)
    feature_grad(gpT, WT, R)
    for third in range(3):
        outer[third].arrive()

        def step(r, w):
            accI[at(0, r, w), columns(third)] = outer[third].total(r, w)
        rows(N, step, SLOT)
        inner[third].direct()

    last = []
    for third in range(3):
        c_axis = AXES[third][2]
        row = lax.broadcasted_iota(jnp.int32, (R, SLOT), 0)
        k = lax.broadcasted_iota(jnp.int32, (R, SLOT), 1)
        block, i = row >> 4, row & 15
        other = block & 1
        core = other + me["core"] - 2 * other * me["core"]
        want = ring_place(block >> 1, me[c_axis]) * 18 + core * 9 + i
        pick = jnp.where((k == want) & (i < 9), 1.0, 0.0).astype(BF16)
        inner[third].arrive()
        mine = inner[third].total(0, SLOT).astype(BF16)
        E[third] = jnp.dot(pick, mine, preferred_element_type=F32).astype(BF16)
        for j, there in enumerate(("core", "+", "+c", "-", "-c", "2", "2c"), 1):
            some = pl.ds(j * 16, 16)
            last.append(send(E.at[third, some, :], Z.at[third, some, :],
                             there if j == 1 else c_axis + there))
    for third in range(3):
        for copy in last[third * 7:third * 7 + 7]:
            copy.wait_recv()
        z = Z[third, 16:128, :].astype(F32)
        same = E[third, 0:16, :].astype(F32) + z[16:32] + z[48:64] + z[80:96]
        swapped = z[0:16] + z[32:48] + z[64:80] + z[96:112]
        dw_ref[0:16, columns(third)] = jnp.where(first, same, swapped)
        dw_ref[16:32, columns(third)] = jnp.where(first, swapped, same)
    for copy in sent:
        if copy is not feat_out:
            copy.wait_send()


def fused(img_feat, txt_feat, w_img, w_txt, ls, bias):
    D = img_feat.shape[1]
    vmem = pl.BlockSpec(memory_space=pltpu.VMEM)
    hbm = pl.BlockSpec(memory_space=pl.ANY)
    smem = pl.BlockSpec(memory_space=pltpu.SMEM)
    sizes = [(2048, BF16), (1024, BF16), (2048, F32), (1024, F32), (1024, BF16), (1024, BF16),
             (1024, BF16), (1024, BF16), (R, BF16), (R, BF16), (512, BF16), (512, BF16),
             (256, BF16), (256, BF16), (256, BF16), (256, BF16), (D, BF16), (D, BF16),
             (R, BF16), (R, BF16), (R, F32), (R, F32), (R, BF16), (R, BF16),
             (2 * R, BF16), (2 * R, BF16), (R, BF16)]
    thirds = [(4 * 4 * SLOT,), (2, 2 * SLOT), (2, 4 * SLOT), (4 * SLOT,), (3, SLOT), (R,), (R,)]
    return pl.pallas_call(
        kernel,
        out_shape=(jax.ShapeDtypeStruct((2 * R, D), BF16), jax.ShapeDtypeStruct((32, D), F32)),
        in_specs=[hbm] * 4 + [smem] * 2,
        out_specs=(vmem,) * 2,
        scratch_shapes=[pltpu.VMEM((n, D), t) for n, t in sizes]
        + [pltpu.VMEM((R, 128), F32)] * 2
        + [pltpu.VMEM((3, 16 * SLOT, 2 * R), BF16)]
        + [pltpu.VMEM((3,) + n + (D // 3,), BF16) for n in thirds]
        + [pltpu.SemaphoreType.DMA((4,))] + [pltpu.SemaphoreType.DMA((144,))] * 2,
        compiler_params=pltpu.CompilerParams(
            collective_id=0, has_side_effects=True, vmem_limit_bytes=62 * 2**20),
    )(img_feat, txt_feat, w_img, w_txt, ls, bias)


def body(img_feat, txt_feat, w_img, w_txt, logit_scale_log, bias):
    gf, dw = fused(img_feat, txt_feat, w_img, w_txt, logit_scale_log, bias)
    return gf[:R], gf[R:], dw[0:9], dw[16:25]


def solution(mesh):
    rows = P(("blk", "group"), None)
    return jax.shard_map(
        body, mesh=mesh, in_specs=(rows, rows, P(), P(), P(), P()),
        out_specs=(rows,) * 4, check_vma=False)
```

```python
import jax
import jax.numpy as jnp
from jax import lax
from jax.experimental import pallas as pl
from jax.experimental.pallas import tpu as pltpu
from jax.sharding import PartitionSpec as P

R = 128
H = 64
LOG2E = 1.4426950408889634
NT = (((1,), (1,)), ((), ()))
TN = (((0,), (0,)), ((), ()))
F32 = jnp.float32
BF16 = jnp.bfloat16


AXES = (("z", "x", "y"), ("x", "y", "z"), ("y", "z", "x"))
SLOT = 80


def place():
    b, g = lax.axis_index("blk"), lax.axis_index("group")
    return {"x": g // 4, "y": (g // 2) % 2 * 2 + b % 2, "z": b // 2, "core": g % 2}


def neighbours(me):
    def device(**moved):
        c = {**me, **moved}
        return (c["z"] * 2 + c["y"] % 2, c["x"] * 4 + c["y"] // 2 * 2 + c["core"])

    near = {"core": device(core=1 - me["core"])}
    for axis in "xyz":
        for name, step in (("+", 1), ("-", 3), ("2", 2)):
            moved = {axis: (me[axis] + step) % 4}
            near[axis + name] = device(**moved)
            near[axis + name + "c"] = device(**moved, core=1 - me["core"])
    greeted = list(near.values())
    near["yi"] = device(y=me["y"] + 1 - 2 * (me["y"] % 2))
    near["yt"] = device(y=3 - me["y"])
    return near, greeted


def ring_place(p, here):
    step = jnp.where(p == 1, 1, jnp.where(p == 2, 3, jnp.where(p == 3, 2, 0)))
    return (here + step) & 3


def row_share(axis, v):
    if axis == "y":
        return (v & 1) * 144 + (v >> 1) * 18
    return v * (288 if axis == "z" else 36)


def over(v, step):
    return sum((v >= step * k).astype(jnp.int32) for k in range(1, 4))


def kernel(img_hbm, txt_hbm, wi_hbm, wt_hbm, ls_ref, bias_ref,
           gf_ref, dw_ref,
           I, T, accI, accT, SC, RC, SXI, SXT, RXI, RXT, RFI, RFT, SY, RY, SF, RYF, WI, WT, IMG, TXT,
           unitI, unitT, gpI, gpT, FL, GL, OUT, invI, invT,
           XP, S1, RX1, RF1, S2, RF2, E, Z, lsem, ssem, rsem):
    D = IMG.shape[1]
    loads = [pltpu.make_async_copy(src, dst, lsem.at[k]) for k, (src, dst) in enumerate(
        ((img_hbm, IMG), (wi_hbm, WI), (txt_hbm, TXT), (wt_hbm, WT)))]
    for load in loads[:2]:
        load.start()
    me = place()
    near, greeted = neighbours(me)
    first = me["core"] == 0
    barrier = pltpu.get_barrier_semaphore()
    for there in greeted:
        pl.semaphore_signal(barrier, inc=1, device_id=there, device_id_type=pl.DeviceIdType.MESH)

    sent = []

    def send(src, dst, to):
        k = len(sent)
        copy = pltpu.make_async_remote_copy(
            src_ref=src, dst_ref=dst, send_sem=ssem.at[k], recv_sem=rsem.at[k],
            device_id=near[to], device_id_type=pl.DeviceIdType.MESH)
        copy.start()
        sent.append(copy)
        return copy

    def project(feat, w, unit, inv, emb):
        p = jnp.dot(feat[...], w[...], preferred_element_type=F32)
        r = lax.rsqrt(jnp.sum(p * p, axis=1, keepdims=True) + 1e-06)
        u = p * r
        unit[...] = u
        inv[...] = jnp.broadcast_to(r, (R, 128))
        emb[0:R, :] = u.astype(BF16)

    ORDER = ((0, 1), (2, 4), (3, 5), (6, 7))

    def islot(p, y, c=0, lo=0, n=R):
        return I.at[pl.ds((ORDER[p][y] * 2 + c) * R + lo, n), :]

    def tslot(p, y, lo=0, n=R):
        return T.at[pl.ds(ORDER[p][y] * R + lo, n), :]

    def own(p, y, lo=0, n=R):
        return islot(p, y, 0, lo, n)

    ig, tg, core_in = {}, {}, {}

    def spread(got, slot, y, ring, halves=(0, 1)):
        for h in halves:
            got["+", y, h] = send(slot(0, y, h * H, H), slot(2, y, h * H, H), ring + "+")
            low = h * H if y else H - h * H
            got["-", y, h] = send(slot(0, y, low, H), slot(1, y, low, H), ring + "-")

    def to_y(got, slot, to):
        for h in range(2):
            got["y", h] = send(slot(0, 0, h * H, H), slot(0, 1, h * H, H), to)

    def pass_on(got, slot, ring):
        got["+", 0, 0].wait_recv()
        got["far+"] = send(slot(2, 0, 0, H), slot(3, 0, 0, H), ring + "+")
        got["-", 0, 0].wait_recv()
        got["far-"] = send(slot(1, 0, H, H), slot(3, 0, H, H), ring + "-")
        got["y", 0].wait_recv()
        spread(got, slot, 1, ring, (0,))

    def pass_rest(got, slot, ring):
        got["y", 1].wait_recv()
        spread(got, slot, 1, ring, (1,))
        got["+", 0, 1].wait_recv()
        got["-", 0, 1].wait_recv()

    def second_in(got):
        for d in "+-":
            for h in range(2):
                got[d, 1, h].wait_recv()

    def far_in(got, slot, to):
        got["far+"].wait_recv()
        got["far-"].wait_recv()
        got["far y"] = send(slot(3, 0), slot(3, 1), to)

    def to_core(*places):
        for p, y in places:
            core_in[p, y] = send(islot(p, y, 0), islot(p, y, 1), "core")

    def from_core(*places):
        for place_y in places:
            core_in[place_y].wait_recv()

    loads[0].wait()
    loads[1].wait()
    loads[2].start()
    loads[3].start()
    project(IMG, WI, unitI, invI, I)
    pl.semaphore_wait(barrier, len(greeted))
    to_y(ig, own, "yi")
    spread(ig, own, 0, "x")
    to_core((0, 0))
    loads[2].wait()
    loads[3].wait()
    project(TXT, WT, unitT, invT, T)
    to_y(tg, tslot, "yt")
    spread(tg, tslot, 0, "z")
    FL[0:R, :] = jnp.where(first, IMG[...], TXT[...])
    OUT[...] = jnp.where(first, TXT[...], IMG[...])
    feat_out = send(OUT, FL.at[pl.ds(R, R), :], "core")
    accT[768:1024, :] = jnp.zeros((256, D), F32)

    feat_out.wait_recv()
    feats = FL[...]
    def arrange_third(third):
        a_axis, b_axis, c_axis = AXES[third]

        def arrange(a, carry):
            s = lax.broadcasted_iota(jnp.int32, (4 * SLOT, 128), 0)
            b = over(s, SLOT)
            k = s - SLOT * b
            c = over(k, 18)
            r = (row_share(a_axis, ring_place(a, me[a_axis]))
                 + row_share(b_axis, ring_place(b, me[b_axis]))
                 + row_share(c_axis, c) + k - 18 * c)
            r = jnp.where(k < 72, r, -1)
            lane = lax.broadcasted_iota(jnp.int32, (4 * SLOT, 128), 1)
            pick = jnp.concatenate(
                [jnp.where(r == lane + 128 * j, 1.0, 0.0).astype(BF16) for j in range(D // 128)],
                axis=1)
            XP[third, pl.ds(pl.multiple_of(a * 4 * SLOT, 16), 4 * SLOT), :] = lax.dot_general(
                pick, feats, NT, preferred_element_type=F32).astype(BF16)
            return carry
        lax.fori_loop(0, 4, arrange, 0)

    arrange_third(0)
    arrange_third(1)
    pass_on(ig, own, "x")
    pass_on(tg, tslot, "z")
    arrange_third(2)
    pass_rest(ig, own, "x")
    to_core((0, 1), (1, 0), (2, 0))
    pass_rest(tg, tslot, "z")

    scale = jnp.exp(jnp.full((1, 512), ls_ref[0], F32))
    slope = scale * (-LOG2E)
    offset = jnp.full((1, 512), bias_ref[0], F32) * (-LOG2E)

    def unit(ilo, m, tlo, n, new_i=False, new_t=False, diag=False):
        irows, trows = slice(ilo, ilo + m), slice(tlo, tlo + n)
        images, texts = I[irows, :], T[trows, :]
        parts = []
        for k in range(0, m, 256):
            s = lax.dot_general(I[ilo + k:ilo + k + 256, :], texts, NT, preferred_element_type=F32)
            x = s * slope[:, :n] + offset[:, :n]
            c = pltpu.reciprocal(1.0 + jnp.exp2(jnp.minimum(x, 126.0)), approx=True).astype(BF16)
            if diag and k == 0:
                up = jnp.exp2(jnp.minimum(-x[:R, :R], 126.0))
                row = lax.broadcasted_iota(jnp.int32, (R, R), 0)
                col = lax.broadcasted_iota(jnp.int32, (R, R), 1)
                corner = jnp.where(row == col, -1.0 / (1.0 + up), c[:R, :R].astype(F32)).astype(BF16)
                c = jnp.concatenate(
                    [jnp.concatenate([corner, c[:R, R:]], axis=1), c[R:, :]], axis=0)
            parts.append(c)
        c = jnp.concatenate(parts, axis=0)
        di = jnp.dot(c, texts, preferred_element_type=F32)
        dt = lax.dot_general(c, images, TN, preferred_element_type=F32)
        accI[irows, :] = di if new_i else accI[irows, :] + di
        accT[trows, :] = dt if new_t else accT[trows, :] + dt

    far_in(ig, own, "yi")
    to_core((3, 0))
    far_in(tg, tslot, "yt")
    from_core((0, 0), (0, 1), (1, 0), (2, 0))
    unit(0, 1024, 0, 512, True, True, True)
    second_in(ig)
    to_core((1, 1), (2, 1))
    second_in(tg)
    unit(0, 1024, 512, 256, False, True)
    ig["far y"].wait_recv()
    to_core((3, 1))
    from_core((1, 1), (2, 1))
    unit(1024, 512, 0, 512, True)
    tg["far y"].wait_recv()
    from_core((3, 0), (3, 1))

    def rows(n, step, size=32):
        def one(k, carry):
            step(k * size, size)
            return carry
        lax.fori_loop(0, n // size, one, 0)

    def at(base, r, n):
        return pl.ds(pl.multiple_of(base + r, 16), n)

    core_out = {}

    def core_send(level):
        for k in (2 * level, 2 * level + 1):
            def step(r, w):
                SC[at(k * R, r, w), :] = accI[at((k * 2 + 1) * R, r, w), :].astype(BF16)
            rows(R, step)
            block = pl.ds(k * R, R)
            core_out[k] = send(SC.at[block, :], RC.at[block, :], "core")

    def core_wait(level):
        core_out[2 * level].wait_recv()
        core_out[2 * level + 1].wait_recv()

    def value_i(p, y, r, w):
        k = ORDER[p][y]
        return accI[at(k * 2 * R, r, w), :] + RC[at(k * R, r, w), :].astype(F32)

    def value_t(p, y, r, w):
        return accT[at(ORDER[p][y] * R, r, w), :]

    class Ring:
        def __init__(self, axis, n, lo, value, stage, rx, rf, sources=2, size=32):
            self.sources, self.size = sources, size
            self.axis, self.n, self.lo, self.got = axis, n, lo, {}
            self.value, self.stage, self.rx, self.rf = value, stage, rx, rf

        def piece(self, key, p, start, n, direction, dst, dst_start, add=None):
            def step(r, w):
                v = self.value(p, start + r, w)
                if add is not None:
                    v = v + add(r, w).astype(F32)
                self.stage(p)[at(start, r, w), :] = v.astype(BF16)
            rows(n, step, self.size)
            self.launch(key, p, start, n, direction, dst, dst_start)

        def launch(self, key, p, start, n, direction, dst, dst_start):
            self.got[key] = send(self.stage(p).at[pl.ds(start, n), :],
                                 dst.at[pl.ds(dst_start, n), :], self.axis + direction)

        def far(self, add=None):
            lo, hi = self.lo, self.n - self.lo
            high = None if add is None else lambda r, w: add(lo + r, w)
            self.piece("far+", 3, 0, lo, "+", self.rx(0), 0, add)
            self.piece("far-", 3, lo, hi, "-", self.rx(1), 0, high)

        def near(self):
            self.piece("b+", 1, self.lo, self.n - self.lo, "+", self.rf(0), self.lo)
            self.piece("a-", 2, 0, self.lo, "-", self.rf(1), 0)

        def whole(self):
            self.piece("a+", 1, 0, self.n, "+", self.rf(0), 0)
            self.piece("a-", 2, 0, self.n, "-", self.rf(1), 0)

        def direct(self):
            for k, (p, there) in enumerate(((3, "2"), (1, "+"), (2, "-"))):
                self.piece(there, p, 0, self.n, there, self.rf(k), 0)

        def onward(self):
            lo, hi = self.lo, self.n - self.lo
            self.got["far+"].wait_recv()
            self.piece("a+", 1, 0, lo, "+", self.rf(0), 0, lambda r, w: self.rx(0)[at(0, r, w), :])
            self.got["far-"].wait_recv()
            self.piece("b-", 2, lo, hi, "-", self.rf(1), lo, lambda r, w: self.rx(1)[at(0, r, w), :])

        def arrive(self):
            for key in ("a+", "b+", "a-", "b-", "+", "-", "2"):
                if key in self.got:
                    self.got[key].wait_recv()

        def staged_far(self):
            lo, hi = self.lo, self.n - self.lo
            self.launch("far+", 3, 0, lo, "+", self.rx(0), 0)
            self.launch("far-", 3, lo, hi, "-", self.rx(1), 0)

        def staged_near(self):
            self.launch("b+", 1, self.lo, self.n - self.lo, "+", self.rf(0), self.lo)
            self.launch("a-", 2, 0, self.lo, "-", self.rf(1), 0)

        def total(self, r, w):
            v = self.value(0, r, w)
            for k in range(self.sources):
                v = v + self.rf(k)[at(0, r, w), :].astype(F32)
            return v

    def block_rings(axis, y, value, stage, rx, rf):
        def half(h):
            return Ring(
                axis, H, H // 2, lambda p, r, w: value(p, y, h * H + r, w),
                lambda p: stage.at[pl.ds(ORDER[p][y] * R + h * H, H), :],
                lambda d: rx.at[pl.ds(d * H + h * (H // 2), H // 2), :],
                lambda d: rf.at[pl.ds((d * 2 + y) * R + h * H, H), :])
        return [half(0), half(1)]

    ring_i = [block_rings("x", y, value_i, SXI, RXI, RFI) for y in range(2)]
    ring_t = [block_rings("z", y, value_t, SXT, RXT, RFT) for y in range(2)]

    def every(rings, what):
        for ring in rings:
            getattr(ring, what)()

    def over_y(n, h, value, stage, arrived, to):
        lo = n * R + h * H

        def step(r, w):
            stage[at(lo, r, w), :] = value(r, w).astype(BF16)
        rows(H, step)
        mine = pl.ds(lo, H)
        return send(stage.at[mine, :], arrived.at[mine, :], to)

    def far_over(rings, n, to):
        return [over_y(n, h, lambda r, w: rings[1][h].value(3, r, w), SF, RYF, to)
                for h in range(2)]

    def far_sum(rings, n, copies):
        for h in range(2):
            copies[h].wait_recv()
            rings[0][h].far(lambda r, w: RYF[at(n * R + h * H, r, w), :])

    def cross(rings, n, to):
        copies = []
        for h in range(2):
            rings[1][h].arrive()
            copies.append(over_y(n, h, rings[1][h].total, SY, RY, to))
        return copies

    def finish(rings, n, crossed, unit_ref, inv_ref, gp):
        t = jnp.exp(jnp.full((1, D), ls_ref[0], F32))

        for h in range(2):
            rings[0][h].arrive()
            crossed[h].wait_recv()

            def step(r, w):
                low = h * H + r
                g = (rings[0][h].total(r, w) + RY[at(n * R, low, w), :].astype(F32)) * t
                u = unit_ref[at(0, low, w), :]
                inv = inv_ref[at(0, low, w), :][:, 0:1]
                along = jnp.sum(u * g, axis=1, keepdims=True)
                gp[at(0, low, w), :] = (inv * (g - u * along)).astype(BF16)
            rows(H, step, 16)

    def feature_grad(gp, w_ref, lo):
        gf_ref[lo:lo + R, :] = lax.dot_general(
            gp[...], w_ref[...], NT, preferred_element_type=F32).astype(BF16)

    unit(1536, 512, 0, 512, True)
    every(ring_t[0], "near")
    unit(1536, 512, 512, 512)
    core_send(3)
    unit(1024, 512, 512, 512)
    core_send(2)
    every(ring_t[1], "whole")
    core_wait(3)
    over_i = far_over(ring_i, 0, "yi")
    core_wait(2)
    every(ring_i[1], "whole")
    unit(0, 1024, 768, 256)
    over_t = far_over(ring_t, 1, "yt")
    core_send(1)
    core_send(0)
    far_sum(ring_i, 0, over_i)
    core_wait(1)
    every(ring_i[0], "near")
    cross_t = cross(ring_t, 1, "yt")
    core_wait(0)
    far_sum(ring_t, 1, over_t)
    cross_i = cross(ring_i, 0, "yi")
    every(ring_i[0], "onward")
    every(ring_t[0], "onward")
    finish(ring_i, 0, cross_i, unitI, invI, gpI)
    finish(ring_t, 1, cross_t, unitT, invT, gpT)

    GL[0:R, :] = jnp.where(first, gpI[...], gpT[...])
    feat_out.wait_send()
    OUT[...] = jnp.where(first, gpT[...], gpI[...])
    grad_in = send(OUT, GL.at[pl.ds(R, R), :], "core")

    def columns(third):
        return slice(third * 384, third * 384 + 384)

    def product(third, lo, n):
        return jnp.dot(XP[third, lo:lo + n, :], GL[:, columns(third)], preferred_element_type=F32)

    def weight_ring(third, axis, n, lo, stage, rx, rf, sources):
        return Ring(
            axis, n, lo, lambda p, r, w: accI[at(p * n, r, w), columns(third)],
            lambda p: stage.at[third, pl.ds(p * n, n), :],
            lambda d: rx.at[third, d], lambda d: rf.at[third, d], sources, SLOT)

    N, half = 4 * SLOT, 2 * SLOT
    outer = [weight_ring(k, AXES[k][0], N, half, S1, RX1, RF1, 2) for k in range(3)]
    inner = [weight_ring(k, AXES[k][1], SLOT, 0, S2, None, RF2, 3) for k in range(3)]
    grad_in.wait_recv()
    for third in range(3):
        S1[third, 3 * N:4 * N, :] = product(third, 3 * N, N).astype(BF16)
        outer[third].staged_far()
    for third in range(3):
        v = product(third, N, N)
        accI[N:N + half, columns(third)] = v[:half]
        S1[third, N + half:2 * N, :] = v[half:].astype(BF16)
        v = product(third, 2 * N, N)
        S1[third, 2 * N:2 * N + half, :] = v[:half].astype(BF16)
        accI[2 * N + half:3 * N, columns(third)] = v[half:]
        outer[third].staged_near()
    every(outer, "onward")
    for third in range(3):
        accI[0:N, columns(third)] = product(third, 0, N)
    feature_grad(gpI, WI, 0)
    feature_grad(gpT, WT, R)
    for third in range(3):
        outer[third].arrive()

        def step(r, w):
            accI[at(0, r, w), columns(third)] = outer[third].total(r, w)
        rows(N, step, SLOT)
        inner[third].direct()

    last = []
    for third in range(3):
        c_axis = AXES[third][2]
        row = lax.broadcasted_iota(jnp.int32, (R, SLOT), 0)
        k = lax.broadcasted_iota(jnp.int32, (R, SLOT), 1)
        block, i = row >> 4, row & 15
        other = block & 1
        core = other + me["core"] - 2 * other * me["core"]
        want = ring_place(block >> 1, me[c_axis]) * 18 + core * 9 + i
        pick = jnp.where((k == want) & (i < 9), 1.0, 0.0).astype(BF16)
        inner[third].arrive()
        mine = inner[third].total(0, SLOT).astype(BF16)
        E[third] = jnp.dot(pick, mine, preferred_element_type=F32).astype(BF16)
        for j, there in enumerate(("core", "+", "+c", "-", "-c", "2", "2c"), 1):
            some = pl.ds(j * 16, 16)
            last.append(send(E.at[third, some, :], Z.at[third, some, :],
                             there if j == 1 else c_axis + there))
    for third in range(3):
        for copy in last[third * 7:third * 7 + 7]:
            copy.wait_recv()
        z = Z[third, 16:128, :].astype(F32)
        same = E[third, 0:16, :].astype(F32) + z[16:32] + z[48:64] + z[80:96]
        swapped = z[0:16] + z[32:48] + z[64:80] + z[96:112]
        dw_ref[0:16, columns(third)] = jnp.where(first, same, swapped)
        dw_ref[16:32, columns(third)] = jnp.where(first, swapped, same)
    for copy in sent:
        if copy is not feat_out:
            copy.wait_send()


def fused(img_feat, txt_feat, w_img, w_txt, ls, bias):
    D = img_feat.shape[1]
    vmem = pl.BlockSpec(memory_space=pltpu.VMEM)
    hbm = pl.BlockSpec(memory_space=pl.ANY)
    smem = pl.BlockSpec(memory_space=pltpu.SMEM)
    sizes = [(2048, BF16), (1024, BF16), (2048, F32), (1024, F32), (1024, BF16), (1024, BF16),
             (1024, BF16), (1024, BF16), (R, BF16), (R, BF16), (512, BF16), (512, BF16),
             (256, BF16), (256, BF16), (256, BF16), (256, BF16), (D, BF16), (D, BF16),
             (R, BF16), (R, BF16), (R, F32), (R, F32), (R, BF16), (R, BF16),
             (2 * R, BF16), (2 * R, BF16), (R, BF16)]
    thirds = [(4 * 4 * SLOT,), (2, 2 * SLOT), (2, 4 * SLOT), (4 * SLOT,), (3, SLOT), (R,), (R,)]
    return pl.pallas_call(
        kernel,
        out_shape=(jax.ShapeDtypeStruct((2 * R, D), BF16), jax.ShapeDtypeStruct((32, D), F32)),
        in_specs=[hbm] * 4 + [smem] * 2,
        out_specs=(vmem,) * 2,
        scratch_shapes=[pltpu.VMEM((n, D), t) for n, t in sizes]
        + [pltpu.VMEM((R, 128), F32)] * 2
        + [pltpu.VMEM((3, 16 * SLOT, 2 * R), BF16)]
        + [pltpu.VMEM((3,) + n + (D // 3,), BF16) for n in thirds]
        + [pltpu.SemaphoreType.DMA((4,))] + [pltpu.SemaphoreType.DMA((144,))] * 2,
        compiler_params=pltpu.CompilerParams(
            collective_id=0, has_side_effects=True, vmem_limit_bytes=62 * 2**20),
    )(img_feat, txt_feat, w_img, w_txt, ls, bias)


def split(gf_ref, dw_ref, gfi_ref, gft_ref, dwi_ref, dwt_ref):
    gfi_ref[...] = gf_ref[0:R, :]
    gft_ref[...] = gf_ref[R:2 * R, :]
    dwi_ref[...] = dw_ref[0:9, :]
    dwt_ref[...] = dw_ref[16:25, :]


def outputs(gf, dw):
    D = gf.shape[1]
    vmem = pl.BlockSpec(memory_space=pltpu.VMEM)
    return pl.pallas_call(
        split,
        out_shape=(jax.ShapeDtypeStruct((R, D), BF16),) * 2 + (jax.ShapeDtypeStruct((9, D), F32),) * 2,
        in_specs=[vmem] * 2, out_specs=(vmem,) * 4)(gf, dw)


def body(img_feat, txt_feat, w_img, w_txt, logit_scale_log, bias):
    gf, dw = fused(img_feat, txt_feat, w_img, w_txt, logit_scale_log, bias)
    return outputs(gf, dw)


def solution(mesh):
    rows = P(("blk", "group"), None)
    return jax.shard_map(
        body, mesh=mesh, in_specs=(rows, rows, P(), P(), P(), P()),
        out_specs=(rows,) * 4, check_vma=False)
```

```python
import jax
import jax.numpy as jnp
from jax import lax
from jax.experimental import pallas as pl
from jax.experimental.pallas import tpu as pltpu
from jax.sharding import PartitionSpec as P

R = 128
H = 64
LOG2E = 1.4426950408889634
NT = (((1,), (1,)), ((), ()))
TN = (((0,), (0,)), ((), ()))
F32 = jnp.float32
BF16 = jnp.bfloat16


AXES = (("z", "x", "y"), ("x", "y", "z"), ("y", "z", "x"))
SLOT = 80


def place():
    b, g = lax.axis_index("blk"), lax.axis_index("group")
    return {"x": g // 4, "y": (g // 2) % 2 * 2 + b % 2, "z": b // 2, "core": g % 2}


def neighbours(me):
    def device(**moved):
        c = {**me, **moved}
        return (c["z"] * 2 + c["y"] % 2, c["x"] * 4 + c["y"] // 2 * 2 + c["core"])

    near = {"core": device(core=1 - me["core"])}
    for axis in "xyz":
        for name, step in (("+", 1), ("-", 3), ("2", 2)):
            moved = {axis: (me[axis] + step) % 4}
            near[axis + name] = device(**moved)
            near[axis + name + "c"] = device(**moved, core=1 - me["core"])
    greeted = list(near.values())
    near["yi"] = device(y=me["y"] + 1 - 2 * (me["y"] % 2))
    near["yt"] = device(y=3 - me["y"])
    return near, greeted


def ring_place(p, here):
    step = jnp.where(p == 1, 1, jnp.where(p == 2, 3, jnp.where(p == 3, 2, 0)))
    return (here + step) & 3


def row_share(axis, v):
    if axis == "y":
        return (v & 1) * 144 + (v >> 1) * 18
    return v * (288 if axis == "z" else 36)


def over(v, step):
    return sum((v >= step * k).astype(jnp.int32) for k in range(1, 4))


def kernel(img_hbm, txt_hbm, wi_hbm, wt_hbm, ls_ref, bias_ref,
           gf_ref, dw_ref,
           I, T, accI, accT, SC, RC, SXI, SXT, RXI, RXT, RFI, RFT, SY, RY, SF, RYF, WI, WT, IMG, TXT,
           unitI, unitT, gpI, gpT, FL, GL, GI, GT, OUT, invI, invT,
           XP, S1, RX1, RF1, S2, RF2, E, Z, lsem, ssem, rsem):
    D = IMG.shape[1]
    K0 = 512
    loads = [pltpu.make_async_copy(src, dst, lsem.at[k]) for k, (src, dst) in enumerate(
        ((img_hbm, IMG), (wi_hbm.at[pl.ds(0, K0), :], WI.at[pl.ds(0, K0), :]),
         (wi_hbm.at[pl.ds(K0, D - K0), :], WI.at[pl.ds(K0, D - K0), :]),
         (txt_hbm, TXT), (wt_hbm, WT)))]
    for load in loads[:3]:
        load.start()
    me = place()
    near, greeted = neighbours(me)
    first = me["core"] == 0
    barrier = pltpu.get_barrier_semaphore()
    for there in greeted:
        pl.semaphore_signal(barrier, inc=1, device_id=there, device_id_type=pl.DeviceIdType.MESH)

    sent = []

    def send(src, dst, to):
        k = len(sent)
        copy = pltpu.make_async_remote_copy(
            src_ref=src, dst_ref=dst, send_sem=ssem.at[k], recv_sem=rsem.at[k],
            device_id=near[to], device_id_type=pl.DeviceIdType.MESH)
        copy.start()
        sent.append(copy)
        return copy

    def project(feat, w, unit, inv, emb, ready):
        ready[0].wait()
        ready[1].wait()
        p = jnp.dot(feat[:, :K0], w[:K0, :], preferred_element_type=F32)
        for load in ready[2:]:
            load.wait()
        p = p + jnp.dot(feat[:, K0:], w[K0:, :], preferred_element_type=F32)
        r = lax.rsqrt(jnp.sum(p * p, axis=1, keepdims=True) + 1e-06)
        u = p * r
        unit[...] = u
        inv[...] = jnp.broadcast_to(r, (R, 128))
        emb[0:R, :] = u.astype(BF16)

    ORDER = ((0, 1), (2, 4), (3, 5), (6, 7))

    def islot(p, y, c=0, lo=0, n=R):
        return I.at[pl.ds((ORDER[p][y] * 2 + c) * R + lo, n), :]

    def tslot(p, y, lo=0, n=R):
        return T.at[pl.ds(ORDER[p][y] * R + lo, n), :]

    def own(p, y, lo=0, n=R):
        return islot(p, y, 0, lo, n)

    ig, tg, core_in = {}, {}, {}

    def spread(got, slot, y, ring, halves=(0, 1)):
        for h in halves:
            got["+", y, h] = send(slot(0, y, h * H, H), slot(2, y, h * H, H), ring + "+")
            low = h * H if y else H - h * H
            got["-", y, h] = send(slot(0, y, low, H), slot(1, y, low, H), ring + "-")

    def to_y(got, slot, to):
        for h in range(2):
            got["y", h] = send(slot(0, 0, h * H, H), slot(0, 1, h * H, H), to)

    def pass_on(got, slot, ring):
        got["+", 0, 0].wait_recv()
        got["far+"] = send(slot(2, 0, 0, H), slot(3, 0, 0, H), ring + "+")
        got["-", 0, 0].wait_recv()
        got["far-"] = send(slot(1, 0, H, H), slot(3, 0, H, H), ring + "-")
        got["y", 0].wait_recv()
        spread(got, slot, 1, ring, (0,))

    def pass_rest(got, slot, ring):
        got["y", 1].wait_recv()
        spread(got, slot, 1, ring, (1,))
        got["+", 0, 1].wait_recv()
        got["-", 0, 1].wait_recv()

    def second_in(got):
        for d in "+-":
            for h in range(2):
                got[d, 1, h].wait_recv()

    def far_in(got, slot, to):
        got["far+"].wait_recv()
        got["far-"].wait_recv()
        got["far y"] = send(slot(3, 0), slot(3, 1), to)

    def to_core(*places):
        for p, y in places:
            core_in[p, y] = send(islot(p, y, 0), islot(p, y, 1), "core")

    def from_core(*places):
        for place_y in places:
            core_in[place_y].wait_recv()

    loads[3].start()
    loads[4].start()
    project(IMG, WI, unitI, invI, I, loads[:3])
    pl.semaphore_wait(barrier, len(greeted))
    to_y(ig, own, "yi")
    spread(ig, own, 0, "x")
    to_core((0, 0))
    project(TXT, WT, unitT, invT, T, loads[3:])
    to_y(tg, tslot, "yt")
    spread(tg, tslot, 0, "z")
    FL[0:R, :] = jnp.where(first, IMG[...], TXT[...])
    OUT[...] = jnp.where(first, TXT[...], IMG[...])
    feat_out = send(OUT, FL.at[pl.ds(R, R), :], "core")
    accT[768:1024, :] = jnp.zeros((256, D), F32)

    feat_out.wait_recv()
    feats = FL[...]
    def arrange_third(third):
        a_axis, b_axis, c_axis = AXES[third]

        def arrange(a, carry):
            s = lax.broadcasted_iota(jnp.int32, (4 * SLOT, 128), 0)
            b = over(s, SLOT)
            k = s - SLOT * b
            c = over(k, 18)
            r = (row_share(a_axis, ring_place(a, me[a_axis]))
                 + row_share(b_axis, ring_place(b, me[b_axis]))
                 + row_share(c_axis, c) + k - 18 * c)
            r = jnp.where(k < 72, r, -1)
            lane = lax.broadcasted_iota(jnp.int32, (4 * SLOT, 128), 1)
            pick = jnp.concatenate(
                [jnp.where(r == lane + 128 * j, 1.0, 0.0).astype(BF16) for j in range(D // 128)],
                axis=1)
            XP[third, pl.ds(pl.multiple_of(a * 4 * SLOT, 16), 4 * SLOT), :] = lax.dot_general(
                pick, feats, NT, preferred_element_type=F32).astype(BF16)
            return carry
        lax.fori_loop(0, 4, arrange, 0)

    arrange_third(0)
    arrange_third(1)
    pass_on(ig, own, "x")
    pass_on(tg, tslot, "z")
    arrange_third(2)
    pass_rest(ig, own, "x")
    to_core((0, 1), (1, 0), (2, 0))
    pass_rest(tg, tslot, "z")

    scale = jnp.exp(jnp.full((1, 512), ls_ref[0], F32))
    slope = scale * (-LOG2E)
    offset = jnp.full((1, 512), bias_ref[0], F32) * (-LOG2E)

    def unit(ilo, m, tlo, n, new_i=False, new_t=False, diag=False):
        irows, trows = slice(ilo, ilo + m), slice(tlo, tlo + n)
        images, texts = I[irows, :], T[trows, :]
        parts = []
        for k in range(0, m, 256):
            s = lax.dot_general(I[ilo + k:ilo + k + 256, :], texts, NT, preferred_element_type=F32)
            x = s * slope[:, :n] + offset[:, :n]
            c = pltpu.reciprocal(1.0 + jnp.exp2(jnp.minimum(x, 126.0)), approx=True).astype(BF16)
            if diag and k == 0:
                up = jnp.exp2(jnp.minimum(-x[:R, :R], 126.0))
                row = lax.broadcasted_iota(jnp.int32, (R, R), 0)
                col = lax.broadcasted_iota(jnp.int32, (R, R), 1)
                corner = jnp.where(row == col, -1.0 / (1.0 + up), c[:R, :R].astype(F32)).astype(BF16)
                c = jnp.concatenate(
                    [jnp.concatenate([corner, c[:R, R:]], axis=1), c[R:, :]], axis=0)
            parts.append(c)
        c = jnp.concatenate(parts, axis=0)
        di = jnp.dot(c, texts, preferred_element_type=F32)
        dt = lax.dot_general(c, images, TN, preferred_element_type=F32)
        accI[irows, :] = di if new_i else accI[irows, :] + di
        accT[trows, :] = dt if new_t else accT[trows, :] + dt

    far_in(ig, own, "yi")
    to_core((3, 0))
    far_in(tg, tslot, "yt")
    from_core((0, 0), (0, 1), (1, 0), (2, 0))
    unit(0, 1024, 0, 512, True, True, True)
    second_in(ig)
    to_core((1, 1), (2, 1))
    second_in(tg)
    unit(0, 1024, 512, 256, False, True)
    ig["far y"].wait_recv()
    to_core((3, 1))
    from_core((1, 1), (2, 1))
    unit(1024, 512, 0, 512, True)
    tg["far y"].wait_recv()
    from_core((3, 0), (3, 1))

    def rows(n, step, size=64):
        def one(k, carry):
            step(k * size, size)
            return carry
        lax.fori_loop(0, n // size, one, 0)

    def at(base, r, n):
        return pl.ds(pl.multiple_of(base + r, 16), n)

    core_out = {}

    def core_send(level):
        for k in (2 * level, 2 * level + 1):
            def step(r, w):
                SC[at(k * R, r, w), :] = accI[at((k * 2 + 1) * R, r, w), :].astype(BF16)
            rows(R, step)
            block = pl.ds(k * R, R)
            core_out[k] = send(SC.at[block, :], RC.at[block, :], "core")

    def core_wait(level):
        core_out[2 * level].wait_recv()
        core_out[2 * level + 1].wait_recv()

    def value_i(p, y, r, w):
        k = ORDER[p][y]
        return accI[at(k * 2 * R, r, w), :] + RC[at(k * R, r, w), :].astype(F32)

    def value_t(p, y, r, w):
        return accT[at(ORDER[p][y] * R, r, w), :]

    class Ring:
        def __init__(self, axis, n, lo, value, stage, rx, rf, sources=2, size=32):
            self.sources, self.size = sources, size
            self.axis, self.n, self.lo, self.got = axis, n, lo, {}
            self.value, self.stage, self.rx, self.rf = value, stage, rx, rf

        def piece(self, key, p, start, n, direction, dst, dst_start, add=None):
            def step(r, w):
                v = self.value(p, start + r, w)
                if add is not None:
                    v = v + add(r, w).astype(F32)
                self.stage(p)[at(start, r, w), :] = v.astype(BF16)
            rows(n, step, self.size)
            self.launch(key, p, start, n, direction, dst, dst_start)

        def launch(self, key, p, start, n, direction, dst, dst_start):
            self.got[key] = send(self.stage(p).at[pl.ds(start, n), :],
                                 dst.at[pl.ds(dst_start, n), :], self.axis + direction)

        def far(self, add=None):
            lo, hi = self.lo, self.n - self.lo
            high = None if add is None else lambda r, w: add(lo + r, w)
            self.piece("far+", 3, 0, lo, "+", self.rx(0), 0, add)
            self.piece("far-", 3, lo, hi, "-", self.rx(1), 0, high)

        def near(self):
            self.piece("b+", 1, self.lo, self.n - self.lo, "+", self.rf(0), self.lo)
            self.piece("a-", 2, 0, self.lo, "-", self.rf(1), 0)

        def whole(self):
            self.piece("a+", 1, 0, self.n, "+", self.rf(0), 0)
            self.piece("a-", 2, 0, self.n, "-", self.rf(1), 0)

        def onward(self):
            lo, hi = self.lo, self.n - self.lo
            self.got["far+"].wait_recv()
            self.piece("a+", 1, 0, lo, "+", self.rf(0), 0, lambda r, w: self.rx(0)[at(0, r, w), :])
            self.got["far-"].wait_recv()
            self.piece("b-", 2, lo, hi, "-", self.rf(1), lo, lambda r, w: self.rx(1)[at(0, r, w), :])

        def arrive(self):
            for key in ("a+", "b+", "a-", "b-", "+", "-", "2"):
                if key in self.got:
                    self.got[key].wait_recv()

        def staged_far(self):
            lo, hi = self.lo, self.n - self.lo
            self.launch("far+", 3, 0, lo, "+", self.rx(0), 0)
            self.launch("far-", 3, lo, hi, "-", self.rx(1), 0)

        def staged_near(self):
            self.launch("b+", 1, self.lo, self.n - self.lo, "+", self.rf(0), self.lo)
            self.launch("a-", 2, 0, self.lo, "-", self.rf(1), 0)

        def total(self, r, w):
            v = self.value(0, r, w)
            for k in range(self.sources):
                v = v + self.rf(k)[at(0, r, w), :].astype(F32)
            return v

    def block_rings(axis, y, value, stage, rx, rf):
        def half(h):
            return Ring(
                axis, H, H // 2, lambda p, r, w: value(p, y, h * H + r, w),
                lambda p: stage.at[pl.ds(ORDER[p][y] * R + h * H, H), :],
                lambda d: rx.at[pl.ds(d * H + h * (H // 2), H // 2), :],
                lambda d: rf.at[pl.ds((d * 2 + y) * R + h * H, H), :])
        return [half(0), half(1)]

    ring_i = [block_rings("x", y, value_i, SXI, RXI, RFI) for y in range(2)]
    ring_t = [block_rings("z", y, value_t, SXT, RXT, RFT) for y in range(2)]

    def every(rings, what):
        for ring in rings:
            getattr(ring, what)()

    def over_y(n, h, value, stage, arrived, to):
        lo = n * R + h * H

        def step(r, w):
            stage[at(lo, r, w), :] = value(r, w).astype(BF16)
        rows(H, step)
        mine = pl.ds(lo, H)
        return send(stage.at[mine, :], arrived.at[mine, :], to)

    def far_over(rings, n, to):
        return [over_y(n, h, lambda r, w: rings[1][h].value(3, r, w), SF, RYF, to)
                for h in range(2)]

    def far_sum(rings, n, copies):
        for h in range(2):
            copies[h].wait_recv()
            rings[0][h].far(lambda r, w: RYF[at(n * R + h * H, r, w), :])

    def cross(rings, n, to):
        copies = []
        for h in range(2):
            rings[1][h].arrive()
            copies.append(over_y(n, h, rings[1][h].total, SY, RY, to))
        return copies

    def finish(rings, n, crossed, unit_ref, inv_ref, gp):
        t = jnp.exp(jnp.full((1, D), ls_ref[0], F32))

        for h in range(2):
            rings[0][h].arrive()
            crossed[h].wait_recv()

            def step(r, w):
                low = h * H + r
                g = (rings[0][h].total(r, w) + RY[at(n * R, low, w), :].astype(F32)) * t
                u = unit_ref[at(0, low, w), :]
                inv = inv_ref[at(0, low, w), :][:, 0:1]
                along = jnp.sum(u * g, axis=1, keepdims=True)
                gp[at(0, low, w), :] = (inv * (g - u * along)).astype(BF16)
            rows(H, step, 32)

    def feature_grad(gp, w_ref, lo):
        gf_ref[lo:lo + R, :] = lax.dot_general(
            gp[...], w_ref[...], NT, preferred_element_type=F32).astype(BF16)

    unit(1536, 512, 0, 512, True)
    every(ring_t[0], "near")
    unit(1536, 512, 512, 512)
    core_send(3)
    unit(1024, 512, 512, 512)
    core_send(2)
    every(ring_t[1], "whole")
    core_wait(3)
    over_i = far_over(ring_i, 0, "yi")
    core_wait(2)
    every(ring_i[1], "whole")
    unit(0, 1024, 768, 256)
    over_t = far_over(ring_t, 1, "yt")
    core_send(1)
    core_send(0)
    far_sum(ring_i, 0, over_i)
    core_wait(1)
    every(ring_i[0], "near")
    cross_t = cross(ring_t, 1, "yt")
    core_wait(0)
    far_sum(ring_t, 1, over_t)
    cross_i = cross(ring_i, 0, "yi")
    every(ring_i[0], "onward")
    every(ring_t[0], "onward")
    finish(ring_i, 0, cross_i, unitI, invI, gpI)
    GI[0:R, :] = gpI[...]
    grad_i = send(gpI, GI.at[pl.ds(R, R), :], "core")
    finish(ring_t, 1, cross_t, unitT, invT, gpT)

    grad_t = send(gpT, GT.at[pl.ds(R, R), :], "core")
    GT[0:R, :] = gpT[...]

    def columns(third):
        return slice(third * 384, third * 384 + 384)

    def product(third, lo, n):
        return jnp.dot(XP[third, lo:lo + n, :], GL[:, columns(third)], preferred_element_type=F32)

    def weight_ring(third, axis, n, lo, stage, rx, rf, sources):
        return Ring(
            axis, n, lo, lambda p, r, w: accI[at(p * n, r, w), columns(third)],
            lambda p: stage.at[third, pl.ds(p * n, n), :],
            lambda d: rx.at[third, d], lambda d: rf.at[third, d], sources, SLOT)

    N, half = 4 * SLOT, 2 * SLOT
    outer = [weight_ring(k, AXES[k][0], N, half, S1, RX1, RF1, 2) for k in range(3)]
    inner = [weight_ring(k, AXES[k][1], SLOT, 0, S2, None, RF2, 3) for k in range(3)]
    feature_grad(gpI, WI, 0)
    grad_i.wait_recv()
    grad_t.wait_recv()
    GL[...] = jnp.where(first, GI[...], GT[...])
    for third in range(3):
        S1[third, 3 * N:4 * N, :] = product(third, 3 * N, N).astype(BF16)
        outer[third].staged_far()
    for third in range(3):
        v = product(third, N, N)
        accI[N:N + half, columns(third)] = v[:half]
        S1[third, N + half:2 * N, :] = v[half:].astype(BF16)
        v = product(third, 2 * N, N)
        S1[third, 2 * N:2 * N + half, :] = v[:half].astype(BF16)
        accI[2 * N + half:3 * N, columns(third)] = v[half:]
        outer[third].staged_near()
    every(outer, "onward")
    for third in range(3):
        accI[0:N, columns(third)] = product(third, 0, N)
    feature_grad(gpT, WT, R)
    for third in range(3):
        outer[third].arrive()

        for k, (p, there) in enumerate(((3, "2"), (1, "+"), (2, "-"))):
            S2[third, p * SLOT:(p + 1) * SLOT, :] = outer[third].total(p * SLOT, SLOT).astype(BF16)
            inner[third].launch(there, p, 0, SLOT, there, inner[third].rf(k), 0)
        accI[0:SLOT, columns(third)] = outer[third].total(0, SLOT)

    last = []
    for third in range(3):
        c_axis = AXES[third][2]
        row = lax.broadcasted_iota(jnp.int32, (R, SLOT), 0)
        k = lax.broadcasted_iota(jnp.int32, (R, SLOT), 1)
        block, i = row >> 4, row & 15
        other = block & 1
        core = other + me["core"] - 2 * other * me["core"]
        want = ring_place(block >> 1, me[c_axis]) * 18 + core * 9 + i
        pick = jnp.where((k == want) & (i < 9), 1.0, 0.0).astype(BF16)
        inner[third].arrive()
        mine = inner[third].total(0, SLOT).astype(BF16)
        E[third] = jnp.dot(pick, mine, preferred_element_type=F32).astype(BF16)
        for j, there in enumerate(("core", "+", "+c", "-", "-c", "2", "2c"), 1):
            some = pl.ds(j * 16, 16)
            last.append(send(E.at[third, some, :], Z.at[third, some, :],
                             there if j == 1 else c_axis + there))
    for third in range(3):
        for copy in last[third * 7:third * 7 + 7]:
            copy.wait_recv()
        z = Z[third, 16:128, :].astype(F32)
        same = E[third, 0:16, :].astype(F32) + z[16:32] + z[48:64] + z[80:96]
        swapped = z[0:16] + z[32:48] + z[64:80] + z[96:112]
        dw_ref[0:16, columns(third)] = jnp.where(first, same, swapped)
        dw_ref[16:32, columns(third)] = jnp.where(first, swapped, same)
    for copy in sent:
        copy.wait_send()


def fused(img_feat, txt_feat, w_img, w_txt, ls, bias):
    D = img_feat.shape[1]
    vmem = pl.BlockSpec(memory_space=pltpu.VMEM)
    hbm = pl.BlockSpec(memory_space=pl.ANY)
    smem = pl.BlockSpec(memory_space=pltpu.SMEM)
    sizes = [(2048, BF16), (1024, BF16), (2048, F32), (1024, F32), (1024, BF16), (1024, BF16),
             (1024, BF16), (1024, BF16), (R, BF16), (R, BF16), (512, BF16), (512, BF16),
             (256, BF16), (256, BF16), (256, BF16), (256, BF16), (D, BF16), (D, BF16),
             (R, BF16), (R, BF16), (R, F32), (R, F32), (R, BF16), (R, BF16),
             (2 * R, BF16), (2 * R, BF16), (2 * R, BF16), (2 * R, BF16), (R, BF16)]
    thirds = [(4 * 4 * SLOT,), (2, 2 * SLOT), (2, 4 * SLOT), (4 * SLOT,), (3, SLOT), (R,), (R,)]
    return pl.pallas_call(
        kernel,
        out_shape=(jax.ShapeDtypeStruct((2 * R, D), BF16), jax.ShapeDtypeStruct((32, D), F32)),
        in_specs=[hbm] * 4 + [smem] * 2,
        out_specs=(vmem,) * 2,
        scratch_shapes=[pltpu.VMEM((n, D), t) for n, t in sizes]
        + [pltpu.VMEM((R, 128), F32)] * 2
        + [pltpu.VMEM((3, 16 * SLOT, 2 * R), BF16)]
        + [pltpu.VMEM((3,) + n + (D // 3,), BF16) for n in thirds]
        + [pltpu.SemaphoreType.DMA((5,))] + [pltpu.SemaphoreType.DMA((144,))] * 2,
        compiler_params=pltpu.CompilerParams(
            collective_id=0, has_side_effects=True, vmem_limit_bytes=62 * 2**20),
    )(img_feat, txt_feat, w_img, w_txt, ls, bias)


def split(gf_ref, dw_ref, gfi_ref, gft_ref, dwi_ref, dwt_ref):
    gfi_ref[...] = gf_ref[0:R, :]
    gft_ref[...] = gf_ref[R:2 * R, :]
    dwi_ref[...] = dw_ref[0:9, :]
    dwt_ref[...] = dw_ref[16:25, :]


def outputs(gf, dw):
    D = gf.shape[1]
    vmem = pl.BlockSpec(memory_space=pltpu.VMEM)
    return pl.pallas_call(
        split,
        out_shape=(jax.ShapeDtypeStruct((R, D), BF16),) * 2 + (jax.ShapeDtypeStruct((9, D), F32),) * 2,
        in_specs=[vmem] * 2, out_specs=(vmem,) * 4)(gf, dw)


def body(img_feat, txt_feat, w_img, w_txt, logit_scale_log, bias):
    gf, dw = fused(img_feat, txt_feat, w_img, w_txt, logit_scale_log, bias)
    return outputs(gf, dw)


def solution(mesh):
    rows = P(("blk", "group"), None)
    return jax.shard_map(
        body, mesh=mesh, in_specs=(rows, rows, P(), P(), P(), P()),
        out_specs=(rows,) * 4, check_vma=False)
```

```python
import jax
import jax.numpy as jnp
from jax import lax
from jax.experimental import pallas as pl
from jax.experimental.pallas import tpu as pltpu
from jax.sharding import PartitionSpec as P

R = 128
H = 64
LOG2E = 1.4426950408889634
NT = (((1,), (1,)), ((), ()))
TN = (((0,), (0,)), ((), ()))
F32 = jnp.float32
BF16 = jnp.bfloat16


AXES = (("z", "x", "y"), ("x", "y", "z"), ("y", "z", "x"))
SLOT = 80


def place():
    b, g = lax.axis_index("blk"), lax.axis_index("group")
    return {"x": g // 4, "y": (g // 2) % 2 * 2 + b % 2, "z": b // 2, "core": g % 2}


def neighbours(me):
    def device(**moved):
        c = {**me, **moved}
        return (c["z"] * 2 + c["y"] % 2, c["x"] * 4 + c["y"] // 2 * 2 + c["core"])

    near = {"core": device(core=1 - me["core"])}
    for axis in "xyz":
        for name, step in (("+", 1), ("-", 3), ("2", 2)):
            moved = {axis: (me[axis] + step) % 4}
            near[axis + name] = device(**moved)
            near[axis + name + "c"] = device(**moved, core=1 - me["core"])
    greeted = list(near.values())
    near["yi"] = device(y=me["y"] + 1 - 2 * (me["y"] % 2))
    near["yt"] = device(y=3 - me["y"])
    return near, greeted


def ring_place(p, here):
    step = jnp.where(p == 1, 1, jnp.where(p == 2, 3, jnp.where(p == 3, 2, 0)))
    return (here + step) & 3


def row_share(axis, v):
    if axis == "y":
        return (v & 1) * 144 + (v >> 1) * 18
    return v * (288 if axis == "z" else 36)


def over(v, step):
    return sum((v >= step * k).astype(jnp.int32) for k in range(1, 4))


def kernel(img_hbm, txt_hbm, wi_hbm, wt_hbm, ls_ref, bias_ref,
           gf_ref, dw_ref,
           I, T, accI, accT, SC, RC, SXI, SXT, RXI, RXT, RFI, RFT, SY, RY, SF, RYF, WI, WT, IMG, TXT,
           unitI, unitT, gpI, gpT, FL, GL, GI, GT, OUT, invI, invT,
           XP, S1, RX1, RF1, S2, RF2, E, Z, lsem, ssem, rsem):
    D = IMG.shape[1]
    K0 = 512
    loads = [pltpu.make_async_copy(src, dst, lsem.at[k]) for k, (src, dst) in enumerate(
        ((img_hbm, IMG), (wi_hbm.at[pl.ds(0, K0), :], WI.at[pl.ds(0, K0), :]),
         (wi_hbm.at[pl.ds(K0, D - K0), :], WI.at[pl.ds(K0, D - K0), :]),
         (txt_hbm, TXT), (wt_hbm, WT)))]
    for load in loads[:3]:
        load.start()
    me = place()
    near, greeted = neighbours(me)
    first = me["core"] == 0
    barrier = pltpu.get_barrier_semaphore()
    for there in greeted:
        pl.semaphore_signal(barrier, inc=1, device_id=there, device_id_type=pl.DeviceIdType.MESH)

    sent = []

    def send(src, dst, to):
        k = len(sent)
        copy = pltpu.make_async_remote_copy(
            src_ref=src, dst_ref=dst, send_sem=ssem.at[k], recv_sem=rsem.at[k],
            device_id=near[to], device_id_type=pl.DeviceIdType.MESH)
        copy.start()
        sent.append(copy)
        return copy

    def project(feat, w, unit, inv, emb, ready, following=()):
        ready[0].wait()
        ready[1].wait()
        p = jnp.dot(feat[:, :K0], w[:K0, :], preferred_element_type=F32)
        for load in ready[2:]:
            load.wait()
        for load in following:
            load.start()
        p = p + jnp.dot(feat[:, K0:], w[K0:, :], preferred_element_type=F32)
        r = lax.rsqrt(jnp.sum(p * p, axis=1, keepdims=True) + 1e-06)
        u = p * r
        unit[...] = u
        inv[...] = jnp.broadcast_to(r, (R, 128))
        emb[0:R, :] = u.astype(BF16)

    ORDER = ((0, 1), (2, 4), (3, 5), (6, 7))

    def islot(p, y, c=0, lo=0, n=R):
        return I.at[pl.ds((ORDER[p][y] * 2 + c) * R + lo, n), :]

    def tslot(p, y, lo=0, n=R):
        return T.at[pl.ds(ORDER[p][y] * R + lo, n), :]

    def own(p, y, lo=0, n=R):
        return islot(p, y, 0, lo, n)

    ig, tg, core_in = {}, {}, {}

    def spread(got, slot, y, ring, halves=(0, 1)):
        for h in halves:
            got["+", y, h] = send(slot(0, y, h * H, H), slot(2, y, h * H, H), ring + "+")
            low = h * H if y else H - h * H
            got["-", y, h] = send(slot(0, y, low, H), slot(1, y, low, H), ring + "-")

    def to_y(got, slot, to):
        for h in range(2):
            got["y", h] = send(slot(0, 0, h * H, H), slot(0, 1, h * H, H), to)

    def pass_on(got, slot, ring):
        got["+", 0, 0].wait_recv()
        got["far+"] = send(slot(2, 0, 0, H), slot(3, 0, 0, H), ring + "+")
        got["-", 0, 0].wait_recv()
        got["far-"] = send(slot(1, 0, H, H), slot(3, 0, H, H), ring + "-")
        got["y", 0].wait_recv()
        spread(got, slot, 1, ring, (0,))

    def pass_rest(got, slot, ring):
        got["y", 1].wait_recv()
        spread(got, slot, 1, ring, (1,))
        got["+", 0, 1].wait_recv()
        got["-", 0, 1].wait_recv()

    def second_in(got):
        for d in "+-":
            for h in range(2):
                got[d, 1, h].wait_recv()

    def far_in(got, slot, to):
        got["far+"].wait_recv()
        got["far-"].wait_recv()
        got["far y"] = send(slot(3, 0), slot(3, 1), to)

    def to_core(*places):
        for p, y in places:
            core_in[p, y] = send(islot(p, y, 0), islot(p, y, 1), "core")

    def from_core(*places):
        for place_y in places:
            core_in[place_y].wait_recv()

    project(IMG, WI, unitI, invI, I, loads[:3], loads[3:])
    pl.semaphore_wait(barrier, len(greeted))
    to_y(ig, own, "yi")
    spread(ig, own, 0, "x")
    to_core((0, 0))
    project(TXT, WT, unitT, invT, T, loads[3:])
    to_y(tg, tslot, "yt")
    spread(tg, tslot, 0, "z")
    FL[0:R, :] = jnp.where(first, IMG[...], TXT[...])
    OUT[...] = jnp.where(first, TXT[...], IMG[...])
    feat_out = send(OUT, FL.at[pl.ds(R, R), :], "core")
    accT[768:1024, :] = jnp.zeros((256, D), F32)

    feat_out.wait_recv()
    feats = FL[...]
    def arrange_third(third):
        a_axis, b_axis, c_axis = AXES[third]

        def arrange(a, carry):
            s = lax.broadcasted_iota(jnp.int32, (4 * SLOT, 128), 0)
            b = over(s, SLOT)
            k = s - SLOT * b
            c = over(k, 18)
            r = (row_share(a_axis, ring_place(a, me[a_axis]))
                 + row_share(b_axis, ring_place(b, me[b_axis]))
                 + row_share(c_axis, c) + k - 18 * c)
            r = jnp.where(k < 72, r, -1)
            lane = lax.broadcasted_iota(jnp.int32, (4 * SLOT, 128), 1)
            pick = jnp.concatenate(
                [jnp.where(r == lane + 128 * j, 1.0, 0.0).astype(BF16) for j in range(D // 128)],
                axis=1)
            XP[third, pl.ds(pl.multiple_of(a * 4 * SLOT, 16), 4 * SLOT), :] = lax.dot_general(
                pick, feats, NT, preferred_element_type=F32).astype(BF16)
            return carry
        lax.fori_loop(0, 4, arrange, 0)

    arrange_third(0)
    arrange_third(1)
    pass_on(ig, own, "x")
    pass_on(tg, tslot, "z")
    arrange_third(2)
    pass_rest(ig, own, "x")
    to_core((0, 1), (1, 0), (2, 0))
    pass_rest(tg, tslot, "z")

    scale = jnp.exp(jnp.full((1, 512), ls_ref[0], F32))
    slope = scale * (-LOG2E)
    offset = jnp.full((1, 512), bias_ref[0], F32) * (-LOG2E)

    def unit(ilo, m, tlo, n, new_i=False, new_t=False, diag=False):
        irows, trows = slice(ilo, ilo + m), slice(tlo, tlo + n)
        images, texts = I[irows, :], T[trows, :]
        parts = []
        for k in range(0, m, 256):
            s = lax.dot_general(I[ilo + k:ilo + k + 256, :], texts, NT, preferred_element_type=F32)
            x = s * slope[:, :n] + offset[:, :n]
            c = pltpu.reciprocal(1.0 + jnp.exp2(jnp.minimum(x, 126.0)), approx=True).astype(BF16)
            if diag and k == 0:
                up = jnp.exp2(jnp.minimum(-x[:R, :R], 126.0))
                row = lax.broadcasted_iota(jnp.int32, (R, R), 0)
                col = lax.broadcasted_iota(jnp.int32, (R, R), 1)
                corner = jnp.where(row == col, -1.0 / (1.0 + up), c[:R, :R].astype(F32)).astype(BF16)
                c = jnp.concatenate(
                    [jnp.concatenate([corner, c[:R, R:]], axis=1), c[R:, :]], axis=0)
            parts.append(c)
        c = jnp.concatenate(parts, axis=0)
        di = jnp.dot(c, texts, preferred_element_type=F32)
        dt = lax.dot_general(c, images, TN, preferred_element_type=F32)
        accI[irows, :] = di if new_i else accI[irows, :] + di
        accT[trows, :] = dt if new_t else accT[trows, :] + dt

    far_in(ig, own, "yi")
    to_core((3, 0))
    far_in(tg, tslot, "yt")
    from_core((0, 0), (0, 1), (1, 0), (2, 0))
    unit(0, 1024, 0, 512, True, True, True)
    second_in(ig)
    to_core((1, 1), (2, 1))
    second_in(tg)
    unit(0, 1024, 512, 256, False, True)
    ig["far y"].wait_recv()
    to_core((3, 1))
    from_core((1, 1), (2, 1))
    unit(1024, 512, 0, 512, True)
    tg["far y"].wait_recv()
    from_core((3, 0), (3, 1))

    def rows(n, step, size=64):
        def one(k, carry):
            step(k * size, size)
            return carry
        lax.fori_loop(0, n // size, one, 0)

    def at(base, r, n):
        return pl.ds(pl.multiple_of(base + r, 16), n)

    core_out = {}

    def core_send(level):
        for k in (2 * level, 2 * level + 1):
            def step(r, w):
                SC[at(k * R, r, w), :] = accI[at((k * 2 + 1) * R, r, w), :].astype(BF16)
            rows(R, step)
            block = pl.ds(k * R, R)
            core_out[k] = send(SC.at[block, :], RC.at[block, :], "core")

    def core_wait(level):
        core_out[2 * level].wait_recv()
        core_out[2 * level + 1].wait_recv()

    def value_i(p, y, r, w):
        k = ORDER[p][y]
        return accI[at(k * 2 * R, r, w), :] + RC[at(k * R, r, w), :].astype(F32)

    def value_t(p, y, r, w):
        return accT[at(ORDER[p][y] * R, r, w), :]

    class Ring:
        def __init__(self, axis, n, lo, value, stage, rx, rf, sources=2, size=32):
            self.sources, self.size = sources, size
            self.axis, self.n, self.lo, self.got = axis, n, lo, {}
            self.value, self.stage, self.rx, self.rf = value, stage, rx, rf

        def piece(self, key, p, start, n, direction, dst, dst_start, add=None):
            def step(r, w):
                v = self.value(p, start + r, w)
                if add is not None:
                    v = v + add(r, w).astype(F32)
                self.stage(p)[at(start, r, w), :] = v.astype(BF16)
            rows(n, step, self.size)
            self.launch(key, p, start, n, direction, dst, dst_start)

        def launch(self, key, p, start, n, direction, dst, dst_start):
            self.got[key] = send(self.stage(p).at[pl.ds(start, n), :],
                                 dst.at[pl.ds(dst_start, n), :], self.axis + direction)

        def far(self, add=None):
            lo, hi = self.lo, self.n - self.lo
            high = None if add is None else lambda r, w: add(lo + r, w)
            self.piece("far+", 3, 0, lo, "+", self.rx(0), 0, add)
            self.piece("far-", 3, lo, hi, "-", self.rx(1), 0, high)

        def near(self):
            self.piece("b+", 1, self.lo, self.n - self.lo, "+", self.rf(0), self.lo)
            self.piece("a-", 2, 0, self.lo, "-", self.rf(1), 0)

        def whole(self):
            self.piece("a+", 1, 0, self.n, "+", self.rf(0), 0)
            self.piece("a-", 2, 0, self.n, "-", self.rf(1), 0)

        def onward(self):
            lo, hi = self.lo, self.n - self.lo
            self.got["far+"].wait_recv()
            self.piece("a+", 1, 0, lo, "+", self.rf(0), 0, lambda r, w: self.rx(0)[at(0, r, w), :])
            self.got["far-"].wait_recv()
            self.piece("b-", 2, lo, hi, "-", self.rf(1), lo, lambda r, w: self.rx(1)[at(0, r, w), :])

        def arrive(self):
            for key in ("a+", "b+", "a-", "b-", "+", "-", "2"):
                if key in self.got:
                    self.got[key].wait_recv()

        def staged_far(self):
            lo, hi = self.lo, self.n - self.lo
            self.launch("far+", 3, 0, lo, "+", self.rx(0), 0)
            self.launch("far-", 3, lo, hi, "-", self.rx(1), 0)

        def staged_near(self):
            self.launch("b+", 1, self.lo, self.n - self.lo, "+", self.rf(0), self.lo)
            self.launch("a-", 2, 0, self.lo, "-", self.rf(1), 0)

        def total(self, r, w):
            v = self.value(0, r, w)
            for k in range(self.sources):
                v = v + self.rf(k)[at(0, r, w), :].astype(F32)
            return v

    def block_rings(axis, y, value, stage, rx, rf):
        def half(h):
            return Ring(
                axis, H, H // 2, lambda p, r, w: value(p, y, h * H + r, w),
                lambda p: stage.at[pl.ds(ORDER[p][y] * R + h * H, H), :],
                lambda d: rx.at[pl.ds(d * H + h * (H // 2), H // 2), :],
                lambda d: rf.at[pl.ds((d * 2 + y) * R + h * H, H), :])
        return [half(0), half(1)]

    ring_i = [block_rings("x", y, value_i, SXI, RXI, RFI) for y in range(2)]
    ring_t = [block_rings("z", y, value_t, SXT, RXT, RFT) for y in range(2)]

    def every(rings, what):
        for ring in rings:
            getattr(ring, what)()

    def over_y(n, h, value, stage, arrived, to):
        lo = n * R + h * H

        def step(r, w):
            stage[at(lo, r, w), :] = value(r, w).astype(BF16)
        rows(H, step)
        mine = pl.ds(lo, H)
        return send(stage.at[mine, :], arrived.at[mine, :], to)

    def far_over(rings, n, to):
        return [over_y(n, h, lambda r, w: rings[1][h].value(3, r, w), SF, RYF, to)
                for h in range(2)]

    def far_sum(rings, n, copies):
        for h in range(2):
            copies[h].wait_recv()
            rings[0][h].far(lambda r, w: RYF[at(n * R + h * H, r, w), :])

    def cross(rings, n, to):
        copies = []
        for h in range(2):
            rings[1][h].arrive()
            copies.append(over_y(n, h, rings[1][h].total, SY, RY, to))
        return copies

    def finish(rings, n, crossed, unit_ref, inv_ref, gp):
        t = jnp.exp(jnp.full((1, D), ls_ref[0], F32))

        for h in range(2):
            rings[0][h].arrive()
            crossed[h].wait_recv()

            def step(r, w):
                low = h * H + r
                g = (rings[0][h].total(r, w) + RY[at(n * R, low, w), :].astype(F32)) * t
                u = unit_ref[at(0, low, w), :]
                inv = inv_ref[at(0, low, w), :][:, 0:1]
                along = jnp.sum(u * g, axis=1, keepdims=True)
                gp[at(0, low, w), :] = (inv * (g - u * along)).astype(BF16)
            rows(H, step, 32)

    def feature_grad(gp, w_ref, lo):
        gf_ref[lo:lo + R, :] = lax.dot_general(
            gp[...], w_ref[...], NT, preferred_element_type=F32).astype(BF16)

    unit(1536, 512, 0, 512, True)
    every(ring_t[0], "near")
    unit(1536, 512, 512, 512)
    core_send(3)
    unit(1024, 512, 512, 512)
    core_send(2)
    every(ring_t[1], "whole")
    core_wait(3)
    over_i = far_over(ring_i, 0, "yi")
    core_wait(2)
    every(ring_i[1], "whole")
    unit(0, 1024, 768, 256)
    over_t = far_over(ring_t, 1, "yt")
    core_send(1)
    core_send(0)
    far_sum(ring_i, 0, over_i)
    core_wait(1)
    every(ring_i[0], "near")
    cross_t = cross(ring_t, 1, "yt")
    core_wait(0)
    far_sum(ring_t, 1, over_t)
    cross_i = cross(ring_i, 0, "yi")
    every(ring_i[0], "onward")
    every(ring_t[0], "onward")
    finish(ring_i, 0, cross_i, unitI, invI, gpI)
    GI[0:R, :] = gpI[...]
    grad_i = send(gpI, GI.at[pl.ds(R, R), :], "core")
    finish(ring_t, 1, cross_t, unitT, invT, gpT)

    grad_t = send(gpT, GT.at[pl.ds(R, R), :], "core")
    GT[0:R, :] = gpT[...]

    def columns(third):
        return slice(third * 384, third * 384 + 384)

    def product(third, lo, n):
        return jnp.dot(XP[third, lo:lo + n, :], GL[:, columns(third)], preferred_element_type=F32)

    def weight_ring(third, axis, n, lo, stage, rx, rf, sources):
        return Ring(
            axis, n, lo, lambda p, r, w: accI[at(p * n, r, w), columns(third)],
            lambda p: stage.at[third, pl.ds(p * n, n), :],
            lambda d: rx.at[third, d], lambda d: rf.at[third, d], sources, SLOT)

    N, half = 4 * SLOT, 2 * SLOT
    outer = [weight_ring(k, AXES[k][0], N, half, S1, RX1, RF1, 2) for k in range(3)]
    inner = [weight_ring(k, AXES[k][1], SLOT, 0, S2, None, RF2, 3) for k in range(3)]
    feature_grad(gpI, WI, 0)
    grad_i.wait_recv()
    grad_t.wait_recv()
    GL[...] = jnp.where(first, GI[...], GT[...])
    for third in range(3):
        S1[third, 3 * N:4 * N, :] = product(third, 3 * N, N).astype(BF16)
        outer[third].staged_far()
    for third in range(3):
        v = product(third, N, N)
        accI[N:N + half, columns(third)] = v[:half]
        S1[third, N + half:2 * N, :] = v[half:].astype(BF16)
        v = product(third, 2 * N, N)
        S1[third, 2 * N:2 * N + half, :] = v[:half].astype(BF16)
        accI[2 * N + half:3 * N, columns(third)] = v[half:]
        outer[third].staged_near()
    every(outer, "onward")
    for third in range(3):
        accI[0:N, columns(third)] = product(third, 0, N)
    feature_grad(gpT, WT, R)
    for third in range(3):
        outer[third].arrive()

        for k, (p, there) in enumerate(((3, "2"), (1, "+"), (2, "-"))):
            S2[third, p * SLOT:(p + 1) * SLOT, :] = outer[third].total(p * SLOT, SLOT).astype(BF16)
            inner[third].launch(there, p, 0, SLOT, there, inner[third].rf(k), 0)
        accI[0:SLOT, columns(third)] = outer[third].total(0, SLOT)

    last = []
    for third in range(3):
        c_axis = AXES[third][2]
        row = lax.broadcasted_iota(jnp.int32, (R, SLOT), 0)
        k = lax.broadcasted_iota(jnp.int32, (R, SLOT), 1)
        block, i = row >> 4, row & 15
        other = block & 1
        core = other + me["core"] - 2 * other * me["core"]
        want = ring_place(block >> 1, me[c_axis]) * 18 + core * 9 + i
        pick = jnp.where((k == want) & (i < 9), 1.0, 0.0).astype(BF16)
        inner[third].arrive()
        mine = inner[third].total(0, SLOT).astype(BF16)
        E[third] = jnp.dot(pick, mine, preferred_element_type=F32).astype(BF16)
        for j, there in enumerate(("core", "+", "+c", "-", "-c", "2", "2c"), 1):
            some = pl.ds(j * 16, 16)
            last.append(send(E.at[third, some, :], Z.at[third, some, :],
                             there if j == 1 else c_axis + there))
    for third in range(3):
        for copy in last[third * 7:third * 7 + 7]:
            copy.wait_recv()
        z = Z[third, 16:128, :].astype(F32)
        same = E[third, 0:16, :].astype(F32) + z[16:32] + z[48:64] + z[80:96]
        swapped = z[0:16] + z[32:48] + z[64:80] + z[96:112]
        dw_ref[0:16, columns(third)] = jnp.where(first, same, swapped)
        dw_ref[16:32, columns(third)] = jnp.where(first, swapped, same)
    for copy in sent:
        copy.wait_send()


def fused(img_feat, txt_feat, w_img, w_txt, ls, bias):
    D = img_feat.shape[1]
    vmem = pl.BlockSpec(memory_space=pltpu.VMEM)
    hbm = pl.BlockSpec(memory_space=pl.ANY)
    smem = pl.BlockSpec(memory_space=pltpu.SMEM)
    sizes = [(2048, BF16), (1024, BF16), (2048, F32), (1024, F32), (1024, BF16), (1024, BF16),
             (1024, BF16), (1024, BF16), (R, BF16), (R, BF16), (512, BF16), (512, BF16),
             (256, BF16), (256, BF16), (256, BF16), (256, BF16), (D, BF16), (D, BF16),
             (R, BF16), (R, BF16), (R, F32), (R, F32), (R, BF16), (R, BF16),
             (2 * R, BF16), (2 * R, BF16), (2 * R, BF16), (2 * R, BF16), (R, BF16)]
    thirds = [(4 * 4 * SLOT,), (2, 2 * SLOT), (2, 4 * SLOT), (4 * SLOT,), (3, SLOT), (R,), (R,)]
    return pl.pallas_call(
        kernel,
        out_shape=(jax.ShapeDtypeStruct((2 * R, D), BF16), jax.ShapeDtypeStruct((32, D), F32)),
        in_specs=[hbm] * 4 + [smem] * 2,
        out_specs=(vmem,) * 2,
        scratch_shapes=[pltpu.VMEM((n, D), t) for n, t in sizes]
        + [pltpu.VMEM((R, 128), F32)] * 2
        + [pltpu.VMEM((3, 16 * SLOT, 2 * R), BF16)]
        + [pltpu.VMEM((3,) + n + (D // 3,), BF16) for n in thirds]
        + [pltpu.SemaphoreType.DMA((5,))] + [pltpu.SemaphoreType.DMA((144,))] * 2,
        compiler_params=pltpu.CompilerParams(
            collective_id=0, has_side_effects=True, vmem_limit_bytes=62 * 2**20),
    )(img_feat, txt_feat, w_img, w_txt, ls, bias)


def split(gf_ref, dw_ref, gfi_ref, gft_ref, dwi_ref, dwt_ref):
    gfi_ref[...] = gf_ref[0:R, :]
    gft_ref[...] = gf_ref[R:2 * R, :]
    dwi_ref[...] = dw_ref[0:9, :]
    dwt_ref[...] = dw_ref[16:25, :]


def outputs(gf, dw):
    D = gf.shape[1]
    vmem = pl.BlockSpec(memory_space=pltpu.VMEM)
    return pl.pallas_call(
        split,
        out_shape=(jax.ShapeDtypeStruct((R, D), BF16),) * 2 + (jax.ShapeDtypeStruct((9, D), F32),) * 2,
        in_specs=[vmem] * 2, out_specs=(vmem,) * 4)(gf, dw)


def body(img_feat, txt_feat, w_img, w_txt, logit_scale_log, bias):
    gf, dw = fused(img_feat, txt_feat, w_img, w_txt, logit_scale_log, bias)
    return outputs(gf, dw)


def solution(mesh):
    rows = P(("blk", "group"), None)
    return jax.shard_map(
        body, mesh=mesh, in_specs=(rows, rows, P(), P(), P(), P()),
        out_specs=(rows,) * 4, check_vma=False)
```
